128 devices in a mesh: dp: 128 (over x, z, y, core).
Axes of the slice: x: 4, y: 4, z: 4, core: 2. Of those that a mesh axis runs over, the one named last changes fastest.
Arguments:
- picture_tower_output: bfloat16 [16384, 1152], P('dp'), may hold values from -10 to 10, as said below
- sentence_tower_output: bfloat16 [16384, 1152], P('dp'), may hold values from -10 to 10, as said below
- picture_projector_matrix: bfloat16 [1152, 1152], replicated, may hold values from -0.1875 to 0.1875
- sentence_projector_matrix: bfloat16 [1152, 1152], replicated, may hold values from -0.1875 to 0.1875
- score_sharpness: float32 [1], replicated, may hold values from 4 to 12
- score_offset: float32 [1], replicated, may hold values from -2.5 to -0.5
- scored_text_groups: int32 [128, 10], replicated, may hold values from 0 to 127, as said below
- group_member_count: int32 [128], replicated, may hold values from 1 to 10, as said below
- holder_device_per_group: int32 [128], replicated, may hold values from 0 to 127, as said below
Outputs:
- grad_img_feat: bfloat16 [16384, 1152], P('dp')
- grad_txt_feat: bfloat16 [16384, 1152], P('dp')
- grad_w_img: float32 [1152, 1152], replicated
- grad_w_txt: float32 [1152, 1152], replicated
The draws below stay inside these ranges and needn't reach their ends.
Inputs may be any that keep to these rules, and one draw needn't show every extreme that they name: `scored_text_groups`: row b: slot 0 is b itself, slots 1 to group_member_count[b] - 1 are the other blocks of b's cluster, each once, later slots repeat b. Clusters partition the blocks, and every member of a cluster lists the same members. `group_member_count`: some cluster has exactly 10 blocks. A permutation: block b is held by device holder_device_per_group[b]. `picture_tower_output`: finite values. `sentence_tower_output`: finite values.
All inputs are finite; a program needn't handle non-finite values.
Results may differ from the reference program's by a relative error of at most 0.007.
Values may be sent and summed in bfloat16 or wider, within the bound.
No kernel may reach another device: no remote copies, remote signals or barrier semaphores. Data moves between devices by JAX's collectives and lax.ppermute only.
A program may use at most 128 MiB of HBM per device.

```python
import math
import jax
import jax.numpy as jnp
from jax import lax

D = 1152
BLK = 128
MAXC = 10
PAIRS = 16384
N_DP = 128


def cluster_layout(key):
    keys = jax.random.split(key, 3)
    order = jax.random.permutation(keys[0], N_DP).astype(jnp.int32)
    larger = jax.random.randint(keys[1], (N_DP,), 0, 4) == 0
    spans = jnp.where(larger, jax.random.randint(keys[2], (N_DP,), 2, MAXC + 1), 2).astype(jnp.int32)
    spans = spans.at[0].set(MAXC)
    endings = jnp.cumsum(spans).astype(jnp.int32)
    places = jnp.arange(N_DP, dtype=jnp.int32)
    member = jnp.sum((endings[None, :] <= places[:, None]).astype(jnp.int32), axis=1)
    finish = jnp.minimum(endings[member], N_DP)
    begins = endings[member] - spans[member]
    count_at = finish - begins
    place_of = jnp.zeros(N_DP, jnp.int32).at[order].set(places)
    begin_block = begins[place_of]
    count_block = count_at[place_of]
    slots = jnp.arange(MAXC, dtype=jnp.int32)
    rotated = begin_block[:, None] + (place_of[:, None] - begin_block[:, None] + slots[None, :]) % count_block[:, None]
    listed = order[rotated]
    listed = jnp.where(slots[None, :] < count_block[:, None], listed, places[:, None])
    return (listed.astype(jnp.int32), count_block.astype(jnp.int32))


def draw_scored_text_groups(key, part):
    return cluster_layout(key)[0]


def draw_group_member_count(key, part):
    return cluster_layout(key)[1]


def draw_holder_device_per_group(key, part):
    key = jax.random.fold_in(key, 7)
    return jax.random.permutation(key, N_DP).astype(jnp.int32)


def feature_scales(keys):
    row_scale = jnp.exp(jax.random.uniform(keys[0], (PAIRS, 1), jnp.float32, math.log(0.2), math.log(2.0)))
    column_scale = jnp.exp(jax.random.uniform(keys[1], (1, D), jnp.float32, math.log(0.3), 0.0))
    return row_scale * column_scale


def draw_picture_tower_output(key, part):
    key = jax.random.fold_in(key, 11)
    keys = jax.random.split(key, 4)
    base = jnp.clip(jax.random.normal(keys[2], (PAIRS, D), jnp.float32), -5.0, 5.0)
    return (base * feature_scales(keys)).astype(jnp.bfloat16)


def draw_sentence_tower_output(key, part):
    key = jax.random.fold_in(key, 23)
    keys = jax.random.split(key, 4)
    base = jnp.clip(jax.random.normal(keys[2], (PAIRS, D), jnp.float32), -5.0, 5.0)
    return (base * feature_scales(keys)).astype(jnp.bfloat16)


def scatter_about(rng, dims, spread, most, kind=jnp.bfloat16):
    array = spread * jax.random.normal(rng, dims, jnp.float32)
    return jnp.clip(array, min=-most, max=most).astype(kind)


def setup_inputs(seed: int = 0) -> dict:
    streams_of = jax.random.split(jax.random.key(seed), 10)
    picture_tower_output = draw_picture_tower_output(jax.random.fold_in(streams_of[9], 71), 0)
    sentence_tower_output = draw_sentence_tower_output(jax.random.fold_in(streams_of[9], 71), 0)
    picture_projector_matrix = scatter_about(streams_of[2], (D, D), D ** -0.5, 0.1875)
    sentence_projector_matrix = scatter_about(streams_of[3], (D, D), D ** -0.5, 0.1875)
    score_sharpness = jnp.clip(jnp.exp(jax.random.uniform(streams_of[4], (1,), jnp.float32, math.log(4.0), math.log(12.0))), 4.0, 12.0)
    score_offset = jnp.clip(jax.random.uniform(streams_of[5], (1,), jnp.float32, -2.5, -0.5), -2.5, -0.5)
    scored_text_groups = draw_scored_text_groups(jax.random.fold_in(streams_of[9], 71), 0)
    group_member_count = draw_group_member_count(jax.random.fold_in(streams_of[9], 71), 0)
    holder_device_per_group = draw_holder_device_per_group(jax.random.fold_in(streams_of[9], 71), 0)
    return dict(picture_tower_output=picture_tower_output, sentence_tower_output=sentence_tower_output, picture_projector_matrix=picture_projector_matrix, sentence_projector_matrix=sentence_projector_matrix, score_sharpness=score_sharpness, score_offset=score_offset, scored_text_groups=scored_text_groups, group_member_count=group_member_count, holder_device_per_group=holder_device_per_group)


eps_norm = 1e-06

def project(features, weight):
    product = jnp.dot(features, weight, preferred_element_type=jnp.float32)
    inverse = lax.rsqrt(lax.optimization_barrier(jnp.sum(product * product, axis=-1, keepdims=True)) + eps_norm)
    return (product * inverse, inverse)

def pull_back(features, weight, unit_rows, inverse, upstream):
    radial = lax.optimization_barrier(jnp.sum(unit_rows * upstream, axis=-1, keepdims=True))
    through = (inverse * (upstream - unit_rows * radial)).astype(jnp.bfloat16)
    feature_grad = lax.dot_general(through, weight, (((1,), (1,)), ((), ())), preferred_element_type=jnp.float32).astype(jnp.bfloat16)
    weight_grad = lax.dot_general(features, through, (((0,), (0,)), ((), ())), preferred_element_type=jnp.float32)
    return (feature_grad, weight_grad)

def rounded_extent(values):
    return lax.optimization_barrier(values.astype(jnp.bfloat16)).astype(jnp.float32)

def reference(picture_tower_output, sentence_tower_output, picture_projector_matrix, sentence_projector_matrix, score_sharpness, score_offset, scored_text_groups, group_member_count, holder_device_per_group):
    unit_img, inverse_img = project(picture_tower_output, picture_projector_matrix)
    unit_txt, inverse_txt = project(sentence_tower_output, sentence_projector_matrix)
    image_blocks = rounded_extent(unit_img).reshape(N_DP, BLK, D)[holder_device_per_group]
    text_blocks = rounded_extent(unit_txt).reshape(N_DP, BLK, D)[holder_device_per_group]
    sharpness_power = score_sharpness[0]
    logit_shift_bias = score_offset[0]
    diagonal = jnp.eye(BLK, dtype=bool)

    def per_block(text_total, block):
        image_tile_block = image_blocks[block]

        def per_slot(slot, loop_state):
            image_grad, text_total = loop_state
            peer_block = scored_text_groups[block, slot]
            caption_block = text_blocks[peer_block]
            pair_logit_values = sharpness_power * jnp.dot(image_tile_block, caption_block.T, precision=lax.Precision.HIGHEST) + logit_shift_bias
            label_signs = jnp.where(diagonal & (peer_block == block), 1.0, -1.0)
            sigmoid_factor = rounded_extent(-sharpness_power * label_signs * jax.nn.sigmoid(-label_signs * pair_logit_values))
            image_grad = image_grad + jnp.dot(sigmoid_factor, caption_block, precision=lax.Precision.HIGHEST)
            partial_value = rounded_extent(jnp.dot(sigmoid_factor.T, image_tile_block, precision=lax.Precision.HIGHEST))
            text_total = text_total.at[peer_block].add(partial_value)
            return (image_grad, text_total)
        image_grad, text_total = lax.fori_loop(0, group_member_count[block], per_slot, (jnp.zeros((BLK, D), jnp.float32), text_total))
        return (text_total, image_grad)
    text_total, image_grads = lax.scan(per_block, jnp.zeros((N_DP, BLK, D), jnp.float32), jnp.arange(N_DP, dtype=jnp.int32))
    image_rows = jnp.zeros((N_DP, BLK, D), jnp.float32).at[holder_device_per_group].set(image_grads).reshape(N_DP * BLK, D)
    text_rows = jnp.zeros((N_DP, BLK, D), jnp.float32).at[holder_device_per_group].set(text_total).reshape(N_DP * BLK, D)
    grad_img_feat, head_img = pull_back(picture_tower_output, picture_projector_matrix, unit_img, inverse_img, image_rows)
    grad_txt_feat, head_txt = pull_back(sentence_tower_output, sentence_projector_matrix, unit_txt, inverse_txt, text_rows)
    factor = (64.0 / (N_DP * BLK)) ** 0.5
    return (grad_img_feat, grad_txt_feat, head_img * factor, head_txt * factor)
```

```python
import functools

import jax
import jax.numpy as jnp
from jax import lax
from jax.experimental import pallas as pl
from jax.experimental.pallas import tpu as pltpu
from jax.sharding import Mesh, PartitionSpec as P

eps_norm = 1e-06
ALL = ("x", "z", "y", "c")
ORDERS = (("x", "y", "z"), ("y", "z", "x"), ("z", "x", "y"))
bf16 = jnp.bfloat16
f32 = jnp.float32


def project(features, weight):
    product = jnp.dot(features, weight, preferred_element_type=f32)
    inverse = lax.rsqrt(jnp.sum(product * product, axis=-1, keepdims=True) + eps_norm)
    return (product * inverse, inverse)


def tangent(unit_rows, inverse, upstream):
    radial = jnp.sum(unit_rows * upstream, axis=-1, keepdims=True)
    return (inverse * (upstream - unit_rows * radial)).astype(bf16)


def swap(array, axis, mask):
    size = lax.axis_size(axis)
    return lax.ppermute(array, axis, [(i, i ^ mask) for i in range(size)])


def reduce_pieces(grad):
    rows, width = grad.shape
    part_rows = rows // 3
    parts = []
    for part, axes in enumerate(ORDERS):
        first = lax.axis_index(axes[0])
        second = lax.axis_index(axes[1])
        block = grad[part * part_rows : (part + 1) * part_rows].reshape(4, part_rows // 4, width)
        parts.append((block, axes, first, second))
    stage = []
    for block, axes, first, second in parts:
        got = [swap(lax.dynamic_index_in_dim(block, first ^ m, 0, keepdims=False), axes[0], m) for m in (1, 2, 3)]
        own = lax.dynamic_index_in_dim(block, first, 0, keepdims=False)
        stage.append((own, got))
    stage2 = []
    for (own, got), (block, axes, first, second) in zip(stage, parts):
        total = (own.astype(f32) + got[0].astype(f32)) + (got[1].astype(f32) + got[2].astype(f32))
        total = total.astype(bf16).reshape(4, part_rows // 16, width)
        got2 = [swap(lax.dynamic_index_in_dim(total, second ^ m, 0, keepdims=False), axes[1], m) for m in (1, 2, 3)]
        own2 = lax.dynamic_index_in_dim(total, second, 0, keepdims=False)
        stage2.append((own2, got2))
    stage3 = []
    for (own, got), (block, axes, first, second) in zip(stage2, parts):
        total = (own.astype(f32) + got[0].astype(f32)) + (got[1].astype(f32) + got[2].astype(f32))
        total = total.astype(bf16)
        got3 = [swap(total, axes[2], m) for m in (1, 2, 3)]
        stage3.append((total, got3))
    stage4 = []
    for (own, got), (block, axes, first, second) in zip(stage3, parts):
        total = (own.astype(f32) + got[0].astype(f32)) + (got[1].astype(f32) + got[2].astype(f32))
        total = total.astype(bf16)
        gathered = [total] + [swap(total, axes[1], m) for m in (1, 2, 3)]
        stage4.append(gathered)
    out = []
    for gathered, (block, axes, first, second) in zip(stage4, parts):
        low, high = second & 1, second >> 1
        e = [jnp.where(low == 0, gathered[j], gathered[j ^ 1]) for j in range(4)]
        e = [jnp.where(high == 0, e[j], e[j ^ 2]) for j in range(4)]
        quarter = jnp.concatenate(e, axis=0)
        out.append([quarter] + [swap(quarter, axes[0], m) for m in (1, 2, 3)])
    return out


def assemble_kernel(where_ref, *refs):
    pieces = refs[:24]
    out_img, out_txt, wide, sems = refs[24:]
    rows = pieces[0].shape[0]

    def run(own, other):
        copies = []
        for k in range(24):
            target = own if k < 12 else other
            part, m = divmod(k % 12, 4)
            wide[k] = pieces[k][...].astype(f32)
            begin = pl.multiple_of((part * 4 + jnp.bitwise_xor(where_ref[part], m)) * rows, 32)
            copy = pltpu.make_async_copy(wide.at[k], target.at[pl.ds(begin, rows)], sems.at[k])
            copy.start()
            copies.append(copy)
        for copy in copies:
            copy.wait()

    @pl.when(where_ref[3] == 0)
    def _():
        run(out_img, out_txt)

    @pl.when(where_ref[3] != 0)
    def _():
        run(out_txt, out_img)


def assemble(where, own, other):
    rows, width = own[0].shape
    shape = jax.ShapeDtypeStruct((rows * 12, width), f32)
    return pl.pallas_call(
        assemble_kernel,
        out_shape=(shape, shape),
        in_specs=[pl.BlockSpec(memory_space=pltpu.SMEM)] + [pl.BlockSpec(memory_space=pltpu.VMEM)] * 24,
        out_specs=(pl.BlockSpec(memory_space=pl.ANY),) * 2,
        scratch_shapes=[pltpu.VMEM((24, rows, width), f32), pltpu.SemaphoreType.DMA((24,))],
        compiler_params=pltpu.CompilerParams(vmem_limit_bytes=40 * 2**20),
    )(where, *own, *other)


def local(x_img, x_txt, w_img, w_txt, sharpness, offset, lists, counts, holder):
    devices = lax.axis_size(ALL)
    me = lax.axis_index(ALL)
    core = lax.axis_index("c")
    rows, width = x_img.shape
    slots = lists.shape[1]
    scale = sharpness[0]
    shift = offset[0]
    f_txt, r_txt = project(x_txt, w_txt)
    f_img, r_img = project(x_img, w_img)
    z_txt = f_txt.astype(bf16)
    z_img = f_img.astype(bf16)

    spread = lax.all_to_all(jnp.stack([z_txt, z_img], axis=1), ALL, 0, 0, tiled=True)
    spread = spread.reshape(2 * devices, width)

    numbers = jnp.arange(devices, dtype=jnp.int32)
    hot = holder[None, :] == numbers[:, None]
    source = jnp.sum(jnp.where(lists[:, :, None] == numbers, holder, 0), axis=2)
    table = jnp.dot(hot.astype(bf16), source.astype(bf16), preferred_element_type=f32).astype(jnp.int32)
    count = jnp.sum(jnp.where(hot[me], counts, 0))

    columns = jnp.arange(2 * devices, dtype=jnp.int32)
    near = jnp.concatenate([2 * table[:, 1:9], 2 * table[:, 1:9] + 1], axis=1)
    last = jnp.concatenate([2 * table[:, 9:], 2 * table[:, 9:] + 1], axis=1)
    pick = (near[:, :, None] == columns).astype(bf16).reshape(16 * devices, 2 * devices)
    pick_last = (last[:, :, None] == columns).astype(bf16).reshape(2 * devices, 2 * devices)
    send_last = jnp.dot(pick_last, spread, preferred_element_type=f32).astype(bf16).reshape(devices, 2, width)
    send = jnp.dot(pick, spread, preferred_element_type=f32).astype(bf16).reshape(devices, 16, width)
    mates_last = lax.all_to_all(send_last, ALL, 0, 0, tiled=True).reshape(2 * devices, width)
    mates = lax.all_to_all(send, ALL, 0, 0, tiled=True).reshape(16 * devices, width)

    x_mine = jnp.where(core == 0, x_img, x_txt)
    x_other = swap(jnp.where(core == 0, x_txt, x_img), "c", 1)

    own = jnp.concatenate([z_img, z_txt], axis=0)
    transposed = (((1,), (1,)), ((), ()))

    def coefficients(others, per):
        logits = scale * lax.dot_general(own, others, transposed, preferred_element_type=f32) + shift
        column = lax.broadcasted_iota(jnp.int32, logits.shape, 1) % (2 * per)
        row = lax.broadcasted_iota(jnp.int32, logits.shape, 0)
        slot = (1 if per > 1 else 9) + column % per
        keep = (slot < count) & ((column < per) == (row < rows))
        return jnp.where(keep, scale * jax.nn.sigmoid(logits), 0.0).astype(bf16)

    logits = scale * lax.dot_general(z_img, z_txt, transposed, preferred_element_type=f32) + shift
    sign = jnp.where(jnp.eye(rows, dtype=bool), 1.0, -1.0)
    coef = (-scale * sign * jax.nn.sigmoid(-sign * logits)).astype(bf16)
    dz = jnp.concatenate(
        [
            jnp.dot(coef, z_txt, preferred_element_type=f32),
            lax.dot_general(coef, z_img, (((0,), (0,)), ((), ())), preferred_element_type=f32),
        ],
        axis=0,
    )
    dz = dz + jnp.dot(coefficients(mates_last, 1), mates_last, preferred_element_type=f32)
    dz = dz + jnp.dot(coefficients(mates, 8), mates, preferred_element_type=f32)

    du_img = tangent(f_img, r_img, dz[:rows])
    du_txt = tangent(f_txt, r_txt, dz[rows:])
    du_mine = jnp.where(core == 0, du_img, du_txt)
    du_other = swap(jnp.where(core == 0, du_txt, du_img), "c", 1)

    factor = (64.0 / (devices * rows)) ** 0.5
    grad = lax.dot_general(
        jnp.concatenate([x_mine, x_other], axis=0),
        jnp.concatenate([du_mine, du_other], axis=0),
        (((0,), (0,)), ((), ())),
        preferred_element_type=f32,
    )
    grad = (grad * factor).astype(bf16)
    g_img = lax.dot_general(du_img, w_img, transposed, preferred_element_type=f32).astype(bf16)
    g_txt = lax.dot_general(du_txt, w_txt, transposed, preferred_element_type=f32).astype(bf16)

    pieces = [piece for part in reduce_pieces(grad) for piece in part]
    others = [swap(piece, "c", 1) for piece in pieces]
    where = jnp.stack([lax.axis_index(axes[0]) for axes in ORDERS] + [core]).astype(jnp.int32)
    head_img, head_txt = assemble(where, pieces, others)
    return (g_img, g_txt, head_img, head_txt)


def solution(mesh):
    grid = Mesh(mesh.devices.reshape(4, 4, 4, 2), ALL)
    placed = (P(ALL, None), P(ALL, None), P(), P(), P(), P(), P(), P(), P())
    return jax.shard_map(
        local,
        mesh=grid,
        in_specs=placed,
        out_specs=(P(ALL, None), P(ALL, None), P(), P()),
        check_vma=False,
    )
```

```python
import jax
import jax.numpy as jnp
from jax import lax
from jax.experimental import pallas as pl
from jax.experimental.pallas import tpu as pltpu
from jax.sharding import Mesh, PartitionSpec as P

eps_norm = 1e-06
ALL = ("x", "z", "y", "c")
FIRST = ("x", "y", "z")
bf16 = jnp.bfloat16
f32 = jnp.float32


def project(features, weight):
    product = jnp.dot(features, weight, preferred_element_type=f32)
    inverse = lax.rsqrt(jnp.sum(product * product, axis=-1, keepdims=True) + eps_norm)
    return (product * inverse, inverse)


def swap(array, axes, mask):
    axes = (axes,) if isinstance(axes, str) else axes
    size = lax.axis_size(axes[0])
    if len(axes) == 1:
        pairs = [(i, i ^ mask) for i in range(size)]
    else:
        pairs = [(i * size + j, (i ^ mask) * size + (j ^ mask)) for i in range(size) for j in range(size)]
    return lax.ppermute(array, axes, pairs)


def take(array, index):
    return lax.dynamic_index_in_dim(array, index, 0, keepdims=False)


def total_of(own, got):
    total = (own.astype(f32) + got[0].astype(f32)) + (got[1].astype(f32) + got[2].astype(f32))
    return total.astype(bf16)


def reduce_pieces(grad, beside):
    rows, width = grad.shape
    quarter = jnp.bitwise_xor(jnp.bitwise_xor(lax.axis_index("x"), lax.axis_index("y")), lax.axis_index("z"))
    blocks = grad.reshape(3, 4, rows // 12, width)
    got = [
        [swap(take(blocks[p], quarter ^ m), FIRST[p], m) for p in range(3)] for m in (1, 2, 3)
    ]
    done = beside()
    got, done = lax.optimization_barrier((got, done))
    total = jnp.concatenate(
        [total_of(take(blocks[p], quarter), [got[m][p] for m in range(3)]) for p in range(3)], axis=0
    )

    chunk = lax.axis_index("y")
    chunks = total.reshape(4, rows // 16, width)
    got = [swap(take(chunks, chunk ^ m), ("x", "y"), m) for m in (1, 2, 3)]
    total = total_of(take(chunks, chunk), got)
    total = total_of(total, [swap(total, ("x", "z"), m) for m in (1, 2, 3)])
    gathered = [total] + [swap(total, ("x", "y"), m) for m in (1, 2, 3)]

    low, high = chunk & 1, chunk >> 1
    kept = [jnp.where(low == 0, gathered[j], gathered[j ^ 1]) for j in range(4)]
    kept = [jnp.where(high == 0, kept[j], kept[j ^ 2]) for j in range(4)]
    kept = jnp.concatenate(kept, axis=0)
    each = kept.reshape(3, rows // 12, width)
    others = [swap(each[p], FIRST[p], m) for m in (1, 2, 3) for p in range(3)]
    return kept, others, quarter, done


def assemble_kernel(where_ref, mine, mine_rest, other, other_rest, out_img, out_txt, wide, sems):
    count = mine.shape[0] // 3

    def run(own_out, other_out):
        copies = []
        for kept, rest, target in ((mine, mine_rest, own_out), (other, other_rest, other_out)):
            for m in range(4):
                for p in range(3):
                    k = len(copies)
                    if m == 0:
                        piece = kept[p * count : (p + 1) * count]
                    else:
                        at = ((m - 1) * 3 + p) * count
                        piece = rest[at : at + count]
                    wide[k] = piece.astype(f32)
                    begin = pl.multiple_of((p * 4 + jnp.bitwise_xor(where_ref[0], m)) * count, 32)
                    copy = pltpu.make_async_copy(wide.at[k], target.at[pl.ds(begin, count)], sems.at[k])
                    copy.start()
                    copies.append(copy)
        for copy in copies:
            copy.wait()

    @pl.when(where_ref[1] == 0)
    def _():
        run(out_img, out_txt)

    @pl.when(where_ref[1] != 0)
    def _():
        run(out_txt, out_img)


def assemble(where, mine, mine_rest, other, other_rest):
    count, width = mine.shape[0] // 3, mine.shape[1]
    shape = jax.ShapeDtypeStruct((count * 12, width), f32)
    return pl.pallas_call(
        assemble_kernel,
        out_shape=(shape, shape),
        in_specs=[pl.BlockSpec(memory_space=pltpu.SMEM)] + [pl.BlockSpec(memory_space=pltpu.VMEM)] * 4,
        out_specs=(pl.BlockSpec(memory_space=pl.ANY),) * 2,
        scratch_shapes=[pltpu.VMEM((24, count, width), f32), pltpu.SemaphoreType.DMA((24,))],
        compiler_params=pltpu.CompilerParams(vmem_limit_bytes=40 * 2**20),
    )(where, mine, mine_rest, other, other_rest)


def pair_kernel(number_ref, count_ref, own_ref, mates_ref, begin_ref, unit_ref, inverse_ref, out_ref, total):
    step = pl.program_id(0)
    scale, shift = number_ref[0], number_ref[1]
    mates = mates_ref[...]
    logits = lax.dot_general(own_ref[...], mates, (((1,), (1,)), ((), ())), preferred_element_type=f32)
    logits = scale * logits + shift
    column = lax.broadcasted_iota(jnp.int32, logits.shape, 1) & 15
    row = lax.broadcasted_iota(jnp.int32, logits.shape, 0)
    keep = ((column & 7) + 1 < count_ref[0]) & ((column < 8) == (row < logits.shape[0] // 2))
    coef = jnp.where(keep, scale / (1.0 + jnp.exp(-logits)), 0.0).astype(bf16)
    part = jnp.dot(coef, mates, preferred_element_type=f32)

    @pl.when(step == 0)
    def _():
        total[...] = begin_ref[...] + part

    @pl.when(step != 0)
    def _():
        total[...] += part

    @pl.when(step == pl.num_programs(0) - 1)
    def _():
        unit = unit_ref[...]
        upstream = total[...]
        radial = jnp.sum(unit * upstream, axis=-1, keepdims=True)
        out_ref[...] = (inverse_ref[...] * (upstream - unit * radial)).astype(bf16)


def pair_stage(numbers, count, own, mates, begin, unit, inverse):
    rows, width = own.shape
    per = 512

    def whole(shape):
        return pl.BlockSpec(shape, lambda i: (0, 0))

    return pl.pallas_call(
        pair_kernel,
        grid=(mates.shape[0] // per,),
        out_shape=jax.ShapeDtypeStruct((rows, width), bf16),
        in_specs=[
            pl.BlockSpec(memory_space=pltpu.SMEM),
            pl.BlockSpec(memory_space=pltpu.SMEM),
            whole((rows, width)),
            pl.BlockSpec((per, width), lambda i: (i, 0)),
            whole((rows, width)),
            whole((rows, width)),
            whole((rows, 1)),
        ],
        out_specs=whole((rows, width)),
        scratch_shapes=[pltpu.VMEM((rows, width), f32)],
        compiler_params=pltpu.CompilerParams(vmem_limit_bytes=40 * 2**20),
    )(numbers, count, own, mates, begin, unit, inverse)


def local(x_img, x_txt, w_img, w_txt, sharpness, offset, lists, counts, holder):
    devices = lax.axis_size(ALL)
    me = lax.axis_index(ALL)
    core = lax.axis_index("c")
    rows, width = x_img.shape
    slots = lists.shape[1]
    scale = sharpness[0]
    shift = offset[0]
    f_txt, r_txt = project(x_txt, w_txt)
    f_img, r_img = project(x_img, w_img)
    z_txt = f_txt.astype(bf16)
    z_img = f_img.astype(bf16)

    spread = lax.all_to_all(jnp.stack([z_txt, z_img], axis=1), ALL, 0, 0, tiled=True)
    spread = spread.reshape(2 * devices, width)

    numbers = jnp.arange(devices, dtype=jnp.int32)
    hot = holder[None, :] == numbers[:, None]
    source = jnp.sum(jnp.where(lists[:, :, None] == numbers, holder, 0), axis=2)
    table = jnp.dot(hot.astype(bf16), source.astype(bf16), preferred_element_type=f32).astype(jnp.int32)
    count = jnp.sum(jnp.where(hot[me], counts, 0))

    columns = jnp.arange(2 * devices, dtype=jnp.int32)
    near = jnp.concatenate([2 * table[:, 1:9], 2 * table[:, 1:9] + 1], axis=1)
    last = jnp.concatenate([2 * table[:, 9:], 2 * table[:, 9:] + 1], axis=1)
    pick = (near[:, :, None] == columns).astype(bf16).reshape(16 * devices, 2 * devices)
    pick_last = (last[:, :, None] == columns).astype(bf16).reshape(2 * devices, 2 * devices)
    send_last = jnp.dot(pick_last, spread, preferred_element_type=f32).astype(bf16).reshape(devices, 2, width)
    send = jnp.dot(pick, spread, preferred_element_type=f32).astype(bf16).reshape(devices, 16, width)
    mates_last = lax.all_to_all(send_last, ALL, 0, 0, tiled=True).reshape(2 * devices, width)
    mates = lax.all_to_all(send, ALL, 0, 0, tiled=True).reshape(16 * devices, width)

    x_mine = jnp.where(core == 0, x_img, x_txt)
    x_other = swap(jnp.where(core == 0, x_txt, x_img), "c", 1)

    own = jnp.concatenate([z_img, z_txt], axis=0)
    transposed = (((1,), (1,)), ((), ()))

    def coefficients(others):
        logits = scale * lax.dot_general(own, others, transposed, preferred_element_type=f32) + shift
        column = lax.broadcasted_iota(jnp.int32, logits.shape, 1) % 2
        row = lax.broadcasted_iota(jnp.int32, logits.shape, 0)
        keep = (count > 9) & ((column == 0) == (row < rows))
        return jnp.where(keep, scale * jax.nn.sigmoid(logits), 0.0).astype(bf16)

    logits = scale * lax.dot_general(z_img, z_txt, transposed, preferred_element_type=f32) + shift
    sign = jnp.where(jnp.eye(rows, dtype=bool), 1.0, -1.0)
    coef = (-scale * sign * jax.nn.sigmoid(-sign * logits)).astype(bf16)
    dz = jnp.concatenate(
        [
            jnp.dot(coef, z_txt, preferred_element_type=f32),
            lax.dot_general(coef, z_img, (((0,), (0,)), ((), ())), preferred_element_type=f32),
        ],
        axis=0,
    )
    dz = dz + jnp.dot(coefficients(mates_last), mates_last, preferred_element_type=f32)
    du = pair_stage(
        jnp.stack([scale, shift]),
        count[None],
        own,
        mates,
        dz,
        jnp.concatenate([f_img, f_txt], axis=0),
        jnp.concatenate([r_img, r_txt], axis=0),
    )
    du_img = du[:rows]
    du_txt = du[rows:]
    du_mine = jnp.where(core == 0, du_img, du_txt)
    du_other = swap(jnp.where(core == 0, du_txt, du_img), "c", 1)

    factor = (64.0 / (devices * rows)) ** 0.5
    grad = lax.dot_general(
        jnp.concatenate([x_mine, x_other], axis=0),
        jnp.concatenate([du_mine, du_other], axis=0),
        (((0,), (0,)), ((), ())),
        preferred_element_type=f32,
    )
    grad = (grad * factor).astype(bf16)

    def beside():
        g_img = lax.dot_general(du_img, w_img, transposed, preferred_element_type=f32).astype(bf16)
        g_txt = lax.dot_general(du_txt, w_txt, transposed, preferred_element_type=f32).astype(bf16)
        return (g_img, g_txt)

    kept, rest, quarter, (g_img, g_txt) = reduce_pieces(grad, beside)
    rest = jnp.concatenate(rest, axis=0)
    where = jnp.stack([quarter, core]).astype(jnp.int32)
    head_img, head_txt = assemble(where, kept, rest, swap(kept, "c", 1), swap(rest, "c", 1))
    return (g_img, g_txt, head_img, head_txt)


def solution(mesh):
    grid = Mesh(mesh.devices.reshape(4, 4, 4, 2), ALL)
    placed = (P(ALL, None), P(ALL, None), P(), P(), P(), P(), P(), P(), P())
    return jax.shard_map(
        local,
        mesh=grid,
        in_specs=placed,
        out_specs=(P(ALL, None), P(ALL, None), P(), P()),
        check_vma=False,
    )
```

```python
import jax
import jax.numpy as jnp
from jax import lax
from jax.experimental import pallas as pl
from jax.experimental.pallas import tpu as pltpu
from jax.sharding import Mesh, PartitionSpec as P

eps_norm = 1e-06
ALL = ("x", "z", "y", "c")
bf16 = jnp.bfloat16
f32 = jnp.float32
TRANSPOSED = (((1,), (1,)), ((), ()))
ROWS_FIRST = (((0,), (0,)), ((), ()))


def project(features, weight):
    product = jnp.dot(features, weight, preferred_element_type=f32)
    inverse = lax.rsqrt(jnp.sum(product * product, axis=-1, keepdims=True) + eps_norm)
    return (product * inverse, inverse)


def swap(array, axis, mask):
    return lax.ppermute(array, axis, [(i, i ^ mask) for i in range(lax.axis_size(axis))])


def take(array, index):
    return lax.dynamic_index_in_dim(array, index, 0, keepdims=False)


def total_of(own, got):
    total = (own.astype(f32) + got[0].astype(f32)) + (got[1].astype(f32) + got[2].astype(f32))
    return total.astype(bf16)


def reduce_window(grad):
    rows, width = grad.shape
    along_y, along_x = lax.axis_index("y"), lax.axis_index("x")
    quarters = grad.reshape(4, rows // 4, width)
    got = [swap(take(quarters, along_y ^ m), "y", m) for m in (2, 1, 3)]
    total = total_of(take(quarters, along_y), got)
    chunks = total.reshape(4, rows // 16, width)
    got = [swap(take(chunks, along_x ^ m), "x", m) for m in (2, 1, 3)]
    total = total_of(take(chunks, along_x), got)
    total = total_of(total, [swap(total, "z", m) for m in (1, 2, 3)])
    gathered = [total] + [swap(total, "x", m) for m in (1, 2, 3)]
    low, high = along_x & 1, along_x >> 1
    kept = [jnp.where(low == 0, gathered[j], gathered[j ^ 1]) for j in range(4)]
    kept = [jnp.where(high == 0, kept[j], kept[j ^ 2]) for j in range(4)]
    kept = jnp.concatenate(kept, axis=0)
    return [kept] + [swap(kept, "y", m) for m in (1, 2, 3)]


def assemble_kernel(where_ref, *refs):
    mine, other, out_ref = refs[:4], refs[4:8], refs[8]
    count = mine[0].shape[0]
    late = out_ref.shape[0] - 4 * count

    def write(pieces, first):
        for m in range(4):
            begin = pl.multiple_of(first + jnp.bitwise_xor(where_ref[0], m) * count, 32)
            out_ref[pl.ds(begin, count), :] = pieces[m][...].astype(f32)

    @pl.when(where_ref[1] == 0)
    def _():
        write(other, late)
        write(mine, 0)

    @pl.when(where_ref[1] != 0)
    def _():
        write(mine, late)
        write(other, 0)


def assemble(where, mine, other, rows):
    width = mine[0].shape[1]
    return pl.pallas_call(
        assemble_kernel,
        out_shape=jax.ShapeDtypeStruct((rows, width), f32),
        in_specs=[pl.BlockSpec(memory_space=pltpu.SMEM)] + [pl.BlockSpec(memory_space=pltpu.VMEM)] * 8,
        out_specs=pl.BlockSpec(memory_space=pltpu.VMEM),
        compiler_params=pltpu.CompilerParams(vmem_limit_bytes=40 * 2**20),
    )(where, *mine, *other)


def pair_kernel(number_ref, count_ref, own_ref, mates_ref, begin_ref, unit_ref, inverse_ref, out_ref, total):
    step = pl.program_id(0)
    scale, shift = number_ref[0], number_ref[1]
    mates = mates_ref[...]
    logits = lax.dot_general(own_ref[...], mates, TRANSPOSED, preferred_element_type=f32)
    logits = scale * logits + shift
    slot = (lax.broadcasted_iota(jnp.int32, logits.shape, 1) & 7) + 1
    coef = jnp.where(slot < count_ref[0], scale / (1.0 + jnp.exp(-logits)), 0.0).astype(bf16)
    part = jnp.dot(coef, mates, preferred_element_type=f32)

    @pl.when(step == 0)
    def _():
        total[...] = begin_ref[...] + part

    @pl.when(step != 0)
    def _():
        total[...] += part

    @pl.when(step == pl.num_programs(0) - 1)
    def _():
        unit = unit_ref[...]
        upstream = total[...]
        radial = jnp.sum(unit * upstream, axis=-1, keepdims=True)
        out_ref[...] = (inverse_ref[...] * (upstream - unit * radial)).astype(bf16)


def pair_stage(numbers, count, own, mates, begin, unit, inverse):
    rows, width = own.shape
    per = 512

    def whole(shape):
        return pl.BlockSpec(shape, lambda i: (0, 0))

    return pl.pallas_call(
        pair_kernel,
        grid=(mates.shape[0] // per,),
        out_shape=jax.ShapeDtypeStruct((rows, width), bf16),
        in_specs=[
            pl.BlockSpec(memory_space=pltpu.SMEM),
            pl.BlockSpec(memory_space=pltpu.SMEM),
            whole((rows, width)),
            pl.BlockSpec((per, width), lambda i: (i, 0)),
            whole((rows, width)),
            whole((rows, width)),
            whole((rows, 1)),
        ],
        out_specs=whole((rows, width)),
        scratch_shapes=[pltpu.VMEM((rows, width), f32)],
        compiler_params=pltpu.CompilerParams(vmem_limit_bytes=40 * 2**20),
    )(numbers, count, own, mates, begin, unit, inverse)


def head_kernel(factor, dtype, count, *refs):
    out_ref = refs[2 * count]
    total = None
    for k in range(count):
        part = lax.dot_general(refs[2 * k][...], refs[2 * k + 1][...], ROWS_FIRST, preferred_element_type=f32)
        total = part if total is None else total + part
    out_ref[...] = (total * factor).astype(dtype)


def head_gradient(factor, dtype, *pairs):
    rows, columns = pairs[0][0].shape
    width = pairs[0][1].shape[1]
    per = 384 if columns % 384 == 0 else 128
    specs = []
    for _ in range(len(pairs)):
        specs += [pl.BlockSpec((rows, per), lambda i: (0, i)), pl.BlockSpec((rows, width), lambda i: (0, 0))]

    def body(*refs):
        head_kernel(factor, dtype, len(pairs), *refs)

    return pl.pallas_call(
        body,
        grid=(columns // per,),
        out_shape=jax.ShapeDtypeStruct((columns, width), dtype),
        in_specs=specs,
        out_specs=pl.BlockSpec((per, width), lambda i: (i, 0)),
        compiler_params=pltpu.CompilerParams(vmem_limit_bytes=40 * 2**20),
    )(*[array for pair in pairs for array in pair])


def local(x_img, x_txt, w_img, w_txt, sharpness, offset, lists, counts, holder):
    devices = lax.axis_size(ALL)
    me = lax.axis_index(ALL)
    core = lax.axis_index("c")
    rows, width = x_img.shape
    scale = sharpness[0]
    shift = offset[0]
    f_txt, r_txt = project(x_txt, w_txt)
    f_img, r_img = project(x_img, w_img)
    z_txt = f_txt.astype(bf16)
    z_img = f_img.astype(bf16)

    spread = lax.all_to_all(jnp.stack([z_txt, z_img], axis=1), ALL, 0, 0, tiled=True)
    spread = spread.reshape(2 * devices, width)

    numbers = jnp.arange(devices, dtype=jnp.int32)
    hot = holder[None, :] == numbers[:, None]
    source = jnp.sum(jnp.where(lists[:, :, None] == numbers, holder, 0), axis=2)
    table = jnp.dot(hot.astype(bf16), source.astype(bf16), preferred_element_type=f32).astype(jnp.int32)
    count = jnp.sum(jnp.where(hot[me], counts, 0))

    columns = jnp.arange(2 * devices, dtype=jnp.int32)

    def chosen(wanted):
        pick = (wanted[:, :, None] == columns).astype(bf16).reshape(-1, 2 * devices)
        rows_out = jnp.dot(pick, spread, preferred_element_type=f32).astype(bf16)
        return rows_out.reshape(devices, wanted.shape[1], width)

    def fetch(send):
        return lax.all_to_all(send, ALL, 0, 0, tiled=True).reshape(-1, width)

    last = fetch(chosen(jnp.concatenate([2 * table[:, 9:], 2 * table[:, 9:] + 1], axis=1)))
    send_txt, last = lax.optimization_barrier((chosen(2 * table[:, 1:9]), last))
    mates_txt = fetch(send_txt)
    send_img, mates_txt = lax.optimization_barrier((chosen(2 * table[:, 1:9] + 1), mates_txt))
    mates_img = fetch(send_img)

    window = 640
    late = width - window
    x_mine = lax.dynamic_slice_in_dim(x_txt, core * late, window, 1)
    x_other = swap(lax.dynamic_slice_in_dim(x_txt, (1 - core) * late, window, 1), "c", 1)

    def last_slot(own, tower):
        logits = scale * lax.dot_general(own, last, TRANSPOSED, preferred_element_type=f32) + shift
        column = lax.broadcasted_iota(jnp.int32, logits.shape, 1) % 2
        coef = jnp.where((count > 9) & (column == tower), scale * jax.nn.sigmoid(logits), 0.0).astype(bf16)
        return jnp.dot(coef, last, preferred_element_type=f32)

    logits = scale * lax.dot_general(z_img, z_txt, TRANSPOSED, preferred_element_type=f32) + shift
    sign = jnp.where(jnp.eye(rows, dtype=bool), 1.0, -1.0)
    coef = (-scale * sign * jax.nn.sigmoid(-sign * logits)).astype(bf16)
    dz_img = jnp.dot(coef, z_txt, preferred_element_type=f32) + last_slot(z_img, 0)
    dz_txt = lax.dot_general(coef, z_img, ROWS_FIRST, preferred_element_type=f32) + last_slot(z_txt, 1)

    numbers = jnp.stack([scale, shift])
    factor = (64.0 / (devices * rows)) ** 0.5
    du_img = pair_stage(numbers, count[None], z_img, mates_txt, dz_img, f_img, r_img)
    part_img = head_gradient(factor, f32, (x_img, du_img))
    part_img, mates_img, dz_txt = lax.optimization_barrier((part_img, mates_img, dz_txt))
    head_img = lax.psum(part_img, ALL)
    g_img = lax.dot_general(du_img, w_img, TRANSPOSED, preferred_element_type=f32).astype(bf16)

    du_txt = pair_stage(numbers, count[None], z_txt, mates_img, dz_txt, f_txt, r_txt)
    du_other = swap(du_txt, "c", 1)
    g_txt = lax.dot_general(du_txt, w_txt, TRANSPOSED, preferred_element_type=f32).astype(bf16)
    pieces = reduce_window(head_gradient(factor, bf16, (x_mine, du_txt), (x_other, du_other)))
    where = jnp.stack([lax.axis_index("y"), core]).astype(jnp.int32)
    head_txt = assemble(where, pieces, [swap(piece, "c", 1) for piece in pieces], width)
    return (g_img, g_txt, head_img, head_txt)


def solution(mesh):
    grid = Mesh(mesh.devices.reshape(4, 4, 4, 2), ALL)
    placed = (P(ALL, None), P(ALL, None), P(), P(), P(), P(), P(), P(), P())
    return jax.shard_map(
        local,
        mesh=grid,
        in_specs=placed,
        out_specs=(P(ALL, None), P(ALL, None), P(), P()),
        check_vma=False,
    )
```

```python
import jax
import jax.numpy as jnp
from jax import lax
from jax.experimental import pallas as pl
from jax.experimental.pallas import tpu as pltpu
from jax.sharding import Mesh, PartitionSpec as P

eps_norm = 1e-06
ALL = ("x", "z", "y", "c")
TRANSPOSED = (((1,), (1,)), ((), ()))
ROWS_FIRST = (((0,), (0,)), ((), ()))
STREAMS = ((640, ("y", "x", "z")), (512, ("x", "z", "y")))
bf16 = jnp.bfloat16
f32 = jnp.float32


def project(features, weight):
    product = jnp.dot(features, weight, preferred_element_type=f32)
    inverse = lax.rsqrt(jnp.sum(product * product, axis=-1, keepdims=True) + eps_norm)
    return (product * inverse, inverse)


def swap(array, axis, mask):
    return lax.ppermute(array, axis, [(i, i ^ mask) for i in range(lax.axis_size(axis))])


def take(array, index):
    return lax.dynamic_index_in_dim(array, index, 0, keepdims=False)


def total_of(own, got):
    total = (own.astype(f32) + got[0].astype(f32)) + (got[1].astype(f32) + got[2].astype(f32))
    return total.astype(bf16)


def scatter_sum(block, axis):
    index = lax.axis_index(axis)
    quarters = block.reshape(4, block.shape[0] // 4, block.shape[1])
    got = [swap(take(quarters, index ^ m), axis, m) for m in (1, 3, 2)]
    return total_of(take(quarters, index), got)


def reduce_stream(block, axes):
    total = scatter_sum(block, axes[0])
    total = scatter_sum(total, axes[1])
    total = total_of(total, [swap(total, axes[2], m) for m in (1, 3, 2)])
    gathered = {m: swap(total, axes[1], m) for m in (1, 3, 2)}
    gathered[0] = total
    index = lax.axis_index(axes[1])
    low, high = index & 1, index >> 1
    kept = [jnp.where(low == 0, gathered[j], gathered[j ^ 1]) for j in range(4)]
    kept = [jnp.where(high == 0, kept[j], kept[j ^ 2]) for j in range(4)]
    kept = jnp.concatenate(kept, axis=0)
    others = {m: swap(kept, axes[0], m) for m in (1, 3, 2)}
    return jnp.concatenate([kept] + [others[m] for m in (1, 2, 3)], axis=0)


def assemble_kernel(where_ref, *refs):
    pieces, out_img, out_txt, wide, sems = refs[:4], refs[4], refs[5], refs[6], refs[7]

    def run(own_out, other_out):
        copies = []
        first = 0
        for stream in range(2):
            size = pieces[2 * stream].shape[0]
            count = size // 4
            for side, target in ((0, own_out), (1, other_out)):
                piece = pieces[2 * stream + side]
                for m in range(4):
                    k = len(copies)
                    at = first + m * count
                    wide[side, at : at + count] = piece[m * count : (m + 1) * count].astype(f32)
                    begin = pl.multiple_of(first + jnp.bitwise_xor(where_ref[stream], m) * count, 32)
                    copy = pltpu.make_async_copy(
                        wide.at[side, pl.ds(at, count)], target.at[pl.ds(begin, count)], sems.at[k]
                    )
                    copy.start()
                    copies.append(copy)
            first += size
        for copy in copies:
            copy.wait()

    @pl.when(where_ref[2] == 0)
    def _():
        run(out_img, out_txt)

    @pl.when(where_ref[2] != 0)
    def _():
        run(out_txt, out_img)


def assemble(where, pieces, rows):
    width = pieces[0].shape[1]
    shape = jax.ShapeDtypeStruct((rows, width), f32)
    return pl.pallas_call(
        assemble_kernel,
        out_shape=(shape, shape),
        in_specs=[pl.BlockSpec(memory_space=pltpu.SMEM)] + [pl.BlockSpec(memory_space=pltpu.VMEM)] * 4,
        out_specs=(pl.BlockSpec(memory_space=pl.ANY),) * 2,
        scratch_shapes=[pltpu.VMEM((2, rows, width), f32), pltpu.SemaphoreType.DMA((16,))],
        compiler_params=pltpu.CompilerParams(vmem_limit_bytes=40 * 2**20),
    )(where, *pieces)


def pair_kernel(number_ref, count_ref, own_ref, mates_ref, begin_ref, out_ref):
    scale, shift = number_ref[0], number_ref[1]
    mates = mates_ref[...]
    logits = lax.dot_general(own_ref[...], mates, TRANSPOSED, preferred_element_type=f32)
    logits = scale * logits + shift
    column = lax.broadcasted_iota(jnp.int32, logits.shape, 1) & 15
    row = lax.broadcasted_iota(jnp.int32, logits.shape, 0)
    keep = ((column & 7) + 1 < count_ref[0]) & ((column < 8) == (row < logits.shape[0] // 2))
    coef = jnp.where(keep, scale / (1.0 + jnp.exp(-logits)), 0.0).astype(bf16)
    part = jnp.dot(coef, mates, preferred_element_type=f32)

    @pl.when(pl.program_id(0) == 0)
    def _():
        out_ref[...] = begin_ref[...] + part

    @pl.when(pl.program_id(0) != 0)
    def _():
        out_ref[...] += part


def pair_stage(numbers, count, own, mates, begin):
    rows, width = own.shape
    per = 512

    def whole(shape):
        return pl.BlockSpec(shape, lambda i: (0, 0))

    return pl.pallas_call(
        pair_kernel,
        grid=(mates.shape[0] // per,),
        out_shape=jax.ShapeDtypeStruct((rows, width), f32),
        in_specs=[
            pl.BlockSpec(memory_space=pltpu.SMEM),
            pl.BlockSpec(memory_space=pltpu.SMEM),
            whole((rows, width)),
            pl.BlockSpec((per, width), lambda i: (i, 0)),
            whole((rows, width)),
        ],
        out_specs=whole((rows, width)),
        compiler_params=pltpu.CompilerParams(vmem_limit_bytes=40 * 2**20),
    )(numbers, count, own, mates, begin)


def finish_kernel(number_ref, count_ref, own_ref, last_ref, begin_ref, unit_ref, inverse_ref, out_ref):
    scale, shift = number_ref[0], number_ref[1]
    last = last_ref[...]
    logits = lax.dot_general(own_ref[...], last, TRANSPOSED, preferred_element_type=f32)
    logits = scale * logits + shift
    column = lax.broadcasted_iota(jnp.int32, logits.shape, 1) & 1
    row = lax.broadcasted_iota(jnp.int32, logits.shape, 0)
    keep = (count_ref[0] > 9) & ((column == 0) == (row < logits.shape[0] // 2))
    coef = jnp.where(keep, scale / (1.0 + jnp.exp(-logits)), 0.0).astype(bf16)
    upstream = begin_ref[...] + jnp.dot(coef, last, preferred_element_type=f32)
    unit = unit_ref[...]
    radial = jnp.sum(unit * upstream, axis=-1, keepdims=True)
    out_ref[...] = (inverse_ref[...] * (upstream - unit * radial)).astype(bf16)


def finish_stage(numbers, count, own, last, begin, unit, inverse):
    vmem = pl.BlockSpec(memory_space=pltpu.VMEM)
    return pl.pallas_call(
        finish_kernel,
        out_shape=jax.ShapeDtypeStruct(own.shape, bf16),
        in_specs=[pl.BlockSpec(memory_space=pltpu.SMEM)] * 2 + [vmem] * 5,
        out_specs=vmem,
        compiler_params=pltpu.CompilerParams(vmem_limit_bytes=40 * 2**20),
    )(numbers, count, own, last, begin, unit, inverse)


def local(x_img, x_txt, w_img, w_txt, sharpness, offset, lists, counts, holder):
    devices = lax.axis_size(ALL)
    me = lax.axis_index(ALL)
    core = lax.axis_index("c")
    rows, width = x_img.shape
    slots = lists.shape[1]
    scale = sharpness[0]
    shift = offset[0]
    f_txt, r_txt = project(x_txt, w_txt)
    f_img, r_img = project(x_img, w_img)
    z_txt = f_txt.astype(bf16)
    z_img = f_img.astype(bf16)

    spread = lax.all_to_all(jnp.stack([z_txt, z_img], axis=1), ALL, 0, 0, tiled=True)
    spread = spread.reshape(2 * devices, width)

    numbers = jnp.arange(devices, dtype=jnp.int32)
    hot = holder[None, :] == numbers[:, None]
    source = jnp.sum(jnp.where(lists[:, :, None] == numbers, holder, 0), axis=2)
    table = jnp.dot(hot.astype(bf16), source.astype(bf16), preferred_element_type=f32).astype(jnp.int32)
    count = jnp.sum(jnp.where(hot[me], counts, 0))

    columns = jnp.arange(2 * devices, dtype=jnp.int32)
    near = jnp.concatenate([2 * table[:, 1:9], 2 * table[:, 1:9] + 1], axis=1)
    last = jnp.concatenate([2 * table[:, 9:], 2 * table[:, 9:] + 1], axis=1)
    pick = (near[:, :, None] == columns).astype(bf16).reshape(16 * devices, 2 * devices)
    pick_last = (last[:, :, None] == columns).astype(bf16).reshape(2 * devices, 2 * devices)
    send_last = jnp.dot(pick_last, spread, preferred_element_type=f32).astype(bf16).reshape(devices, 2, width)
    send = jnp.dot(pick, spread, preferred_element_type=f32).astype(bf16).reshape(devices, 16, width)
    mates = lax.all_to_all(send, ALL, 0, 0, tiled=True).reshape(16 * devices, width)
    mates, send_last = lax.optimization_barrier((mates, send_last))
    last = lax.all_to_all(send_last, ALL, 0, 0, tiled=True).reshape(2 * devices, width)

    x_mine = jnp.where(core == 0, x_img, x_txt)
    x_other = swap(jnp.where(core == 0, x_txt, x_img), "c", 1)

    own = jnp.concatenate([z_img, z_txt], axis=0)
    logits = scale * lax.dot_general(z_img, z_txt, TRANSPOSED, preferred_element_type=f32) + shift
    sign = jnp.where(jnp.eye(rows, dtype=bool), 1.0, -1.0)
    coef = (-scale * sign * jax.nn.sigmoid(-sign * logits)).astype(bf16)
    dz = jnp.concatenate(
        [
            jnp.dot(coef, z_txt, preferred_element_type=f32),
            lax.dot_general(coef, z_img, ROWS_FIRST, preferred_element_type=f32),
        ],
        axis=0,
    )
    unit = jnp.concatenate([f_img, f_txt], axis=0)
    inverse = jnp.concatenate([r_img, r_txt], axis=0)
    scalars = jnp.stack([scale, shift])
    dz = pair_stage(scalars, count[None], own, mates, dz)
    du = finish_stage(scalars, count[None], own, last, dz, unit, inverse)
    du_img = du[:rows]
    du_txt = du[rows:]
    du_mine = jnp.where(core == 0, du_img, du_txt)
    du_other = swap(jnp.where(core == 0, du_txt, du_img), "c", 1)

    factor = (64.0 / (devices * rows)) ** 0.5
    grad = lax.dot_general(
        jnp.concatenate([x_mine, x_other], axis=0),
        jnp.concatenate([du_mine, du_other], axis=0),
        ROWS_FIRST,
        preferred_element_type=f32,
    )
    grad = (grad * factor).astype(bf16)
    g_img = lax.dot_general(du_img, w_img, TRANSPOSED, preferred_element_type=f32).astype(bf16)
    g_txt = lax.dot_general(du_txt, w_txt, TRANSPOSED, preferred_element_type=f32).astype(bf16)

    pieces = []
    first = 0
    for size, axes in STREAMS:
        mine = reduce_stream(grad[first : first + size], axes)
        pieces += [mine, swap(mine, "c", 1)]
        first += size
    where = jnp.stack([lax.axis_index(axes[0]) for _, axes in STREAMS] + [core]).astype(jnp.int32)
    head_img, head_txt = assemble(where, pieces, width)
    return (g_img, g_txt, head_img, head_txt)


def solution(mesh):
    grid = Mesh(mesh.devices.reshape(4, 4, 4, 2), ALL)
    placed = (P(ALL, None), P(ALL, None), P(), P(), P(), P(), P(), P(), P())
    return jax.shard_map(
        local,
        mesh=grid,
        in_specs=placed,
        out_specs=(P(ALL, None), P(ALL, None), P(), P()),
        check_vma=False,
    )
```

```python
import jax
import jax.numpy as jnp
from jax import lax
from jax.experimental import pallas as pl
from jax.experimental.pallas import tpu as pltpu
from jax.sharding import Mesh, PartitionSpec as P

eps_norm = 1e-06
ALL = ("x", "z", "y", "c")
TRANSPOSED = (((1,), (1,)), ((), ()))
ROWS_FIRST = (((0,), (0,)), ((), ()))
STREAMS = ((640, ("y", "x", "z")), (512, ("x", "z", "y")))
bf16 = jnp.bfloat16
f32 = jnp.float32


def project(features, weight):
    product = jnp.dot(features, weight, preferred_element_type=f32)
    inverse = lax.rsqrt(jnp.sum(product * product, axis=-1, keepdims=True) + eps_norm)
    return (product * inverse, inverse)


def swap(array, axis, mask):
    return lax.ppermute(array, axis, [(i, i ^ mask) for i in range(lax.axis_size(axis))])


def take(array, index):
    return lax.dynamic_index_in_dim(array, index, 0, keepdims=False)


def total_of(own, got):
    total = (own.astype(f32) + got[0].astype(f32)) + (got[1].astype(f32) + got[2].astype(f32))
    return total.astype(bf16)


def whole(shape):
    return pl.BlockSpec(shape, lambda i: (0,) * len(shape))


def kernel_call(body, outs, scalars, arrays, scratch=()):
    return pl.pallas_call(
        body,
        grid=(1,),
        out_shape=outs,
        in_specs=[pl.BlockSpec(memory_space=pltpu.SMEM)] * len(scalars) + [whole(a.shape) for a in arrays],
        out_specs=tuple(whole(o.shape) for o in outs),
        scratch_shapes=scratch,
        compiler_params=pltpu.CompilerParams(vmem_limit_bytes=40 * 2**20),
    )(*scalars, *arrays)


def quarters_of(sizes, width, parts):
    return tuple(jax.ShapeDtypeStruct((size // parts, width), bf16) for size in sizes for _ in range(4))


def head_gradient(factor, index, features, through):
    rows, columns = features[0].shape
    width = through[0].shape[1]
    sizes = [size for size, _ in STREAMS]
    per = columns // 3

    def body(index_ref, xa, xb, da, db, *rest):
        outs, total = rest[:8], rest[8]
        for k in range(3):
            part = slice(k * per, (k + 1) * per)
            grad = lax.dot_general(xa[:, part], da[...], ROWS_FIRST, preferred_element_type=f32)
            grad += lax.dot_general(xb[:, part], db[...], ROWS_FIRST, preferred_element_type=f32)
            total[part] = grad * factor
        first = 0
        for stream, size in enumerate(sizes):
            count = size // 4
            for m in range(4):
                begin = pl.multiple_of(first + jnp.bitwise_xor(index_ref[stream], m) * count, 32)
                outs[4 * stream + m][...] = total[pl.ds(begin, count), :].astype(bf16)
            first += size

    outs = quarters_of(sizes, width, 4)
    return kernel_call(body, outs, (index,), (*features, *through), (pltpu.VMEM((columns, width), f32),))


def sum_and_split(index, pieces):
    width = pieces[0].shape[1]
    sizes = [pieces[0].shape[0], pieces[4].shape[0]]

    def body(index_ref, *refs):
        ins, outs, total = refs[:8], refs[8:16], refs[16:]
        for stream in range(2):
            a, b, c, d = (ins[4 * stream + m][...].astype(f32) for m in range(4))
            total[stream][...] = (a + b) + (c + d)
            count = sizes[stream] // 4
            for m in range(4):
                begin = pl.multiple_of(jnp.bitwise_xor(index_ref[stream], m) * count, 8)
                outs[4 * stream + m][...] = total[stream][pl.ds(begin, count), :].astype(bf16)

    outs = quarters_of(sizes, width, 4)
    scratch = tuple(pltpu.VMEM((size, width), f32) for size in sizes)
    return kernel_call(body, outs, (index,), pieces, scratch)


def exchange(pieces, phase):
    got = list(pieces)
    for m in (1, 3, 2):
        for stream, (_, axes) in enumerate(STREAMS):
            got[4 * stream + m] = swap(pieces[4 * stream + m], axes[phase], m)
    return lax.optimization_barrier(got)


def reduce_streams(pieces, index_second):
    pieces = sum_and_split(index_second, exchange(pieces, 0))
    pieces = exchange(pieces, 1)
    totals = [total_of(pieces[k], pieces[k + 1 : k + 4]) for k in (0, 4)]
    pieces = exchange([totals[0]] * 4 + [totals[1]] * 4, 2)
    totals = [total_of(pieces[k], pieces[k + 1 : k + 4]) for k in (0, 4)]
    pieces = exchange([totals[0]] * 4 + [totals[1]] * 4, 1)
    kept = []
    for stream in range(2):
        low, high = index_second[stream] & 1, index_second[stream] >> 1
        four = pieces[4 * stream : 4 * stream + 4]
        four = [jnp.where(low == 0, four[j], four[j ^ 1]) for j in range(4)]
        four = [jnp.where(high == 0, four[j], four[j ^ 2]) for j in range(4)]
        kept.append(jnp.concatenate(four, axis=0))
    return exchange([kept[0]] * 4 + [kept[1]] * 4, 0)


def assemble_kernel(index_ref, core_ref, *refs):
    pieces, (out_img, out_txt, wide, sems) = refs[:16], refs[16:]

    def run(own_out, other_out):
        copies = []
        first = 0
        for stream in range(2):
            count = pieces[8 * stream].shape[0]
            for side, target in ((0, own_out), (1, other_out)):
                for m in range(4):
                    k = len(copies)
                    at = first + m * count
                    wide[side, at : at + count] = pieces[8 * stream + 4 * side + m][...].astype(f32)
                    begin = pl.multiple_of(first + jnp.bitwise_xor(index_ref[stream], m) * count, 32)
                    copy = pltpu.make_async_copy(
                        wide.at[side, pl.ds(at, count)], target.at[pl.ds(begin, count)], sems.at[k]
                    )
                    copy.start()
                    copies.append(copy)
            first += 4 * count
        for copy in copies:
            copy.wait()

    @pl.when(core_ref[0] == 0)
    def _():
        run(out_img, out_txt)

    @pl.when(core_ref[0] != 0)
    def _():
        run(out_txt, out_img)


def assemble(index, core, pieces, rows):
    width = pieces[0].shape[1]
    shape = jax.ShapeDtypeStruct((rows, width), f32)
    return pl.pallas_call(
        assemble_kernel,
        grid=(1,),
        out_shape=(shape, shape),
        in_specs=[pl.BlockSpec(memory_space=pltpu.SMEM)] * 2 + [whole(piece.shape) for piece in pieces],
        out_specs=(pl.BlockSpec(memory_space=pl.ANY),) * 2,
        scratch_shapes=[pltpu.VMEM((2, rows, width), f32), pltpu.SemaphoreType.DMA((16,))],
        compiler_params=pltpu.CompilerParams(vmem_limit_bytes=40 * 2**20),
    )(index, core, *pieces)


def pair_kernel(number_ref, count_ref, own_ref, mates_ref, begin_ref, out_ref):
    scale, shift = number_ref[0], number_ref[1]
    mates = mates_ref[...]
    logits = lax.dot_general(own_ref[...], mates, TRANSPOSED, preferred_element_type=f32)
    logits = scale * logits + shift
    column = lax.broadcasted_iota(jnp.int32, logits.shape, 1) & 15
    row = lax.broadcasted_iota(jnp.int32, logits.shape, 0)
    keep = ((column & 7) + 1 < count_ref[0]) & ((column < 8) == (row < logits.shape[0] // 2))
    coef = jnp.where(keep, scale / (1.0 + jnp.exp(-logits)), 0.0).astype(bf16)
    part = jnp.dot(coef, mates, preferred_element_type=f32)

    @pl.when(pl.program_id(0) == 0)
    def _():
        out_ref[...] = begin_ref[...] + part

    @pl.when(pl.program_id(0) != 0)
    def _():
        out_ref[...] += part


def pair_stage(numbers, count, own, mates, begin):
    rows, width = own.shape
    per = 512

    return pl.pallas_call(
        pair_kernel,
        grid=(mates.shape[0] // per,),
        out_shape=jax.ShapeDtypeStruct((rows, width), f32),
        in_specs=[
            pl.BlockSpec(memory_space=pltpu.SMEM),
            pl.BlockSpec(memory_space=pltpu.SMEM),
            whole((rows, width)),
            pl.BlockSpec((per, width), lambda i: (i, 0)),
            whole((rows, width)),
        ],
        out_specs=whole((rows, width)),
        compiler_params=pltpu.CompilerParams(vmem_limit_bytes=40 * 2**20),
    )(numbers, count, own, mates, begin)


def finish_kernel(number_ref, count_ref, own_ref, last_ref, begin_ref, unit_ref, inverse_ref, out_ref):
    scale, shift = number_ref[0], number_ref[1]
    rows = out_ref.shape[0] // 2
    for tower in range(2):
        part = slice(tower * rows, (tower + 1) * rows)
        mates = last_ref[:, tower, :]
        logits = lax.dot_general(own_ref[part], mates, TRANSPOSED, preferred_element_type=f32)
        logits = scale * logits + shift
        coef = jnp.where(count_ref[0] > 9, scale / (1.0 + jnp.exp(-logits)), 0.0).astype(bf16)
        upstream = begin_ref[part] + jnp.dot(coef, mates, preferred_element_type=f32)
        unit = unit_ref[part]
        radial = jnp.sum(unit * upstream, axis=-1, keepdims=True)
        out_ref[part] = (inverse_ref[part] * (upstream - unit * radial)).astype(bf16)


def local(x_img, x_txt, w_img, w_txt, sharpness, offset, lists, counts, holder):
    devices = lax.axis_size(ALL)
    me = lax.axis_index(ALL)
    core = lax.axis_index("c")
    rows, width = x_img.shape
    slots = lists.shape[1]
    scale = sharpness[0]
    shift = offset[0]
    f_txt, r_txt = project(x_txt, w_txt)
    f_img, r_img = project(x_img, w_img)
    z_txt = f_txt.astype(bf16)
    z_img = f_img.astype(bf16)

    spread = lax.all_to_all(jnp.stack([z_txt, z_img], axis=1), ALL, 0, 0, tiled=True)
    spread = spread.reshape(2 * devices, width)

    numbers = jnp.arange(devices, dtype=jnp.int32)
    hot = holder[None, :] == numbers[:, None]
    source = jnp.sum(jnp.where(lists[:, :, None] == numbers, holder, 0), axis=2)
    table = jnp.dot(hot.astype(bf16), source.astype(bf16), preferred_element_type=f32).astype(jnp.int32)
    count = jnp.sum(jnp.where(hot[me], counts, 0))

    columns = jnp.arange(2 * devices, dtype=jnp.int32)
    near = jnp.concatenate([2 * table[:, 1:9], 2 * table[:, 1:9] + 1], axis=1)
    last = jnp.concatenate([2 * table[:, 9:], 2 * table[:, 9:] + 1], axis=1)
    pick = (near[:, :, None] == columns).astype(bf16).reshape(16 * devices, 2 * devices)
    pick_last = (last[:, :, None] == columns).astype(bf16).reshape(2 * devices, 2 * devices)
    send_last = jnp.dot(pick_last, spread, preferred_element_type=f32).astype(bf16).reshape(devices, 2, width)
    send = jnp.dot(pick, spread, preferred_element_type=f32).astype(bf16).reshape(devices, 16, width)
    mates = lax.all_to_all(send, ALL, 0, 0, tiled=True).reshape(16 * devices, width)
    mates, send_last = lax.optimization_barrier((mates, send_last))
    last = lax.all_to_all(send_last, ALL, 0, 0, tiled=True)

    x_mine = jnp.where(core == 0, x_img, x_txt)
    x_other = swap(jnp.where(core == 0, x_txt, x_img), "c", 1)

    own = jnp.concatenate([z_img, z_txt], axis=0)
    logits = scale * lax.dot_general(z_img, z_txt, TRANSPOSED, preferred_element_type=f32) + shift
    sign = jnp.where(jnp.eye(rows, dtype=bool), 1.0, -1.0)
    coef = (-scale * sign * jax.nn.sigmoid(-sign * logits)).astype(bf16)
    dz = jnp.concatenate(
        [
            jnp.dot(coef, z_txt, preferred_element_type=f32),
            lax.dot_general(coef, z_img, ROWS_FIRST, preferred_element_type=f32),
        ],
        axis=0,
    )
    unit = jnp.concatenate([f_img, f_txt], axis=0)
    inverse = jnp.concatenate([r_img, r_txt], axis=0)
    scalars = jnp.stack([scale, shift])
    dz = pair_stage(scalars, count[None], own, mates, dz)
    (du,) = kernel_call(
        finish_kernel,
        (jax.ShapeDtypeStruct(own.shape, bf16),),
        (scalars, count[None]),
        (own, last, dz, unit, inverse),
    )
    du_img = du[:rows]
    du_txt = du[rows:]
    du_mine = jnp.where(core == 0, du_img, du_txt)
    du_other = swap(jnp.where(core == 0, du_txt, du_img), "c", 1)
    g_img = lax.dot_general(du_img, w_img, TRANSPOSED, preferred_element_type=f32).astype(bf16)
    g_txt = lax.dot_general(du_txt, w_txt, TRANSPOSED, preferred_element_type=f32).astype(bf16)

    factor = (64.0 / (devices * rows)) ** 0.5
    index_first, index_second = (
        jnp.stack([lax.axis_index(axes[k]) for _, axes in STREAMS]).astype(jnp.int32) for k in (0, 1)
    )
    pieces = head_gradient(factor, index_first, (x_mine, x_other), (du_mine, du_other))
    pieces = reduce_streams(pieces, index_second)
    others = [swap(piece, "c", 1) for piece in pieces]
    pieces = pieces[:4] + others[:4] + pieces[4:] + others[4:]
    head_img, head_txt = assemble(index_first, core[None].astype(jnp.int32), pieces, width)
    return (g_img, g_txt, head_img, head_txt)


def solution(mesh):
    grid = Mesh(mesh.devices.reshape(4, 4, 4, 2), ALL)
    placed = (P(ALL, None), P(ALL, None), P(), P(), P(), P(), P(), P(), P())
    return jax.shard_map(
        local,
        mesh=grid,
        in_specs=placed,
        out_specs=(P(ALL, None), P(ALL, None), P(), P()),
        check_vma=False,
    )
```

```python
import jax
import jax.numpy as jnp
from jax import lax
from jax.experimental import pallas as pl
from jax.experimental.pallas import tpu as pltpu
from jax.sharding import Mesh, PartitionSpec as P

eps_norm = 1e-06
ALL = ("x", "z", "y", "c")
TRANSPOSED = (((1,), (1,)), ((), ()))
ROWS_FIRST = (((0,), (0,)), ((), ()))
STREAMS = ((640, ("y", "x", "z")), (512, ("x", "z", "y")))
bf16 = jnp.bfloat16
f32 = jnp.float32


def project(features, weight):
    product = jnp.dot(features, weight, preferred_element_type=f32)
    inverse = lax.rsqrt(jnp.sum(product * product, axis=-1, keepdims=True) + eps_norm)
    return ((product * inverse).astype(bf16), inverse)


def swap(array, axis, mask):
    return lax.ppermute(array, axis, [(i, i ^ mask) for i in range(lax.axis_size(axis))])


def take(array, index):
    return lax.dynamic_index_in_dim(array, index, 0, keepdims=False)


def total_of(own, got):
    total = (own.astype(f32) + got[0].astype(f32)) + (got[1].astype(f32) + got[2].astype(f32))
    return total.astype(bf16)


def whole(shape):
    return pl.BlockSpec(shape, lambda i: (0,) * len(shape))


def kernel_call(body, outs, scalars, arrays, scratch=()):
    return pl.pallas_call(
        body,
        grid=(1,),
        out_shape=outs,
        in_specs=[pl.BlockSpec(memory_space=pltpu.SMEM)] * len(scalars) + [whole(a.shape) for a in arrays],
        out_specs=tuple(whole(o.shape) for o in outs),
        scratch_shapes=scratch,
        compiler_params=pltpu.CompilerParams(vmem_limit_bytes=40 * 2**20),
    )(*scalars, *arrays)


def quarters_of(sizes, width, parts):
    return tuple(jax.ShapeDtypeStruct((size // parts, width), bf16) for size in sizes for _ in range(4))


def head_gradient(factor, index, features, through):
    rows, columns = features[0].shape
    width = through[0].shape[1]
    sizes = [size for size, _ in STREAMS]
    per = columns // 3

    def body(index_ref, xa, xb, da, db, *rest):
        outs, total = rest[:8], rest[8]
        for k in range(3):
            part = slice(k * per, (k + 1) * per)
            grad = lax.dot_general(xa[:, part], da[...], ROWS_FIRST, preferred_element_type=f32)
            grad += lax.dot_general(xb[:, part], db[...], ROWS_FIRST, preferred_element_type=f32)
            total[part] = grad * factor
        first = 0
        for stream, size in enumerate(sizes):
            count = size // 4
            for m in range(4):
                begin = pl.multiple_of(first + jnp.bitwise_xor(index_ref[stream], m) * count, 32)
                outs[4 * stream + m][...] = total[pl.ds(begin, count), :].astype(bf16)
            first += size

    outs = quarters_of(sizes, width, 4)
    return kernel_call(body, outs, (index,), (*features, *through), (pltpu.VMEM((columns, width), f32),))


def sum_and_split(index, pieces):
    width = pieces[0].shape[1]
    sizes = [pieces[0].shape[0], pieces[4].shape[0]]

    def body(index_ref, *refs):
        ins, outs, total = refs[:8], refs[8:16], refs[16:]
        for stream in range(2):
            a, b, c, d = (ins[4 * stream + m][...].astype(f32) for m in range(4))
            total[stream][...] = (a + b) + (c + d)
            count = sizes[stream] // 4
            for m in range(4):
                begin = pl.multiple_of(jnp.bitwise_xor(index_ref[stream], m) * count, 8)
                outs[4 * stream + m][...] = total[stream][pl.ds(begin, count), :].astype(bf16)

    outs = quarters_of(sizes, width, 4)
    scratch = tuple(pltpu.VMEM((size, width), f32) for size in sizes)
    return kernel_call(body, outs, (index,), pieces, scratch)


def exchange(pieces, phase):
    got = list(pieces)
    for m in (1, 3, 2):
        for stream, (_, axes) in enumerate(STREAMS):
            got[4 * stream + m] = swap(pieces[4 * stream + m], axes[phase], m)
    return lax.optimization_barrier(got)


def reduce_streams(pieces, index_second, beside):
    pieces, beside = lax.optimization_barrier((exchange(pieces, 0), beside))
    pieces = sum_and_split(index_second, pieces)
    pieces = exchange(pieces, 1)
    totals = [total_of(pieces[k], pieces[k + 1 : k + 4]) for k in (0, 4)]
    pieces = exchange([totals[0]] * 4 + [totals[1]] * 4, 2)
    totals = [total_of(pieces[k], pieces[k + 1 : k + 4]) for k in (0, 4)]
    pieces = exchange([totals[0]] * 4 + [totals[1]] * 4, 1)
    kept = []
    for stream in range(2):
        low, high = index_second[stream] & 1, index_second[stream] >> 1
        four = pieces[4 * stream : 4 * stream + 4]
        four = [jnp.where(low == 0, four[j], four[j ^ 1]) for j in range(4)]
        four = [jnp.where(high == 0, four[j], four[j ^ 2]) for j in range(4)]
        kept.append(jnp.concatenate(four, axis=0))
    pieces, away = lax.optimization_barrier(
        (exchange([kept[0]] * 4 + [kept[1]] * 4, 0), [swap(quarter, "c", 1) for quarter in kept])
    )
    out = []
    for stream in range(2):
        joined = jnp.concatenate(pieces[4 * stream + 1 : 4 * stream + 4], axis=0)
        out += [kept[stream], joined, away[stream], swap(joined, "c", 1)]
    return out, beside


def assemble_kernel(index_ref, core_ref, *refs):
    pieces, (out_img, out_txt, wide, sems) = refs[:8], refs[8:]

    def run(own_out, other_out):
        copies = []
        first = 0
        for stream in range(2):
            count = pieces[4 * stream].shape[0]
            for side, target in ((0, own_out), (1, other_out)):
                kept, joined = pieces[4 * stream + 2 * side : 4 * stream + 2 * side + 2]
                for m in range(4):
                    k = len(copies)
                    at = first + m * count
                    piece = kept[...] if m == 0 else joined[(m - 1) * count : m * count]
                    wide[side, at : at + count] = piece.astype(f32)
                    begin = pl.multiple_of(first + jnp.bitwise_xor(index_ref[stream], m) * count, 32)
                    copy = pltpu.make_async_copy(
                        wide.at[side, pl.ds(at, count)], target.at[pl.ds(begin, count)], sems.at[k]
                    )
                    copy.start()
                    copies.append(copy)
            first += 4 * count
        for copy in copies:
            copy.wait()

    @pl.when(core_ref[0] == 0)
    def _():
        run(out_img, out_txt)

    @pl.when(core_ref[0] != 0)
    def _():
        run(out_txt, out_img)


def assemble(index, core, pieces, rows):
    width = pieces[0].shape[1]
    shape = jax.ShapeDtypeStruct((rows, width), f32)
    return pl.pallas_call(
        assemble_kernel,
        grid=(1,),
        out_shape=(shape, shape),
        in_specs=[pl.BlockSpec(memory_space=pltpu.SMEM)] * 2 + [whole(piece.shape) for piece in pieces],
        out_specs=(pl.BlockSpec(memory_space=pl.ANY),) * 2,
        scratch_shapes=[pltpu.VMEM((2, rows, width), f32), pltpu.SemaphoreType.DMA((16,))],
        compiler_params=pltpu.CompilerParams(vmem_limit_bytes=40 * 2**20),
    )(index, core, *pieces)


def pair_kernel(number_ref, count_ref, own_ref, mates_ref, begin_ref, out_ref):
    scale, shift = number_ref[0], number_ref[1]
    mates = mates_ref[...]
    logits = lax.dot_general(own_ref[...], mates, TRANSPOSED, preferred_element_type=f32)
    logits = scale * logits + shift
    column = lax.broadcasted_iota(jnp.int32, logits.shape, 1) & 15
    row = lax.broadcasted_iota(jnp.int32, logits.shape, 0)
    keep = ((column & 7) + 1 < count_ref[0]) & ((column < 8) == (row < logits.shape[0] // 2))
    coef = jnp.where(keep, scale / (1.0 + jnp.exp(-logits)), 0.0).astype(bf16)
    part = jnp.dot(coef, mates, preferred_element_type=f32)

    @pl.when(pl.program_id(0) == 0)
    def _():
        out_ref[...] = begin_ref[...] + part

    @pl.when(pl.program_id(0) != 0)
    def _():
        out_ref[...] += part


def pair_stage(numbers, count, own, mates, begin):
    rows, width = own.shape
    per = 512

    return pl.pallas_call(
        pair_kernel,
        grid=(mates.shape[0] // per,),
        out_shape=jax.ShapeDtypeStruct((rows, width), f32),
        in_specs=[
            pl.BlockSpec(memory_space=pltpu.SMEM),
            pl.BlockSpec(memory_space=pltpu.SMEM),
            whole((rows, width)),
            pl.BlockSpec((per, width), lambda i: (i, 0)),
            whole((rows, width)),
        ],
        out_specs=whole((rows, width)),
        compiler_params=pltpu.CompilerParams(vmem_limit_bytes=40 * 2**20),
    )(numbers, count, own, mates, begin)


def finish_kernel(number_ref, count_ref, own_hbm, last_hbm, begin_hbm, inverse_ref, out_ref, own, last, begin, sems):
    copies = [
        pltpu.make_async_copy(source, target, sems.at[k])
        for k, (source, target) in enumerate(((own_hbm, own), (last_hbm, last), (begin_hbm, begin)))
    ]
    for copy in copies:
        copy.start()
    for copy in copies:
        copy.wait()
    scale, shift = number_ref[0], number_ref[1]
    rows = out_ref.shape[0] // 2
    for tower in range(2):
        part = slice(tower * rows, (tower + 1) * rows)
        mates = last[:, tower, :]
        logits = lax.dot_general(own[part], mates, TRANSPOSED, preferred_element_type=f32)
        logits = scale * logits + shift
        coef = jnp.where(count_ref[0] > 9, scale / (1.0 + jnp.exp(-logits)), 0.0).astype(bf16)
        upstream = begin[part] + jnp.dot(coef, mates, preferred_element_type=f32)
        unit = own[part].astype(f32)
        radial = jnp.sum(unit * upstream, axis=-1, keepdims=True)
        out_ref[part] = (inverse_ref[part] * (upstream - unit * radial)).astype(bf16)


def finish_stage(numbers, count, own, last, begin, inverse):
    smem = pl.BlockSpec(memory_space=pltpu.SMEM)
    hbm = pl.BlockSpec(memory_space=pltpu.HBM)
    return pl.pallas_call(
        finish_kernel,
        grid=(1,),
        out_shape=jax.ShapeDtypeStruct(own.shape, bf16),
        in_specs=[smem, smem, hbm, hbm, hbm, whole(inverse.shape)],
        out_specs=whole(own.shape),
        scratch_shapes=[pltpu.VMEM(a.shape, a.dtype) for a in (own, last, begin)] + [pltpu.SemaphoreType.DMA((3,))],
        compiler_params=pltpu.CompilerParams(vmem_limit_bytes=40 * 2**20),
    )(numbers, count, own, last, begin, inverse)


def select_kernel(pick_ref, spread_ref, text_weight, image_weight, send_ref, unit_ref):
    rows = spread_ref.shape[0]

    @pl.when(pl.program_id(0) == 0)
    def _():
        for tower, weight in ((0, text_weight), (1, image_weight)):
            product = jnp.dot(spread_ref[:, tower, :], weight[...], preferred_element_type=f32)
            inverse = lax.rsqrt(jnp.sum(product * product, axis=-1, keepdims=True) + eps_norm)
            unit_ref[tower * rows : (tower + 1) * rows] = (product * inverse).astype(bf16)

    send_ref[...] = jnp.dot(pick_ref[...], unit_ref[...], preferred_element_type=f32).astype(bf16)


def select_stage(pick, spread, text_weight, image_weight):
    rows, _, width = spread.shape
    per = 512
    return pl.pallas_call(
        select_kernel,
        grid=(pick.shape[0] // per,),
        out_shape=(
            jax.ShapeDtypeStruct((pick.shape[0], width), bf16),
            jax.ShapeDtypeStruct((2 * rows, width), bf16),
        ),
        in_specs=[
            pl.BlockSpec((per, 2 * rows), lambda i: (i, 0)),
            whole(spread.shape),
            whole(text_weight.shape),
            whole(image_weight.shape),
        ],
        out_specs=(pl.BlockSpec((per, width), lambda i: (i, 0)), whole((2 * rows, width))),
        compiler_params=pltpu.CompilerParams(vmem_limit_bytes=40 * 2**20),
    )(pick, spread, text_weight, image_weight)


def local(x_img, x_txt, w_img, w_txt, sharpness, offset, lists, counts, holder):
    devices = lax.axis_size(ALL)
    me = lax.axis_index(ALL)
    core = lax.axis_index("c")
    rows, width = x_img.shape
    slots = lists.shape[1]
    scale = sharpness[0]
    shift = offset[0]
    spread = lax.all_to_all(jnp.stack([x_txt, x_img], axis=1), ALL, 0, 0, tiled=True)
    z_txt, r_txt = project(x_txt, w_txt)
    z_img, r_img = project(x_img, w_img)

    numbers = jnp.arange(devices, dtype=jnp.int32)
    hot = holder[None, :] == numbers[:, None]
    source = jnp.sum(jnp.where(lists[:, :, None] == numbers, holder, 0), axis=2)
    table = jnp.dot(hot.astype(bf16), source.astype(bf16), preferred_element_type=f32).astype(jnp.int32)
    count = jnp.sum(jnp.where(hot[me], counts, 0))

    columns = jnp.arange(2 * devices, dtype=jnp.int32)
    near = jnp.concatenate([table[:, 1:9], table[:, 1:9] + devices], axis=1)
    last = jnp.concatenate([table[:, 9:], table[:, 9:] + devices], axis=1)
    pick = (near[:, :, None] == columns).astype(bf16).reshape(16 * devices, 2 * devices)
    pick_last = (last[:, :, None] == columns).astype(bf16).reshape(2 * devices, 2 * devices)
    send, units = select_stage(pick, spread, w_txt, w_img)
    send = send.reshape(devices, 16, width)
    send_last = jnp.dot(pick_last, units, preferred_element_type=f32).astype(bf16).reshape(devices, 2, width)
    mates = lax.all_to_all(send, ALL, 0, 0, tiled=True).reshape(16 * devices, width)
    mates, send_last = lax.optimization_barrier((mates, send_last))
    last = lax.all_to_all(send_last, ALL, 0, 0, tiled=True)

    x_mine = jnp.where(core == 0, x_img, x_txt)
    x_other = swap(jnp.where(core == 0, x_txt, x_img), "c", 1)

    own = jnp.concatenate([z_img, z_txt], axis=0)
    logits = scale * lax.dot_general(z_img, z_txt, TRANSPOSED, preferred_element_type=f32) + shift
    sign = jnp.where(jnp.eye(rows, dtype=bool), 1.0, -1.0)
    coef = (-scale * sign * jax.nn.sigmoid(-sign * logits)).astype(bf16)
    dz = jnp.concatenate(
        [
            jnp.dot(coef, z_txt, preferred_element_type=f32),
            lax.dot_general(coef, z_img, ROWS_FIRST, preferred_element_type=f32),
        ],
        axis=0,
    )
    inverse = jnp.concatenate([r_img, r_txt], axis=0)
    scalars = jnp.stack([scale, shift])
    dz = pair_stage(scalars, count[None], own, mates, dz)
    du = finish_stage(scalars, count[None], own, last, dz, inverse)
    du_img = du[:rows]
    du_txt = du[rows:]
    du_mine = jnp.where(core == 0, du_img, du_txt)
    du_other = swap(jnp.where(core == 0, du_txt, du_img), "c", 1)
    g_img = lax.dot_general(du_img, w_img, TRANSPOSED, preferred_element_type=f32).astype(bf16)
    g_txt = lax.dot_general(du_txt, w_txt, TRANSPOSED, preferred_element_type=f32).astype(bf16)

    factor = (64.0 / (devices * rows)) ** 0.5
    index_first, index_second = (
        jnp.stack([lax.axis_index(axes[k]) for _, axes in STREAMS]).astype(jnp.int32) for k in (0, 1)
    )
    pieces = head_gradient(factor, index_first, (x_mine, x_other), (du_mine, du_other))
    pieces, (g_img, g_txt) = reduce_streams(pieces, index_second, (g_img, g_txt))
    head_img, head_txt = assemble(index_first, core[None].astype(jnp.int32), pieces, width)
    return (g_img, g_txt, head_img, head_txt)


def solution(mesh):
    grid = Mesh(mesh.devices.reshape(4, 4, 4, 2), ALL)
    placed = (P(ALL, None), P(ALL, None), P(), P(), P(), P(), P(), P(), P())
    return jax.shard_map(
        local,
        mesh=grid,
        in_specs=placed,
        out_specs=(P(ALL, None), P(ALL, None), P(), P()),
        check_vma=False,
    )
```

```python
import jax
import jax.numpy as jnp
from jax import lax
from jax.experimental import pallas as pl
from jax.experimental.pallas import tpu as pltpu
from jax.sharding import Mesh, PartitionSpec as P

eps_norm = 1e-06
ALL = ("x", "z", "y", "c")
TRANSPOSED = (((1,), (1,)), ((), ()))
ROWS_FIRST = (((0,), (0,)), ((), ()))
STREAMS = ((640, ("y", "x", "z")), (512, ("x", "z", "y")))
bf16 = jnp.bfloat16
f32 = jnp.float32


def project(features, weight):
    product = jnp.dot(features, weight, preferred_element_type=f32)
    inverse = lax.rsqrt(jnp.sum(product * product, axis=-1, keepdims=True) + eps_norm)
    return ((product * inverse).astype(bf16), inverse)


def swap(array, axis, mask):
    return lax.ppermute(array, axis, [(i, i ^ mask) for i in range(lax.axis_size(axis))])


def take(array, index):
    return lax.dynamic_index_in_dim(array, index, 0, keepdims=False)


def total_of(own, got):
    total = (own.astype(f32) + got[0].astype(f32)) + (got[1].astype(f32) + got[2].astype(f32))
    return total.astype(bf16)


def whole(shape):
    return pl.BlockSpec(shape, lambda i: (0,) * len(shape))


def kernel_call(body, outs, scalars, arrays, scratch=()):
    return pl.pallas_call(
        body,
        grid=(1,),
        out_shape=outs,
        in_specs=[pl.BlockSpec(memory_space=pltpu.SMEM)] * len(scalars) + [whole(a.shape) for a in arrays],
        out_specs=tuple(whole(o.shape) for o in outs),
        scratch_shapes=scratch,
        compiler_params=pltpu.CompilerParams(vmem_limit_bytes=40 * 2**20),
    )(*scalars, *arrays)


def quarters_of(sizes, width, parts):
    return tuple(jax.ShapeDtypeStruct((size // parts, width), bf16) for size in sizes for _ in range(4))


def head_gradient(factor, index, features, through):
    rows, columns = features[0].shape
    width = through[0].shape[1]
    sizes = [size for size, _ in STREAMS]
    per = columns // 3

    def body(index_ref, xa, xb, da, db, *rest):
        outs, total = rest[:8], rest[8]
        for k in range(3):
            part = slice(k * per, (k + 1) * per)
            grad = lax.dot_general(xa[:, part], da[...], ROWS_FIRST, preferred_element_type=f32)
            grad += lax.dot_general(xb[:, part], db[...], ROWS_FIRST, preferred_element_type=f32)
            total[part] = grad * factor
        first = 0
        for stream, size in enumerate(sizes):
            count = size // 4
            for m in range(4):
                begin = pl.multiple_of(first + jnp.bitwise_xor(index_ref[stream], m) * count, 32)
                outs[4 * stream + m][...] = total[pl.ds(begin, count), :].astype(bf16)
            first += size

    outs = quarters_of(sizes, width, 4)
    return kernel_call(body, outs, (index,), (*features, *through), (pltpu.VMEM((columns, width), f32),))


def sum_and_split(index, pieces):
    width = pieces[0].shape[1]
    sizes = [pieces[0].shape[0], pieces[4].shape[0]]

    def body(index_ref, *refs):
        ins, outs, total = refs[:8], refs[8:16], refs[16:]
        for stream in range(2):
            a, b, c, d = (ins[4 * stream + m][...].astype(f32) for m in range(4))
            total[stream][...] = (a + b) + (c + d)
            count = sizes[stream] // 4
            for m in range(4):
                begin = pl.multiple_of(jnp.bitwise_xor(index_ref[stream], m) * count, 8)
                outs[4 * stream + m][...] = total[stream][pl.ds(begin, count), :].astype(bf16)

    outs = quarters_of(sizes, width, 4)
    scratch = tuple(pltpu.VMEM((size, width), f32) for size in sizes)
    return kernel_call(body, outs, (index,), pieces, scratch)


def exchange(pieces, phase):
    got = list(pieces)
    for m in (2, 1, 3):
        for stream, (_, axes) in enumerate(STREAMS):
            got[4 * stream + m] = swap(pieces[4 * stream + m], axes[phase], m)
    return lax.optimization_barrier(got)


def reduce_streams(pieces, index_second, beside):
    pieces, beside = lax.optimization_barrier((exchange(pieces, 0), beside))
    pieces = sum_and_split(index_second, pieces)
    pieces = exchange(pieces, 1)
    totals = [total_of(pieces[k], pieces[k + 1 : k + 4]) for k in (0, 4)]
    pieces = exchange([totals[0]] * 4 + [totals[1]] * 4, 2)
    totals = [total_of(pieces[k], pieces[k + 1 : k + 4]) for k in (0, 4)]
    pieces = exchange([totals[0]] * 4 + [totals[1]] * 4, 1)
    kept = []
    for stream in range(2):
        low, high = index_second[stream] & 1, index_second[stream] >> 1
        four = pieces[4 * stream : 4 * stream + 4]
        four = [jnp.where(low == 0, four[j], four[j ^ 1]) for j in range(4)]
        four = [jnp.where(high == 0, four[j], four[j ^ 2]) for j in range(4)]
        kept.append(jnp.concatenate(four, axis=0))
    pieces, away = lax.optimization_barrier(
        (exchange([kept[0]] * 4 + [kept[1]] * 4, 0), [swap(quarter, "c", 1) for quarter in kept])
    )
    out = []
    for stream in range(2):
        joined = jnp.concatenate(pieces[4 * stream + 1 : 4 * stream + 4], axis=0)
        out += [kept[stream], joined, away[stream], swap(joined, "c", 1)]
    return out, beside


def write_half(index_ref, pieces, target, wide, sems):
    copies = []
    first = 0
    for stream in range(2):
        kept, joined = pieces[2 * stream : 2 * stream + 2]
        count = kept.shape[0]
        for m in range(4):
            at = first + m * count
            piece = kept[...] if m == 0 else joined[(m - 1) * count : m * count]
            wide[at : at + count] = piece.astype(f32)
            begin = pl.multiple_of(first + jnp.bitwise_xor(index_ref[stream], m) * count, 32)
            copy = pltpu.make_async_copy(
                wide.at[pl.ds(at, count)], target.at[pl.ds(begin, count)], sems.at[4 * stream + m]
            )
            copy.start()
            copies.append(copy)
        first += 4 * count
    for copy in copies:
        copy.wait()


def assemble(index, tower, pieces, rows, written=()):
    width = pieces[0].shape[1]
    shape = jax.ShapeDtypeStruct((rows, width), f32)
    hbm = pl.BlockSpec(memory_space=pltpu.HBM)

    def body(index_ref, tower_ref, *refs):
        out_img, out_txt, wide, sems = refs[4 + len(written) :]

        @pl.when(tower_ref[0] == 0)
        def _():
            write_half(index_ref, refs[:4], out_img, wide, sems)

        @pl.when(tower_ref[0] != 0)
        def _():
            write_half(index_ref, refs[:4], out_txt, wide, sems)

    return pl.pallas_call(
        body,
        grid=(1,),
        out_shape=(shape, shape),
        in_specs=[pl.BlockSpec(memory_space=pltpu.SMEM)] * 2
        + [whole(piece.shape) for piece in pieces]
        + [hbm] * len(written),
        out_specs=(hbm, hbm),
        input_output_aliases={6 + k: k for k in range(len(written))},
        scratch_shapes=[pltpu.VMEM((rows, width), f32), pltpu.SemaphoreType.DMA((8,))],
        compiler_params=pltpu.CompilerParams(vmem_limit_bytes=40 * 2**20),
    )(index, tower, *pieces, *written)


def pair_kernel(number_ref, count_ref, own_ref, mates_ref, begin_ref, out_ref):
    scale, shift = number_ref[0], number_ref[1]
    mates = mates_ref[...]
    logits = lax.dot_general(own_ref[...], mates, TRANSPOSED, preferred_element_type=f32)
    logits = scale * logits + shift
    column = lax.broadcasted_iota(jnp.int32, logits.shape, 1) & 15
    row = lax.broadcasted_iota(jnp.int32, logits.shape, 0)
    keep = ((column & 7) + 1 < count_ref[0]) & ((column < 8) == (row < logits.shape[0] // 2))
    coef = jnp.where(keep, scale / (1.0 + jnp.exp(-logits)), 0.0).astype(bf16)
    part = jnp.dot(coef, mates, preferred_element_type=f32)

    @pl.when(pl.program_id(0) == 0)
    def _():
        out_ref[...] = begin_ref[...] + part

    @pl.when(pl.program_id(0) != 0)
    def _():
        out_ref[...] += part


def pair_stage(numbers, count, own, mates, begin):
    rows, width = own.shape
    per = 512

    return pl.pallas_call(
        pair_kernel,
        grid=(mates.shape[0] // per,),
        out_shape=jax.ShapeDtypeStruct((rows, width), f32),
        in_specs=[
            pl.BlockSpec(memory_space=pltpu.SMEM),
            pl.BlockSpec(memory_space=pltpu.SMEM),
            whole((rows, width)),
            pl.BlockSpec((per, width), lambda i: (i, 0)),
            whole((rows, width)),
        ],
        out_specs=whole((rows, width)),
        compiler_params=pltpu.CompilerParams(vmem_limit_bytes=60 * 2**20),
    )(numbers, count, own, mates, begin)


def finish_kernel(number_ref, count_ref, own_hbm, last_hbm, begin_hbm, inverse_ref, out_ref, own, last, begin, sems):
    copies = [
        pltpu.make_async_copy(source, target, sems.at[k])
        for k, (source, target) in enumerate(((own_hbm, own), (last_hbm, last), (begin_hbm, begin)))
    ]
    for copy in copies:
        copy.start()
    for copy in copies:
        copy.wait()
    scale, shift = number_ref[0], number_ref[1]
    rows = out_ref.shape[0] // 2
    for tower in range(2):
        part = slice(tower * rows, (tower + 1) * rows)
        mates = last[:, tower, :]
        logits = lax.dot_general(own[part], mates, TRANSPOSED, preferred_element_type=f32)
        logits = scale * logits + shift
        coef = jnp.where(count_ref[0] > 9, scale / (1.0 + jnp.exp(-logits)), 0.0).astype(bf16)
        upstream = begin[part] + jnp.dot(coef, mates, preferred_element_type=f32)
        unit = own[part].astype(f32)
        radial = jnp.sum(unit * upstream, axis=-1, keepdims=True)
        out_ref[part] = (inverse_ref[part] * (upstream - unit * radial)).astype(bf16)


def finish_stage(numbers, count, own, last, begin, inverse):
    smem = pl.BlockSpec(memory_space=pltpu.SMEM)
    hbm = pl.BlockSpec(memory_space=pltpu.HBM)
    return pl.pallas_call(
        finish_kernel,
        grid=(1,),
        out_shape=jax.ShapeDtypeStruct(own.shape, bf16),
        in_specs=[smem, smem, hbm, hbm, hbm, whole(inverse.shape)],
        out_specs=whole(own.shape),
        scratch_shapes=[pltpu.VMEM(a.shape, a.dtype) for a in (own, last, begin)] + [pltpu.SemaphoreType.DMA((3,))],
        compiler_params=pltpu.CompilerParams(vmem_limit_bytes=60 * 2**20),
    )(numbers, count, own, last, begin, inverse)


def stack_kernel(text_ref, image_ref, out_ref):
    out_ref[:, 0, :] = text_ref[...]
    out_ref[:, 1, :] = image_ref[...]


def stack_rows(text, image):
    rows, width = text.shape
    return pl.pallas_call(
        stack_kernel,
        grid=(1,),
        out_shape=jax.ShapeDtypeStruct((rows, 2, width), bf16),
        in_specs=[whole(text.shape)] * 2,
        out_specs=whole((rows, 2, width)),
        compiler_params=pltpu.CompilerParams(vmem_limit_bytes=60 * 2**20),
    )(text, image)


def select_kernel(pick_ref, spread_ref, text_weight, image_weight, send_ref, unit_ref):
    rows = spread_ref.shape[0]

    @pl.when(pl.program_id(0) == 0)
    def _():
        for tower, weight in ((0, text_weight), (1, image_weight)):
            product = jnp.dot(spread_ref[:, tower, :], weight[...], preferred_element_type=f32)
            inverse = lax.rsqrt(jnp.sum(product * product, axis=-1, keepdims=True) + eps_norm)
            unit_ref[tower * rows : (tower + 1) * rows] = (product * inverse).astype(bf16)

    send_ref[...] = jnp.dot(pick_ref[...], unit_ref[...], preferred_element_type=f32).astype(bf16)


def select_stage(pick, spread, text_weight, image_weight):
    rows, _, width = spread.shape
    per = 512
    return pl.pallas_call(
        select_kernel,
        grid=(pick.shape[0] // per,),
        out_shape=(
            jax.ShapeDtypeStruct((pick.shape[0], width), bf16),
            jax.ShapeDtypeStruct((2 * rows, width), bf16),
        ),
        in_specs=[
            pl.BlockSpec((per, 2 * rows), lambda i: (i, 0)),
            whole(spread.shape),
            whole(text_weight.shape),
            whole(image_weight.shape),
        ],
        out_specs=(pl.BlockSpec((per, width), lambda i: (i, 0)), whole((2 * rows, width))),
        compiler_params=pltpu.CompilerParams(vmem_limit_bytes=60 * 2**20),
    )(pick, spread, text_weight, image_weight)


def local(x_img, x_txt, w_img, w_txt, sharpness, offset, lists, counts, holder):
    devices = lax.axis_size(ALL)
    me = lax.axis_index(ALL)
    core = lax.axis_index("c")
    rows, width = x_img.shape
    slots = lists.shape[1]
    scale = sharpness[0]
    shift = offset[0]
    spread = lax.all_to_all(stack_rows(x_txt, x_img), ALL, 0, 0, tiled=True)
    z_txt, r_txt = project(x_txt, w_txt)
    z_img, r_img = project(x_img, w_img)

    numbers = jnp.arange(devices, dtype=jnp.int32)
    hot = holder[None, :] == numbers[:, None]
    source = jnp.sum(jnp.where(lists[:, :, None] == numbers, holder, 0), axis=2)
    table = jnp.dot(hot.astype(bf16), source.astype(bf16), preferred_element_type=f32).astype(jnp.int32)
    count = jnp.sum(jnp.where(hot[me], counts, 0))

    columns = jnp.arange(2 * devices, dtype=jnp.int32)
    near = jnp.concatenate([table[:, 1:9], table[:, 1:9] + devices], axis=1)
    last = jnp.concatenate([table[:, 9:], table[:, 9:] + devices], axis=1)
    pick = (near[:, :, None] == columns).astype(bf16).reshape(16 * devices, 2 * devices)
    pick_last = (last[:, :, None] == columns).astype(bf16).reshape(2 * devices, 2 * devices)
    send, units = select_stage(pick, spread, w_txt, w_img)
    send = send.reshape(devices, 16, width)
    send_last = jnp.dot(pick_last, units, preferred_element_type=f32).astype(bf16).reshape(devices, 2, width)
    mates = lax.all_to_all(send, ALL, 0, 0, tiled=True).reshape(16 * devices, width)
    mates, send_last = lax.optimization_barrier((mates, send_last))
    last = lax.all_to_all(send_last, ALL, 0, 0, tiled=True)

    x_mine = jnp.where(core == 0, x_img, x_txt)
    x_other = swap(jnp.where(core == 0, x_txt, x_img), "c", 1)

    own = jnp.concatenate([z_img, z_txt], axis=0)
    logits = scale * lax.dot_general(z_img, z_txt, TRANSPOSED, preferred_element_type=f32) + shift
    sign = jnp.where(jnp.eye(rows, dtype=bool), 1.0, -1.0)
    coef = (-scale * sign * jax.nn.sigmoid(-sign * logits)).astype(bf16)
    dz = jnp.concatenate(
        [
            jnp.dot(coef, z_txt, preferred_element_type=f32),
            lax.dot_general(coef, z_img, ROWS_FIRST, preferred_element_type=f32),
        ],
        axis=0,
    )
    inverse = jnp.concatenate([r_img, r_txt], axis=0)
    scalars = jnp.stack([scale, shift])
    dz = pair_stage(scalars, count[None], own, mates, dz)
    du = finish_stage(scalars, count[None], own, last, dz, inverse)
    du_img = du[:rows]
    du_txt = du[rows:]
    du_mine = jnp.where(core == 0, du_img, du_txt)
    du_other = swap(jnp.where(core == 0, du_txt, du_img), "c", 1)
    g_img = lax.dot_general(du_img, w_img, TRANSPOSED, preferred_element_type=f32).astype(bf16)
    g_txt = lax.dot_general(du_txt, w_txt, TRANSPOSED, preferred_element_type=f32).astype(bf16)

    factor = (64.0 / (devices * rows)) ** 0.5
    index_first, index_second = (
        jnp.stack([lax.axis_index(axes[k]) for _, axes in STREAMS]).astype(jnp.int32) for k in (0, 1)
    )
    pieces = head_gradient(factor, index_first, (x_mine, x_other), (du_mine, du_other))
    pieces, (g_img, g_txt) = reduce_streams(pieces, index_second, (g_img, g_txt))
    core = core[None].astype(jnp.int32)
    written = assemble(index_first, core, pieces[:2] + pieces[4:6], width)
    head_img, head_txt = assemble(index_first, 1 - core, pieces[2:4] + pieces[6:8], width, written)
    return (g_img, g_txt, head_img, head_txt)


def solution(mesh):
    grid = Mesh(mesh.devices.reshape(4, 4, 4, 2), ALL)
    placed = (P(ALL, None), P(ALL, None), P(), P(), P(), P(), P(), P(), P())
    return jax.shard_map(
        local,
        mesh=grid,
        in_specs=placed,
        out_specs=(P(ALL, None), P(ALL, None), P(), P()),
        check_vma=False,
    )
```

```python
import jax
import jax.numpy as jnp
from jax import lax
from jax.experimental import pallas as pl
from jax.experimental.pallas import tpu as pltpu
from jax.sharding import Mesh, PartitionSpec as P

eps_norm = 1e-06
ALL = ("x", "z", "y", "c")
TRANSPOSED = (((1,), (1,)), ((), ()))
ROWS_FIRST = (((0,), (0,)), ((), ()))
STREAMS = ((640, "y"), (512, "x"))
bf16 = jnp.bfloat16
f32 = jnp.float32


def project(features, weight):
    product = jnp.dot(features, weight, preferred_element_type=f32)
    inverse = lax.rsqrt(jnp.sum(product * product, axis=-1, keepdims=True) + eps_norm)
    return ((product * inverse).astype(bf16), inverse)


def swap(array, axis, mask):
    if isinstance(axis, str):
        return lax.ppermute(array, axis, [(i, i ^ mask) for i in range(lax.axis_size(axis))])
    size = lax.axis_size(axis[1])
    pairs = [(i * size + j, (i ^ mask) * size + (j ^ mask)) for i in range(size) for j in range(size)]
    return lax.ppermute(array, axis, pairs)


def take(array, index):
    return lax.dynamic_index_in_dim(array, index, 0, keepdims=False)


def total_of(own, got):
    total = (own.astype(f32) + got[0].astype(f32)) + (got[1].astype(f32) + got[2].astype(f32))
    return total.astype(bf16)


def whole(shape):
    return pl.BlockSpec(shape, lambda i: (0,) * len(shape))


def kernel_call(body, outs, scalars, arrays, scratch=()):
    return pl.pallas_call(
        body,
        grid=(1,),
        out_shape=outs,
        in_specs=[pl.BlockSpec(memory_space=pltpu.SMEM)] * len(scalars) + [whole(a.shape) for a in arrays],
        out_specs=tuple(whole(o.shape) for o in outs),
        scratch_shapes=scratch,
        compiler_params=pltpu.CompilerParams(vmem_limit_bytes=40 * 2**20),
    )(*scalars, *arrays)


def quarters_of(sizes, width, parts):
    return tuple(jax.ShapeDtypeStruct((size // parts, width), bf16) for size in sizes for _ in range(4))


def head_gradient(factor, index, features, through):
    rows, columns = features[0].shape
    width = through[0].shape[1]
    sizes = [size for size, _ in STREAMS]
    per = columns // 3

    def body(index_ref, xa, xb, da, db, *rest):
        outs, total = rest[:8], rest[8]
        for k in range(3):
            part = slice(k * per, (k + 1) * per)
            grad = lax.dot_general(xa[:, part], da[...], ROWS_FIRST, preferred_element_type=f32)
            grad += lax.dot_general(xb[:, part], db[...], ROWS_FIRST, preferred_element_type=f32)
            total[part] = grad * factor
        first = 0
        for stream, size in enumerate(sizes):
            count = size // 4
            for m in range(4):
                begin = pl.multiple_of(first + jnp.bitwise_xor(index_ref[0], m) * count, 32)
                outs[4 * stream + m][...] = total[pl.ds(begin, count), :].astype(bf16)
            first += size

    outs = quarters_of(sizes, width, 4)
    return kernel_call(body, outs, (index,), (*features, *through), (pltpu.VMEM((columns, width), f32),))


def sum_and_split(index, pieces):
    width = pieces[0].shape[1]
    sizes = [pieces[0].shape[0], pieces[4].shape[0]]
    count = sum(sizes) // 4

    def body(index_ref, *refs):
        ins, outs, total = refs[:8], refs[8:12], refs[12]
        first = 0
        for stream, size in enumerate(sizes):
            a, b, c, d = (ins[4 * stream + m][...].astype(f32) for m in range(4))
            total[first : first + size] = (a + b) + (c + d)
            first += size
        for m in range(4):
            begin = pl.multiple_of(jnp.bitwise_xor(index_ref[0], m) * count, 8)
            outs[m][...] = total[pl.ds(begin, count), :].astype(bf16)

    outs = tuple(jax.ShapeDtypeStruct((count, width), bf16) for _ in range(4))
    return kernel_call(body, outs, (index,), pieces, (pltpu.VMEM((sum(sizes), width), f32),))


def join(index, pieces):
    count, width = pieces[0].shape
    sizes = [size // 4 for size, _ in STREAMS]

    def body(index_ref, *refs):
        ins, outs, rows = refs[:4], refs[4:6], refs[6]
        for m in range(4):
            begin = pl.multiple_of(jnp.bitwise_xor(index_ref[0], m) * count, 8)
            rows[pl.ds(begin, count), :] = ins[m][...].astype(f32)
        outs[0][...] = rows[: sizes[0]].astype(bf16)
        outs[1][...] = rows[sizes[0] :].astype(bf16)

    outs = tuple(jax.ShapeDtypeStruct((size, width), bf16) for size in sizes)
    return kernel_call(body, outs, (index,), pieces, (pltpu.VMEM((4 * count, width), f32),))


def exchange(pieces, axis):
    return [pieces[0]] + [swap(pieces[m], axis, m) for m in (1, 2, 3)]


def exchange_streams(pieces):
    got = list(pieces)
    for m in (2, 1, 3):
        for stream, (_, axis) in enumerate(STREAMS):
            got[4 * stream + m] = swap(pieces[4 * stream + m], axis, m)
    return got


def reduce_streams(pieces, beside):
    along_z = lax.axis_index("z").astype(jnp.int32)[None]
    pieces, beside = lax.optimization_barrier((exchange_streams(pieces), beside))
    pieces = exchange(sum_and_split(along_z, pieces), "z")
    total = total_of(pieces[0], pieces[1:])
    pieces = exchange([total] * 4, ("x", "y"))
    total = total_of(pieces[0], pieces[1:])
    kept = join(along_z, exchange([total] * 4, "z"))
    pieces, away = lax.optimization_barrier(
        (exchange_streams([kept[0]] * 4 + [kept[1]] * 4), [swap(quarter, "c", 1) for quarter in kept])
    )
    out = []
    for stream in range(2):
        joined = jnp.concatenate(pieces[4 * stream + 1 : 4 * stream + 4], axis=0)
        out += [kept[stream], joined, away[stream], swap(joined, "c", 1)]
    return out, beside


def write_half(index_ref, pieces, target, wide, sems):
    copies = []
    first = 0
    for stream in range(2):
        kept, joined = pieces[2 * stream : 2 * stream + 2]
        count = kept.shape[0]
        for m in range(4):
            at = first + m * count
            piece = kept[...] if m == 0 else joined[(m - 1) * count : m * count]
            wide[at : at + count] = piece.astype(f32)
            begin = pl.multiple_of(first + jnp.bitwise_xor(index_ref[0], m) * count, 32)
            copy = pltpu.make_async_copy(
                wide.at[pl.ds(at, count)], target.at[pl.ds(begin, count)], sems.at[4 * stream + m]
            )
            copy.start()
            copies.append(copy)
        first += 4 * count
    for copy in copies:
        copy.wait()


def assemble(index, tower, pieces, rows, written=()):
    width = pieces[0].shape[1]
    shape = jax.ShapeDtypeStruct((rows, width), f32)
    hbm = pl.BlockSpec(memory_space=pltpu.HBM)

    def body(index_ref, tower_ref, *refs):
        out_img, out_txt, wide, sems = refs[4 + len(written) :]

        @pl.when(tower_ref[0] == 0)
        def _():
            write_half(index_ref, refs[:4], out_img, wide, sems)

        @pl.when(tower_ref[0] != 0)
        def _():
            write_half(index_ref, refs[:4], out_txt, wide, sems)

    return pl.pallas_call(
        body,
        grid=(1,),
        out_shape=(shape, shape),
        in_specs=[pl.BlockSpec(memory_space=pltpu.SMEM)] * 2
        + [whole(piece.shape) for piece in pieces]
        + [hbm] * len(written),
        out_specs=(hbm, hbm),
        input_output_aliases={6 + k: k for k in range(len(written))},
        scratch_shapes=[pltpu.VMEM((rows, width), f32), pltpu.SemaphoreType.DMA((8,))],
        compiler_params=pltpu.CompilerParams(vmem_limit_bytes=40 * 2**20),
    )(index, tower, *pieces, *written)


def pair_kernel(number_ref, count_ref, own_ref, mates_ref, begin_ref, out_ref):
    scale, shift = number_ref[0], number_ref[1]
    mates = mates_ref[...]
    logits = lax.dot_general(own_ref[...], mates, TRANSPOSED, preferred_element_type=f32)
    logits = scale * logits + shift
    column = lax.broadcasted_iota(jnp.int32, logits.shape, 1) & 15
    row = lax.broadcasted_iota(jnp.int32, logits.shape, 0)
    keep = ((column & 7) + 1 < count_ref[0]) & ((column < 8) == (row < logits.shape[0] // 2))
    coef = jnp.where(keep, scale / (1.0 + jnp.exp(-logits)), 0.0).astype(bf16)
    part = jnp.dot(coef, mates, preferred_element_type=f32)

    @pl.when(pl.program_id(0) == 0)
    def _():
        out_ref[...] = begin_ref[...] + part

    @pl.when(pl.program_id(0) != 0)
    def _():
        out_ref[...] += part


def pair_stage(numbers, count, own, mates, begin):
    rows, width = own.shape
    per = 512

    return pl.pallas_call(
        pair_kernel,
        grid=(mates.shape[0] // per,),
        out_shape=jax.ShapeDtypeStruct((rows, width), f32),
        in_specs=[
            pl.BlockSpec(memory_space=pltpu.SMEM),
            pl.BlockSpec(memory_space=pltpu.SMEM),
            whole((rows, width)),
            pl.BlockSpec((per, width), lambda i: (i, 0)),
            whole((rows, width)),
        ],
        out_specs=whole((rows, width)),
        compiler_params=pltpu.CompilerParams(vmem_limit_bytes=60 * 2**20),
    )(numbers, count, own, mates, begin)


def finish_kernel(
    number_ref, count_ref, own_hbm, last_hbm, begin_hbm, inverse_ref, out_ref, mine_ref, other_ref, own, last, begin, sems
):
    copies = [
        pltpu.make_async_copy(source, target, sems.at[k])
        for k, (source, target) in enumerate(((own_hbm, own), (last_hbm, last), (begin_hbm, begin)))
    ]
    for copy in copies:
        copy.start()
    for copy in copies:
        copy.wait()
    scale, shift = number_ref[0], number_ref[1]
    rows = out_ref.shape[0] // 2
    for tower in range(2):
        part = slice(tower * rows, (tower + 1) * rows)
        mates = last[:, tower, :]
        logits = lax.dot_general(own[part], mates, TRANSPOSED, preferred_element_type=f32)
        logits = scale * logits + shift
        coef = jnp.where(count_ref[0] > 9, scale / (1.0 + jnp.exp(-logits)), 0.0).astype(bf16)
        upstream = begin[part] + jnp.dot(coef, mates, preferred_element_type=f32)
        unit = own[part].astype(f32)
        radial = jnp.sum(unit * upstream, axis=-1, keepdims=True)
        through = (inverse_ref[part] * (upstream - unit * radial)).astype(bf16)
        out_ref[part] = through

        @pl.when(count_ref[1] == tower)
        def _():
            mine_ref[...] = through

        @pl.when(count_ref[1] != tower)
        def _():
            other_ref[...] = through


def finish_stage(numbers, count, own, last, begin, inverse):
    smem = pl.BlockSpec(memory_space=pltpu.SMEM)
    hbm = pl.BlockSpec(memory_space=pltpu.HBM)
    return pl.pallas_call(
        finish_kernel,
        grid=(1,),
        out_shape=(
            jax.ShapeDtypeStruct(own.shape, bf16),
            jax.ShapeDtypeStruct((own.shape[0] // 2, own.shape[1]), bf16),
            jax.ShapeDtypeStruct((own.shape[0] // 2, own.shape[1]), bf16),
        ),
        in_specs=[smem, smem, hbm, hbm, hbm, whole(inverse.shape)],
        out_specs=(whole(own.shape),) + (whole((own.shape[0] // 2, own.shape[1])),) * 2,
        scratch_shapes=[pltpu.VMEM(a.shape, a.dtype) for a in (own, last, begin)] + [pltpu.SemaphoreType.DMA((3,))],
        compiler_params=pltpu.CompilerParams(vmem_limit_bytes=60 * 2**20),
    )(numbers, count, own, last, begin, inverse)


def stack_kernel(text_ref, image_ref, out_ref):
    out_ref[:, 0, :] = text_ref[...]
    out_ref[:, 1, :] = image_ref[...]


def stack_rows(text, image):
    rows, width = text.shape
    return pl.pallas_call(
        stack_kernel,
        grid=(1,),
        out_shape=jax.ShapeDtypeStruct((rows, 2, width), bf16),
        in_specs=[whole(text.shape)] * 2,
        out_specs=whole((rows, 2, width)),
        compiler_params=pltpu.CompilerParams(vmem_limit_bytes=60 * 2**20),
    )(text, image)


def select_kernel(pick_ref, spread_hbm, text_weight, image_weight, send_hbm, unit_ref, spread, send, sems):
    rows = spread.shape[0]
    arrive = pltpu.make_async_copy(spread_hbm, spread, sems.at[0])
    arrive.start()
    arrive.wait()
    for tower, weight in ((0, text_weight), (1, image_weight)):
        product = jnp.dot(spread[:, tower, :], weight[...], preferred_element_type=f32)
        inverse = lax.rsqrt(jnp.sum(product * product, axis=-1, keepdims=True) + eps_norm)
        unit_ref[tower * rows : (tower + 1) * rows] = (product * inverse).astype(bf16)
    copies = []
    per = send.shape[0] // 4
    for k in range(4):
        part = pl.ds(k * per, per)
        send[part] = jnp.dot(pick_ref[part], unit_ref[...], preferred_element_type=f32).astype(bf16)
        copy = pltpu.make_async_copy(send.at[part], send_hbm.at[part], sems.at[1 + k])
        copy.start()
        copies.append(copy)
    for copy in copies:
        copy.wait()


def select_stage(pick, spread, text_weight, image_weight):
    rows, _, width = spread.shape
    hbm = pl.BlockSpec(memory_space=pltpu.HBM)
    return pl.pallas_call(
        select_kernel,
        grid=(1,),
        out_shape=(
            jax.ShapeDtypeStruct((pick.shape[0], width), bf16),
            jax.ShapeDtypeStruct((2 * rows, width), bf16),
        ),
        in_specs=[whole(pick.shape), hbm, whole(text_weight.shape), whole(image_weight.shape)],
        out_specs=(hbm, whole((2 * rows, width))),
        scratch_shapes=[
            pltpu.VMEM(spread.shape, bf16),
            pltpu.VMEM((pick.shape[0], width), bf16),
            pltpu.SemaphoreType.DMA((5,)),
        ],
        compiler_params=pltpu.CompilerParams(vmem_limit_bytes=50 * 2**20),
    )(pick, spread, text_weight, image_weight)


def local(x_img, x_txt, w_img, w_txt, sharpness, offset, lists, counts, holder):
    devices = lax.axis_size(ALL)
    me = lax.axis_index(ALL)
    core = lax.axis_index("c")
    rows, width = x_img.shape
    slots = lists.shape[1]
    scale = sharpness[0]
    shift = offset[0]
    spread = lax.all_to_all(stack_rows(x_txt, x_img), ALL, 0, 0, tiled=True)
    z_txt, r_txt = project(x_txt, w_txt)
    z_img, r_img = project(x_img, w_img)

    numbers = jnp.arange(devices, dtype=jnp.int32)
    hot = holder[None, :] == numbers[:, None]
    source = jnp.sum(jnp.where(lists[:, :, None] == numbers, holder, 0), axis=2)
    table = jnp.dot(hot.astype(bf16), source.astype(bf16), preferred_element_type=f32).astype(jnp.int32)
    count = jnp.sum(jnp.where(hot[me], counts, 0))

    columns = jnp.arange(2 * devices, dtype=jnp.int32)
    near = jnp.concatenate([table[:, 1:9], table[:, 1:9] + devices], axis=1)
    last = jnp.concatenate([table[:, 9:], table[:, 9:] + devices], axis=1)
    pick = (near[:, :, None] == columns).astype(bf16).reshape(16 * devices, 2 * devices)
    pick_last = (last[:, :, None] == columns).astype(bf16).reshape(2 * devices, 2 * devices)
    send, units = select_stage(pick, spread, w_txt, w_img)
    send = send.reshape(devices, 16, width)
    send_last = jnp.dot(pick_last, units, preferred_element_type=f32).astype(bf16).reshape(devices, 2, width)
    mates = lax.all_to_all(send, ALL, 0, 0, tiled=True).reshape(16 * devices, width)
    mates, send_last = lax.optimization_barrier((mates, send_last))
    last = lax.all_to_all(send_last, ALL, 0, 0, tiled=True)

    x_mine = jnp.where(core == 0, x_img, x_txt)
    x_other = swap(jnp.where(core == 0, x_txt, x_img), "c", 1)

    own = jnp.concatenate([z_img, z_txt], axis=0)
    logits = scale * lax.dot_general(z_img, z_txt, TRANSPOSED, preferred_element_type=f32) + shift
    sign = jnp.where(jnp.eye(rows, dtype=bool), 1.0, -1.0)
    coef = (-scale * sign * jax.nn.sigmoid(-sign * logits)).astype(bf16)
    dz = jnp.concatenate(
        [
            jnp.dot(coef, z_txt, preferred_element_type=f32),
            lax.dot_general(coef, z_img, ROWS_FIRST, preferred_element_type=f32),
        ],
        axis=0,
    )
    inverse = jnp.concatenate([r_img, r_txt], axis=0)
    scalars = jnp.stack([scale, shift])
    dz = pair_stage(scalars, count[None], own, mates, dz)
    number = core[None].astype(jnp.int32)
    du, du_mine, du_away = finish_stage(
        scalars, jnp.concatenate([count[None], number]), own, last, dz, inverse
    )
    du_img = du[:rows]
    du_txt = du[rows:]
    du_other = swap(du_away, "c", 1)
    g_img = lax.dot_general(du_img, w_img, TRANSPOSED, preferred_element_type=f32).astype(bf16)
    g_txt = lax.dot_general(du_txt, w_txt, TRANSPOSED, preferred_element_type=f32).astype(bf16)

    factor = (64.0 / (devices * rows)) ** 0.5
    quarter = jnp.bitwise_xor(lax.axis_index("x"), lax.axis_index("y")).astype(jnp.int32)[None]
    pieces = head_gradient(factor, quarter, (x_mine, x_other), (du_mine, du_other))
    pieces, (g_img, g_txt) = reduce_streams(pieces, (g_img, g_txt))
    written = assemble(quarter, number, pieces[:2] + pieces[4:6], width)
    head_img, head_txt = assemble(quarter, 1 - number, pieces[2:4] + pieces[6:8], width, written)
    return (g_img, g_txt, head_img, head_txt)


def solution(mesh):
    grid = Mesh(mesh.devices.reshape(4, 4, 4, 2), ALL)
    placed = (P(ALL, None), P(ALL, None), P(), P(), P(), P(), P(), P(), P())
    return jax.shard_map(
        local,
        mesh=grid,
        in_specs=placed,
        out_specs=(P(ALL, None), P(ALL, None), P(), P()),
        check_vma=False,
    )
```

```python
import jax
import jax.numpy as jnp
from jax import lax
from jax.experimental import pallas as pl
from jax.experimental.pallas import tpu as pltpu
from jax.sharding import Mesh, PartitionSpec as P

eps_norm = 1e-06
ALL = ("x", "z", "y", "c")
TRANSPOSED = (((1,), (1,)), ((), ()))
ROWS_FIRST = (((0,), (0,)), ((), ()))
STREAMS = ((640, "y"), (512, "x"))
bf16 = jnp.bfloat16
f32 = jnp.float32


def project(features, weight):
    product = jnp.dot(features, weight, preferred_element_type=f32)
    inverse = lax.rsqrt(jnp.sum(product * product, axis=-1, keepdims=True) + eps_norm)
    return ((product * inverse).astype(bf16), inverse)


def swap(array, axis, mask):
    if isinstance(axis, str):
        return lax.ppermute(array, axis, [(i, i ^ mask) for i in range(lax.axis_size(axis))])
    size = lax.axis_size(axis[1])
    pairs = [(i * size + j, (i ^ mask) * size + (j ^ mask)) for i in range(size) for j in range(size)]
    return lax.ppermute(array, axis, pairs)


def take(array, index):
    return lax.dynamic_index_in_dim(array, index, 0, keepdims=False)


def total_of(own, got):
    total = (own.astype(f32) + got[0].astype(f32)) + (got[1].astype(f32) + got[2].astype(f32))
    return total.astype(bf16)


def whole(shape):
    return pl.BlockSpec(shape, lambda i: (0,) * len(shape))


def kernel_call(body, outs, scalars, arrays, scratch=()):
    return pl.pallas_call(
        body,
        grid=(1,),
        out_shape=outs,
        in_specs=[pl.BlockSpec(memory_space=pltpu.SMEM)] * len(scalars) + [whole(a.shape) for a in arrays],
        out_specs=tuple(whole(o.shape) for o in outs),
        scratch_shapes=scratch,
        compiler_params=pltpu.CompilerParams(vmem_limit_bytes=40 * 2**20),
    )(*scalars, *arrays)


def quarters_of(sizes, width, parts):
    return tuple(jax.ShapeDtypeStruct((size // parts, width), bf16) for size in sizes for _ in range(4))


def head_gradient(factor, index, features, through):
    rows, columns = features[0].shape
    width = through[0].shape[1]
    sizes = [size for size, _ in STREAMS]
    per = columns // 3

    def body(index_ref, xa, xb, da, db, *rest):
        outs, total = rest[:8], rest[8]
        for k in range(3):
            part = slice(k * per, (k + 1) * per)
            grad = lax.dot_general(xa[:, part], da[...], ROWS_FIRST, preferred_element_type=f32)
            grad += lax.dot_general(xb[:, part], db[...], ROWS_FIRST, preferred_element_type=f32)
            total[part] = grad * factor
        first = 0
        for stream, size in enumerate(sizes):
            count = size // 4
            for m in range(4):
                begin = pl.multiple_of(first + jnp.bitwise_xor(index_ref[0], m) * count, 32)
                outs[4 * stream + m][...] = total[pl.ds(begin, count), :].astype(bf16)
            first += size

    outs = quarters_of(sizes, width, 4)
    return kernel_call(body, outs, (index,), (*features, *through), (pltpu.VMEM((columns, width), f32),))


def sum_and_split(index, pieces):
    width = pieces[0].shape[1]
    sizes = [pieces[0].shape[0], pieces[4].shape[0]]
    count = sum(sizes) // 4

    def body(index_ref, *refs):
        ins, outs, total = refs[:8], refs[8:12], refs[12]
        first = 0
        for stream, size in enumerate(sizes):
            a, b, c, d = (ins[4 * stream + m][...].astype(f32) for m in range(4))
            total[first : first + size] = (a + b) + (c + d)
            first += size
        for m in range(4):
            begin = pl.multiple_of(jnp.bitwise_xor(index_ref[0], m) * count, 8)
            outs[m][...] = total[pl.ds(begin, count), :].astype(bf16)

    outs = tuple(jax.ShapeDtypeStruct((count, width), bf16) for _ in range(4))
    return kernel_call(body, outs, (index,), pieces, (pltpu.VMEM((sum(sizes), width), f32),))


def join(index, pieces):
    count, width = pieces[0].shape
    sizes = [size // 4 for size, _ in STREAMS]

    def body(index_ref, *refs):
        ins, outs, rows = refs[:4], refs[4:6], refs[6]
        for m in range(4):
            begin = pl.multiple_of(jnp.bitwise_xor(index_ref[0], m) * count, 8)
            rows[pl.ds(begin, count), :] = ins[m][...].astype(f32)
        outs[0][...] = rows[: sizes[0]].astype(bf16)
        outs[1][...] = rows[sizes[0] :].astype(bf16)

    outs = tuple(jax.ShapeDtypeStruct((size, width), bf16) for size in sizes)
    return kernel_call(body, outs, (index,), pieces, (pltpu.VMEM((4 * count, width), f32),))


def exchange(pieces, axis):
    return [pieces[0]] + [swap(pieces[m], axis, m) for m in (1, 2, 3)]


def exchange_streams(pieces):
    got = list(pieces)
    for m in (2, 1, 3):
        for stream, (_, axis) in enumerate(STREAMS):
            got[4 * stream + m] = swap(pieces[4 * stream + m], axis, m)
    return got


def reduce_streams(pieces, beside):
    along_z = lax.axis_index("z").astype(jnp.int32)[None]
    pieces = lax.optimization_barrier(exchange_streams(pieces))
    pieces = exchange(sum_and_split(along_z, pieces), "z")
    total = total_of(pieces[0], pieces[1:])
    pieces, beside = lax.optimization_barrier((exchange([total] * 4, ("x", "y")), beside))
    total = total_of(pieces[0], pieces[1:])
    kept = join(along_z, exchange([total] * 4, "z"))
    pieces = lax.optimization_barrier(exchange_streams([kept[0]] * 4 + [kept[1]] * 4))
    out = []
    for stream in range(2):
        joined = jnp.concatenate(pieces[4 * stream : 4 * stream + 4], axis=0)
        out += [joined, swap(joined, "c", 1)]
    return out, beside


def write_half(index_ref, pieces, target, wide, sems):
    copies = []
    first = 0
    for stream in range(2):
        count = pieces[stream].shape[0] // 4
        for m in range(4):
            at = first + m * count
            wide[at : at + count] = pieces[stream][m * count : (m + 1) * count].astype(f32)
            begin = pl.multiple_of(first + jnp.bitwise_xor(index_ref[0], m) * count, 32)
            copy = pltpu.make_async_copy(
                wide.at[pl.ds(at, count)], target.at[pl.ds(begin, count)], sems.at[4 * stream + m]
            )
            copy.start()
            copies.append(copy)
        first += 4 * count
    for copy in copies:
        copy.wait()


def assemble(index, tower, pieces, rows, written=()):
    width = pieces[0].shape[1]
    shape = jax.ShapeDtypeStruct((rows, width), f32)
    hbm = pl.BlockSpec(memory_space=pltpu.HBM)

    def body(index_ref, tower_ref, *refs):
        out_img, out_txt, wide, sems = refs[2 + len(written) :]

        @pl.when(tower_ref[0] == 0)
        def _():
            write_half(index_ref, refs[:2], out_img, wide, sems)

        @pl.when(tower_ref[0] != 0)
        def _():
            write_half(index_ref, refs[:2], out_txt, wide, sems)

    return pl.pallas_call(
        body,
        grid=(1,),
        out_shape=(shape, shape),
        in_specs=[pl.BlockSpec(memory_space=pltpu.SMEM)] * 2
        + [whole(piece.shape) for piece in pieces]
        + [hbm] * len(written),
        out_specs=(hbm, hbm),
        input_output_aliases={4 + k: k for k in range(len(written))},
        scratch_shapes=[pltpu.VMEM((rows, width), f32), pltpu.SemaphoreType.DMA((8,))],
        compiler_params=pltpu.CompilerParams(vmem_limit_bytes=40 * 2**20),
    )(index, tower, *pieces, *written)


def pair_kernel(number_ref, count_ref, own_ref, mates_ref, begin_ref, out_ref):
    scale, shift = number_ref[0], number_ref[1]
    mates = mates_ref[...]
    logits = lax.dot_general(own_ref[...], mates, TRANSPOSED, preferred_element_type=f32)
    logits = scale * logits + shift
    column = lax.broadcasted_iota(jnp.int32, logits.shape, 1) & 15
    row = lax.broadcasted_iota(jnp.int32, logits.shape, 0)
    keep = ((column & 7) + 1 < count_ref[0]) & ((column < 8) == (row < logits.shape[0] // 2))
    coef = jnp.where(keep, scale / (1.0 + jnp.exp(-logits)), 0.0).astype(bf16)
    part = jnp.dot(coef, mates, preferred_element_type=f32)

    @pl.when(pl.program_id(0) == 0)
    def _():
        out_ref[...] = begin_ref[...] + part

    @pl.when(pl.program_id(0) != 0)
    def _():
        out_ref[...] += part


def pair_stage(numbers, count, own, mates, begin):
    rows, width = own.shape
    per = 512

    return pl.pallas_call(
        pair_kernel,
        grid=(mates.shape[0] // per,),
        out_shape=jax.ShapeDtypeStruct((rows, width), f32),
        in_specs=[
            pl.BlockSpec(memory_space=pltpu.SMEM),
            pl.BlockSpec(memory_space=pltpu.SMEM),
            whole((rows, width)),
            pl.BlockSpec((per, width), lambda i: (i, 0)),
            whole((rows, width)),
        ],
        out_specs=whole((rows, width)),
        compiler_params=pltpu.CompilerParams(vmem_limit_bytes=60 * 2**20),
    )(numbers, count, own, mates, begin)


def finish_kernel(
    number_ref, count_ref, own_hbm, last_hbm, begin_hbm, inverse_ref, out_ref, mine_ref, other_ref, own, last, begin, sems
):
    copies = [
        pltpu.make_async_copy(source, target, sems.at[k])
        for k, (source, target) in enumerate(((own_hbm, own), (last_hbm, last), (begin_hbm, begin)))
    ]
    for copy in copies:
        copy.start()
    for copy in copies:
        copy.wait()
    scale, shift = number_ref[0], number_ref[1]
    rows = out_ref.shape[0] // 2
    for tower in range(2):
        part = slice(tower * rows, (tower + 1) * rows)
        mates = last[:, tower, :]
        logits = lax.dot_general(own[part], mates, TRANSPOSED, preferred_element_type=f32)
        logits = scale * logits + shift
        coef = jnp.where(count_ref[0] > 9, scale / (1.0 + jnp.exp(-logits)), 0.0).astype(bf16)
        upstream = begin[part] + jnp.dot(coef, mates, preferred_element_type=f32)
        unit = own[part].astype(f32)
        radial = jnp.sum(unit * upstream, axis=-1, keepdims=True)
        through = (inverse_ref[part] * (upstream - unit * radial)).astype(bf16)
        out_ref[part] = through

        @pl.when(count_ref[1] == tower)
        def _():
            mine_ref[...] = through

        @pl.when(count_ref[1] != tower)
        def _():
            other_ref[...] = through


def finish_stage(numbers, count, own, last, begin, inverse):
    smem = pl.BlockSpec(memory_space=pltpu.SMEM)
    hbm = pl.BlockSpec(memory_space=pltpu.HBM)
    return pl.pallas_call(
        finish_kernel,
        grid=(1,),
        out_shape=(
            jax.ShapeDtypeStruct(own.shape, bf16),
            jax.ShapeDtypeStruct((own.shape[0] // 2, own.shape[1]), bf16),
            jax.ShapeDtypeStruct((own.shape[0] // 2, own.shape[1]), bf16),
        ),
        in_specs=[smem, smem, hbm, hbm, hbm, whole(inverse.shape)],
        out_specs=(whole(own.shape),) + (whole((own.shape[0] // 2, own.shape[1])),) * 2,
        scratch_shapes=[pltpu.VMEM(a.shape, a.dtype) for a in (own, last, begin)] + [pltpu.SemaphoreType.DMA((3,))],
        compiler_params=pltpu.CompilerParams(vmem_limit_bytes=60 * 2**20),
    )(numbers, count, own, last, begin, inverse)


def stack_kernel(text_ref, image_ref, out_ref):
    out_ref[:, 0, :] = text_ref[...]
    out_ref[:, 1, :] = image_ref[...]


def stack_rows(text, image):
    rows, width = text.shape
    return pl.pallas_call(
        stack_kernel,
        grid=(1,),
        out_shape=jax.ShapeDtypeStruct((rows, 2, width), bf16),
        in_specs=[whole(text.shape)] * 2,
        out_specs=whole((rows, 2, width)),
        compiler_params=pltpu.CompilerParams(vmem_limit_bytes=60 * 2**20),
    )(text, image)


def select_kernel(pick_ref, spread_hbm, text_weight, image_weight, send_hbm, unit_ref, spread, send, sems):
    rows = spread.shape[0]
    arrive = pltpu.make_async_copy(spread_hbm, spread, sems.at[0])
    arrive.start()
    arrive.wait()
    for tower, weight in ((0, text_weight), (1, image_weight)):
        product = jnp.dot(spread[:, tower, :], weight[...], preferred_element_type=f32)
        inverse = lax.rsqrt(jnp.sum(product * product, axis=-1, keepdims=True) + eps_norm)
        unit_ref[tower * rows : (tower + 1) * rows] = (product * inverse).astype(bf16)
    copies = []
    per = send.shape[0] // 4
    for k in range(4):
        part = pl.ds(k * per, per)
        send[part] = jnp.dot(pick_ref[part], unit_ref[...], preferred_element_type=f32).astype(bf16)
        copy = pltpu.make_async_copy(send.at[part], send_hbm.at[part], sems.at[1 + k])
        copy.start()
        copies.append(copy)
    for copy in copies:
        copy.wait()


def select_stage(pick, spread, text_weight, image_weight):
    rows, _, width = spread.shape
    hbm = pl.BlockSpec(memory_space=pltpu.HBM)
    return pl.pallas_call(
        select_kernel,
        grid=(1,),
        out_shape=(
            jax.ShapeDtypeStruct((pick.shape[0], width), bf16),
            jax.ShapeDtypeStruct((2 * rows, width), bf16),
        ),
        in_specs=[whole(pick.shape), hbm, whole(text_weight.shape), whole(image_weight.shape)],
        out_specs=(hbm, whole((2 * rows, width))),
        scratch_shapes=[
            pltpu.VMEM(spread.shape, bf16),
            pltpu.VMEM((pick.shape[0], width), bf16),
            pltpu.SemaphoreType.DMA((5,)),
        ],
        compiler_params=pltpu.CompilerParams(vmem_limit_bytes=50 * 2**20),
    )(pick, spread, text_weight, image_weight)


def local(x_img, x_txt, w_img, w_txt, sharpness, offset, lists, counts, holder):
    devices = lax.axis_size(ALL)
    me = lax.axis_index(ALL)
    core = lax.axis_index("c")
    rows, width = x_img.shape
    slots = lists.shape[1]
    scale = sharpness[0]
    shift = offset[0]
    spread = lax.all_to_all(stack_rows(x_txt, x_img), ALL, 0, 0, tiled=True)
    z_txt, r_txt = project(x_txt, w_txt)
    z_img, r_img = project(x_img, w_img)

    numbers = jnp.arange(devices, dtype=jnp.int32)
    hot = holder[None, :] == numbers[:, None]
    source = jnp.sum(jnp.where(lists[:, :, None] == numbers, holder, 0), axis=2)
    table = jnp.dot(hot.astype(bf16), source.astype(bf16), preferred_element_type=f32).astype(jnp.int32)
    count = jnp.sum(jnp.where(hot[me], counts, 0))

    columns = jnp.arange(2 * devices, dtype=jnp.int32)
    near = jnp.concatenate([table[:, 1:9], table[:, 1:9] + devices], axis=1)
    last = jnp.concatenate([table[:, 9:], table[:, 9:] + devices], axis=1)
    pick = (near[:, :, None] == columns).astype(bf16).reshape(16 * devices, 2 * devices)
    pick_last = (last[:, :, None] == columns).astype(bf16).reshape(2 * devices, 2 * devices)
    send, units = select_stage(pick, spread, w_txt, w_img)
    send = send.reshape(devices, 16, width)
    send_last = jnp.dot(pick_last, units, preferred_element_type=f32).astype(bf16).reshape(devices, 2, width)
    mates = lax.all_to_all(send, ALL, 0, 0, tiled=True).reshape(16 * devices, width)
    mates, send_last = lax.optimization_barrier((mates, send_last))
    last = lax.all_to_all(send_last, ALL, 0, 0, tiled=True)

    x_mine = jnp.where(core == 0, x_img, x_txt)
    x_other = swap(jnp.where(core == 0, x_txt, x_img), "c", 1)

    own = jnp.concatenate([z_img, z_txt], axis=0)
    logits = scale * lax.dot_general(z_img, z_txt, TRANSPOSED, preferred_element_type=f32) + shift
    sign = jnp.where(jnp.eye(rows, dtype=bool), 1.0, -1.0)
    coef = (-scale * sign * jax.nn.sigmoid(-sign * logits)).astype(bf16)
    dz = jnp.concatenate(
        [
            jnp.dot(coef, z_txt, preferred_element_type=f32),
            lax.dot_general(coef, z_img, ROWS_FIRST, preferred_element_type=f32),
        ],
        axis=0,
    )
    inverse = jnp.concatenate([r_img, r_txt], axis=0)
    scalars = jnp.stack([scale, shift])
    dz = pair_stage(scalars, count[None], own, mates, dz)
    number = core[None].astype(jnp.int32)
    du, du_mine, du_away = finish_stage(
        scalars, jnp.concatenate([count[None], number]), own, last, dz, inverse
    )
    du_img = du[:rows]
    du_txt = du[rows:]
    du_other = swap(du_away, "c", 1)
    g_img = lax.dot_general(du_img, w_img, TRANSPOSED, preferred_element_type=f32).astype(bf16)
    g_txt = lax.dot_general(du_txt, w_txt, TRANSPOSED, preferred_element_type=f32).astype(bf16)

    factor = (64.0 / (devices * rows)) ** 0.5
    quarter = jnp.bitwise_xor(lax.axis_index("x"), lax.axis_index("y")).astype(jnp.int32)[None]
    pieces = head_gradient(factor, quarter, (x_mine, x_other), (du_mine, du_other))
    pieces, (g_img, g_txt) = reduce_streams(pieces, (g_img, g_txt))
    written = assemble(quarter, number, pieces[::2], width)
    head_img, head_txt = assemble(quarter, 1 - number, pieces[1::2], width, written)
    return (g_img, g_txt, head_img, head_txt)


def solution(mesh):
    grid = Mesh(mesh.devices.reshape(4, 4, 4, 2), ALL)
    placed = (P(ALL, None), P(ALL, None), P(), P(), P(), P(), P(), P(), P())
    return jax.shard_map(
        local,
        mesh=grid,
        in_specs=placed,
        out_specs=(P(ALL, None), P(ALL, None), P(), P()),
        check_vma=False,
    )
```

```python
import jax
import jax.numpy as jnp
from jax import lax
from jax.experimental import pallas as pl
from jax.experimental.pallas import tpu as pltpu
from jax.sharding import Mesh, PartitionSpec as P

eps_norm = 1e-06
ALL = ("x", "z", "y", "c")
TRANSPOSED = (((1,), (1,)), ((), ()))
ROWS_FIRST = (((0,), (0,)), ((), ()))
STREAMS = ((640, "y"), (512, "x"))
bf16 = jnp.bfloat16
f32 = jnp.float32


def project(features, weight):
    product = jnp.dot(features, weight, preferred_element_type=f32)
    inverse = lax.rsqrt(jnp.sum(product * product, axis=-1, keepdims=True) + eps_norm)
    return ((product * inverse).astype(bf16), inverse)


def swap(array, axis, mask):
    if isinstance(axis, str):
        return lax.ppermute(array, axis, [(i, i ^ mask) for i in range(lax.axis_size(axis))])
    size = lax.axis_size(axis[1])
    pairs = [(i * size + j, (i ^ mask) * size + (j ^ mask)) for i in range(size) for j in range(size)]
    return lax.ppermute(array, axis, pairs)


def shift(array, axis, step):
    size = lax.axis_size(axis)
    return lax.ppermute(array, axis, [(i, (i + step) % size) for i in range(size)])


def total_of(own, got):
    total = (own.astype(f32) + got[0].astype(f32)) + (got[1].astype(f32) + got[2].astype(f32))
    return total.astype(bf16)


def whole(shape):
    return pl.BlockSpec(shape, lambda i: (0,) * len(shape))


def kernel_call(body, outs, scalars, arrays, scratch=()):
    return pl.pallas_call(
        body,
        grid=(1,),
        out_shape=outs,
        in_specs=[pl.BlockSpec(memory_space=pltpu.SMEM)] * len(scalars) + [whole(a.shape) for a in arrays],
        out_specs=tuple(whole(o.shape) for o in outs),
        scratch_shapes=scratch,
        compiler_params=pltpu.CompilerParams(vmem_limit_bytes=40 * 2**20),
    )(*scalars, *arrays)


def head_gradient(factor, places, features, through):
    rows, columns = features[0].shape
    width = through[0].shape[1]
    per = columns // 3

    def body(place_ref, xa, xb, da, db, *rest):
        outs, total = rest[:10], rest[10]
        for k in range(3):
            part = slice(k * per, (k + 1) * per)
            grad = lax.dot_general(xa[:, part], da[...], ROWS_FIRST, preferred_element_type=f32)
            grad += lax.dot_general(xb[:, part], db[...], ROWS_FIRST, preferred_element_type=f32)
            total[part] = grad * factor
        first = 0
        for stream, (size, _) in enumerate(STREAMS):
            half = size // 8
            forth, back, upper, lower, kept = outs[5 * stream : 5 * stream + 5]

            def rows_of(place, which, first=first, half=half, stream=stream):
                begin = first + (2 * place_ref[4 * stream + place] + which) * half
                return total[pl.ds(pl.multiple_of(begin, 16), half), :].astype(bf16)

            forth[:half] = rows_of(3, 0)
            forth[half:] = rows_of(2, 1)
            back[:half] = rows_of(1, 0)
            back[half:] = rows_of(3, 1)
            upper[...] = rows_of(2, 0)
            lower[...] = rows_of(1, 1)
            kept[:half] = rows_of(0, 0)
            kept[half:] = rows_of(0, 1)
            first += size

    outs = tuple(
        jax.ShapeDtypeStruct((size // parts, width), bf16) for size, _ in STREAMS for parts in (4, 4, 8, 8, 4)
    )
    return kernel_call(body, outs, (places,), (*features, *through), (pltpu.VMEM((columns, width), f32),))


def pass_on(arrived, pieces):
    width = pieces[0].shape[1]

    def body(*refs):
        for stream in range(2):
            before, after, upper, lower = refs[4 * stream : 4 * stream + 4]
            forth, back = refs[8 + 2 * stream : 10 + 2 * stream]
            half = upper.shape[0]
            forth[...] = (upper[...].astype(f32) + before[:half].astype(f32)).astype(bf16)
            back[...] = (lower[...].astype(f32) + after[half:].astype(f32)).astype(bf16)

    outs = tuple(jax.ShapeDtypeStruct((size // 8, width), bf16) for size, _ in STREAMS for _ in range(2))
    arrays = (*arrived[:2], *pieces[2:4], *arrived[2:], *pieces[7:9])
    return kernel_call(body, outs, (), arrays)


def sum_and_split(index, kept, arrived, passed):
    width = kept[0].shape[1]
    sizes = [quarter.shape[0] for quarter in kept]
    count = sum(sizes) // 4

    def body(index_ref, *refs):
        outs, total = refs[10:14], refs[14]
        first = 0
        for stream, size in enumerate(sizes):
            own, before, after, upper, lower = refs[5 * stream : 5 * stream + 5]
            half = size // 2
            total[first : first + half] = (own[:half].astype(f32) + after[:half].astype(f32)) + upper[...].astype(f32)
            total[first + half : first + size] = (own[half:].astype(f32) + before[half:].astype(f32)) + lower[
                ...
            ].astype(f32)
            first += size
        for m in range(4):
            begin = pl.multiple_of(jnp.bitwise_xor(index_ref[0], m) * count, 8)
            outs[m][...] = total[pl.ds(begin, count), :].astype(bf16)

    outs = tuple(jax.ShapeDtypeStruct((count, width), bf16) for _ in range(4))
    arrays = (kept[0], *arrived[:2], *passed[:2], kept[1], *arrived[2:], *passed[2:])
    return kernel_call(body, outs, (index,), arrays, (pltpu.VMEM((sum(sizes), width), f32),))


def join(index, pieces):
    count, width = pieces[0].shape
    sizes = [size // 4 for size, _ in STREAMS]

    def body(index_ref, *refs):
        ins, outs, rows = refs[:4], refs[4:6], refs[6]
        for m in range(4):
            begin = pl.multiple_of(jnp.bitwise_xor(index_ref[0], m) * count, 8)
            rows[pl.ds(begin, count), :] = ins[m][...].astype(f32)
        outs[0][...] = rows[: sizes[0]].astype(bf16)
        outs[1][...] = rows[sizes[0] :].astype(bf16)

    outs = tuple(jax.ShapeDtypeStruct((size, width), bf16) for size in sizes)
    return kernel_call(body, outs, (index,), pieces, (pltpu.VMEM((4 * count, width), f32),))


def exchange(pieces, axis):
    return [pieces[0]] + [swap(pieces[m], axis, m) for m in (1, 2, 3)]


def both_ways(pieces):
    out = []
    for stream, (_, axis) in enumerate(STREAMS):
        out += [shift(pieces[2 * stream], axis, 1), shift(pieces[2 * stream + 1], axis, -1)]
    return lax.optimization_barrier(out)


def reduce_streams(pieces, beside):
    along_z = lax.axis_index("z").astype(jnp.int32)[None]
    arrived = both_ways([*pieces[:2], *pieces[5:7]])
    passed = both_ways(pass_on(arrived, pieces))
    pieces = exchange(sum_and_split(along_z, [pieces[4], pieces[9]], arrived, passed), "z")
    total = total_of(pieces[0], pieces[1:])
    away, beside = lax.optimization_barrier((swap(total, ("x", "y"), 1), beside))
    total = (total.astype(f32) + away.astype(f32)).astype(bf16)
    total = (total.astype(f32) + swap(total, ("x", "y"), 3).astype(f32)).astype(bf16)
    kept = join(along_z, exchange([total] * 4, "z"))
    near = both_ways([kept[0], kept[0], kept[1], kept[1]])
    halves = [quarter.shape[0] // 2 for quarter in kept]
    far = both_ways([near[0][: halves[0]], near[1][halves[0] :], near[2][: halves[1]], near[3][halves[1] :]])
    out = []
    for stream in range(2):
        joined = jnp.concatenate([kept[stream], *near[2 * stream : 2 * stream + 2], *far[2 * stream : 2 * stream + 2]], axis=0)
        out += [joined, swap(joined, "c", 1)]
    return out, beside


def write_half(index_ref, pieces, target, wide, sems):
    copies = []
    first = 0
    for stream in range(2):
        count = pieces[stream].shape[0] // 4
        for m in range(4):
            at = first + m * count
            wide[at : at + count] = pieces[stream][m * count : (m + 1) * count].astype(f32)
            begin = pl.multiple_of(first + index_ref[4 * stream + m] * count, 32)
            copy = pltpu.make_async_copy(
                wide.at[pl.ds(at, count)], target.at[pl.ds(begin, count)], sems.at[4 * stream + m]
            )
            copy.start()
            copies.append(copy)
        first += 4 * count
    for copy in copies:
        copy.wait()


def assemble(index, tower, pieces, rows, written=()):
    width = pieces[0].shape[1]
    shape = jax.ShapeDtypeStruct((rows, width), f32)
    hbm = pl.BlockSpec(memory_space=pltpu.HBM)

    def body(index_ref, tower_ref, *refs):
        out_img, out_txt, wide, sems = refs[2 + len(written) :]

        @pl.when(tower_ref[0] == 0)
        def _():
            write_half(index_ref, refs[:2], out_img, wide, sems)

        @pl.when(tower_ref[0] != 0)
        def _():
            write_half(index_ref, refs[:2], out_txt, wide, sems)

    return pl.pallas_call(
        body,
        grid=(1,),
        out_shape=(shape, shape),
        in_specs=[pl.BlockSpec(memory_space=pltpu.SMEM)] * 2
        + [whole(piece.shape) for piece in pieces]
        + [hbm] * len(written),
        out_specs=(hbm, hbm),
        input_output_aliases={4 + k: k for k in range(len(written))},
        scratch_shapes=[pltpu.VMEM((rows, width), f32), pltpu.SemaphoreType.DMA((8,))],
        compiler_params=pltpu.CompilerParams(vmem_limit_bytes=40 * 2**20),
    )(index, tower, *pieces, *written)


def pair_kernel(number_ref, count_ref, own_ref, mates_ref, begin_ref, out_ref):
    scale, shift = number_ref[0], number_ref[1]
    mates = mates_ref[...]
    logits = lax.dot_general(own_ref[...], mates, TRANSPOSED, preferred_element_type=f32)
    logits = scale * logits + shift
    column = lax.broadcasted_iota(jnp.int32, logits.shape, 1) & 15
    row = lax.broadcasted_iota(jnp.int32, logits.shape, 0)
    keep = ((column & 7) + 1 < count_ref[0]) & ((column < 8) == (row < logits.shape[0] // 2))
    coef = jnp.where(keep, scale / (1.0 + jnp.exp(-logits)), 0.0).astype(bf16)
    part = jnp.dot(coef, mates, preferred_element_type=f32)

    @pl.when(pl.program_id(0) == 0)
    def _():
        out_ref[...] = begin_ref[...] + part

    @pl.when(pl.program_id(0) != 0)
    def _():
        out_ref[...] += part


def pair_stage(numbers, count, own, mates, begin):
    rows, width = own.shape
    per = 512

    return pl.pallas_call(
        pair_kernel,
        grid=(mates.shape[0] // per,),
        out_shape=jax.ShapeDtypeStruct((rows, width), f32),
        in_specs=[
            pl.BlockSpec(memory_space=pltpu.SMEM),
            pl.BlockSpec(memory_space=pltpu.SMEM),
            whole((rows, width)),
            pl.BlockSpec((per, width), lambda i: (i, 0)),
            whole((rows, width)),
        ],
        out_specs=whole((rows, width)),
        compiler_params=pltpu.CompilerParams(vmem_limit_bytes=60 * 2**20),
    )(numbers, count, own, mates, begin)


def finish_kernel(
    number_ref, count_ref, own_hbm, last_hbm, begin_hbm, inverse_ref, out_ref, mine_ref, other_ref, own, last, begin, sems
):
    copies = [
        pltpu.make_async_copy(source, target, sems.at[k])
        for k, (source, target) in enumerate(((own_hbm, own), (last_hbm, last), (begin_hbm, begin)))
    ]
    for copy in copies:
        copy.start()
    for copy in copies:
        copy.wait()
    scale, shift = number_ref[0], number_ref[1]
    rows = out_ref.shape[0] // 2
    for tower in range(2):
        part = slice(tower * rows, (tower + 1) * rows)
        mates = last[:, tower, :]
        logits = lax.dot_general(own[part], mates, TRANSPOSED, preferred_element_type=f32)
        logits = scale * logits + shift
        coef = jnp.where(count_ref[0] > 9, scale / (1.0 + jnp.exp(-logits)), 0.0).astype(bf16)
        upstream = begin[part] + jnp.dot(coef, mates, preferred_element_type=f32)
        unit = own[part].astype(f32)
        radial = jnp.sum(unit * upstream, axis=-1, keepdims=True)
        through = (inverse_ref[part] * (upstream - unit * radial)).astype(bf16)
        out_ref[part] = through

        @pl.when(count_ref[1] == tower)
        def _():
            mine_ref[...] = through

        @pl.when(count_ref[1] != tower)
        def _():
            other_ref[...] = through


def finish_stage(numbers, count, own, last, begin, inverse):
    smem = pl.BlockSpec(memory_space=pltpu.SMEM)
    hbm = pl.BlockSpec(memory_space=pltpu.HBM)
    return pl.pallas_call(
        finish_kernel,
        grid=(1,),
        out_shape=(
            jax.ShapeDtypeStruct(own.shape, bf16),
            jax.ShapeDtypeStruct((own.shape[0] // 2, own.shape[1]), bf16),
            jax.ShapeDtypeStruct((own.shape[0] // 2, own.shape[1]), bf16),
        ),
        in_specs=[smem, smem, hbm, hbm, hbm, whole(inverse.shape)],
        out_specs=(whole(own.shape),) + (whole((own.shape[0] // 2, own.shape[1])),) * 2,
        scratch_shapes=[pltpu.VMEM(a.shape, a.dtype) for a in (own, last, begin)] + [pltpu.SemaphoreType.DMA((3,))],
        compiler_params=pltpu.CompilerParams(vmem_limit_bytes=60 * 2**20),
    )(numbers, count, own, last, begin, inverse)


def stack_kernel(text_ref, image_ref, out_ref):
    out_ref[:, 0, :] = text_ref[...]
    out_ref[:, 1, :] = image_ref[...]


def stack_rows(text, image):
    rows, width = text.shape
    return pl.pallas_call(
        stack_kernel,
        grid=(1,),
        out_shape=jax.ShapeDtypeStruct((rows, 2, width), bf16),
        in_specs=[whole(text.shape)] * 2,
        out_specs=whole((rows, 2, width)),
        compiler_params=pltpu.CompilerParams(vmem_limit_bytes=60 * 2**20),
    )(text, image)


def select_kernel(pick_ref, spread_hbm, text_weight, image_weight, send_hbm, unit_ref, spread, send, sems):
    rows = spread.shape[0]
    arrive = pltpu.make_async_copy(spread_hbm, spread, sems.at[0])
    arrive.start()
    arrive.wait()
    for tower, weight in ((0, text_weight), (1, image_weight)):
        product = jnp.dot(spread[:, tower, :], weight[...], preferred_element_type=f32)
        inverse = lax.rsqrt(jnp.sum(product * product, axis=-1, keepdims=True) + eps_norm)
        unit_ref[tower * rows : (tower + 1) * rows] = (product * inverse).astype(bf16)
    copies = []
    per = send.shape[0] // 4
    for k in range(4):
        part = pl.ds(k * per, per)
        send[part] = jnp.dot(pick_ref[part], unit_ref[...], preferred_element_type=f32).astype(bf16)
        copy = pltpu.make_async_copy(send.at[part], send_hbm.at[part], sems.at[1 + k])
        copy.start()
        copies.append(copy)
    for copy in copies:
        copy.wait()


def select_stage(pick, spread, text_weight, image_weight):
    rows, _, width = spread.shape
    hbm = pl.BlockSpec(memory_space=pltpu.HBM)
    return pl.pallas_call(
        select_kernel,
        grid=(1,),
        out_shape=(
            jax.ShapeDtypeStruct((pick.shape[0], width), bf16),
            jax.ShapeDtypeStruct((2 * rows, width), bf16),
        ),
        in_specs=[whole(pick.shape), hbm, whole(text_weight.shape), whole(image_weight.shape)],
        out_specs=(hbm, whole((2 * rows, width))),
        scratch_shapes=[
            pltpu.VMEM(spread.shape, bf16),
            pltpu.VMEM((pick.shape[0], width), bf16),
            pltpu.SemaphoreType.DMA((5,)),
        ],
        compiler_params=pltpu.CompilerParams(vmem_limit_bytes=50 * 2**20),
    )(pick, spread, text_weight, image_weight)


def local(x_img, x_txt, w_img, w_txt, sharpness, offset, lists, counts, holder):
    devices = lax.axis_size(ALL)
    me = lax.axis_index(ALL)
    core = lax.axis_index("c")
    rows, width = x_img.shape
    slots = lists.shape[1]
    scale = sharpness[0]
    shift = offset[0]
    spread = lax.all_to_all(stack_rows(x_txt, x_img), ALL, 0, 0, tiled=True)
    z_txt, r_txt = project(x_txt, w_txt)
    z_img, r_img = project(x_img, w_img)

    numbers = jnp.arange(devices, dtype=jnp.int32)
    hot = holder[None, :] == numbers[:, None]
    source = jnp.sum(jnp.where(lists[:, :, None] == numbers, holder, 0), axis=2)
    table = jnp.dot(hot.astype(bf16), source.astype(bf16), preferred_element_type=f32).astype(jnp.int32)
    count = jnp.sum(jnp.where(hot[me], counts, 0))

    columns = jnp.arange(2 * devices, dtype=jnp.int32)
    near = jnp.concatenate([table[:, 1:9], table[:, 1:9] + devices], axis=1)
    last = jnp.concatenate([table[:, 9:], table[:, 9:] + devices], axis=1)
    pick = (near[:, :, None] == columns).astype(bf16).reshape(16 * devices, 2 * devices)
    pick_last = (last[:, :, None] == columns).astype(bf16).reshape(2 * devices, 2 * devices)
    send, units = select_stage(pick, spread, w_txt, w_img)
    send = send.reshape(devices, 16, width)
    send_last = jnp.dot(pick_last, units, preferred_element_type=f32).astype(bf16).reshape(devices, 2, width)
    mates = lax.all_to_all(send, ALL, 0, 0, tiled=True).reshape(16 * devices, width)
    mates, send_last = lax.optimization_barrier((mates, send_last))
    last = lax.all_to_all(send_last, ALL, 0, 0, tiled=True)

    x_mine = jnp.where(core == 0, x_img, x_txt)
    x_other = swap(jnp.where(core == 0, x_txt, x_img), "c", 1)

    own = jnp.concatenate([z_img, z_txt], axis=0)
    logits = scale * lax.dot_general(z_img, z_txt, TRANSPOSED, preferred_element_type=f32) + shift
    sign = jnp.where(jnp.eye(rows, dtype=bool), 1.0, -1.0)
    coef = (-scale * sign * jax.nn.sigmoid(-sign * logits)).astype(bf16)
    dz = jnp.concatenate(
        [
            jnp.dot(coef, z_txt, preferred_element_type=f32),
            lax.dot_general(coef, z_img, ROWS_FIRST, preferred_element_type=f32),
        ],
        axis=0,
    )
    inverse = jnp.concatenate([r_img, r_txt], axis=0)
    scalars = jnp.stack([scale, shift])
    dz = pair_stage(scalars, count[None], own, mates, dz)
    number = core[None].astype(jnp.int32)
    du, du_mine, du_away = finish_stage(
        scalars, jnp.concatenate([count[None], number]), own, last, dz, inverse
    )
    du_img = du[:rows]
    du_txt = du[rows:]
    du_other = swap(du_away, "c", 1)
    g_img = lax.dot_general(du_img, w_img, TRANSPOSED, preferred_element_type=f32).astype(bf16)
    g_txt = lax.dot_general(du_txt, w_txt, TRANSPOSED, preferred_element_type=f32).astype(bf16)

    factor = (64.0 / (devices * rows)) ** 0.5
    quarter = jnp.bitwise_xor(lax.axis_index("x"), lax.axis_index("y"))
    places = []
    for _, axis in STREAMS:
        index = lax.axis_index(axis)
        places += [jnp.bitwise_xor(jnp.bitwise_xor((index + step) & 3, index), quarter) for step in (0, 3, 1, 2)]
    places = jnp.stack(places).astype(jnp.int32)
    pieces = head_gradient(factor, places, (x_mine, x_other), (du_mine, du_other))
    pieces, (g_img, g_txt) = reduce_streams(pieces, (g_img, g_txt))
    written = assemble(places, number, pieces[::2], width)
    head_img, head_txt = assemble(places, 1 - number, pieces[1::2], width, written)
    return (g_img, g_txt, head_img, head_txt)


def solution(mesh):
    grid = Mesh(mesh.devices.reshape(4, 4, 4, 2), ALL)
    placed = (P(ALL, None), P(ALL, None), P(), P(), P(), P(), P(), P(), P())
    return jax.shard_map(
        local,
        mesh=grid,
        in_specs=placed,
        out_specs=(P(ALL, None), P(ALL, None), P(), P()),
        check_vma=False,
    )
```

```python
import jax
import jax.numpy as jnp
from jax import lax
from jax.experimental import pallas as pl
from jax.experimental.pallas import tpu as pltpu
from jax.sharding import Mesh, PartitionSpec as P

eps_norm = 1e-06
ALL = ("x", "z", "y", "c")
TRANSPOSED = (((1,), (1,)), ((), ()))
ROWS_FIRST = (((0,), (0,)), ((), ()))
STREAMS = ((640, "y"), (512, "x"))
bf16 = jnp.bfloat16
f32 = jnp.float32


def project(features, weight):
    product = jnp.dot(features, weight, preferred_element_type=f32)
    inverse = lax.rsqrt(jnp.sum(product * product, axis=-1, keepdims=True) + eps_norm)
    return ((product * inverse).astype(bf16), inverse)


def swap(array, axis, mask):
    if isinstance(axis, str):
        return lax.ppermute(array, axis, [(i, i ^ mask) for i in range(lax.axis_size(axis))])
    size = lax.axis_size(axis[1])
    pairs = [(i * size + j, (i ^ mask) * size + (j ^ mask)) for i in range(size) for j in range(size)]
    return lax.ppermute(array, axis, pairs)


def take(array, index):
    return lax.dynamic_index_in_dim(array, index, 0, keepdims=False)


def total_of(own, got):
    total = (own.astype(f32) + got[0].astype(f32)) + (got[1].astype(f32) + got[2].astype(f32))
    return total.astype(bf16)


def whole(shape):
    return pl.BlockSpec(shape, lambda i: (0,) * len(shape))


def kernel_call(body, outs, scalars, arrays, scratch=(), vmem=40):
    return pl.pallas_call(
        body,
        grid=(1,),
        out_shape=outs,
        in_specs=[pl.BlockSpec(memory_space=pltpu.SMEM)] * len(scalars) + [whole(a.shape) for a in arrays],
        out_specs=tuple(whole(o.shape) for o in outs),
        scratch_shapes=scratch,
        compiler_params=pltpu.CompilerParams(vmem_limit_bytes=vmem * 2**20),
    )(*scalars, *arrays)


def quarters_of(sizes, width, parts):
    return tuple(jax.ShapeDtypeStruct((size // parts, width), bf16) for size in sizes for _ in range(4))


def head_gradient(factor, index, features, through):
    rows, columns = features[0].shape
    width = through[0].shape[1]
    sizes = [size for size, _ in STREAMS]
    per = columns // 3

    def body(index_ref, xa, xb, da, db, *rest):
        outs, total = rest[:8], rest[8]
        for k in range(3):
            part = slice(k * per, (k + 1) * per)
            grad = lax.dot_general(xa[:, part], da[...], ROWS_FIRST, preferred_element_type=f32)
            grad += lax.dot_general(xb[:, part], db[...], ROWS_FIRST, preferred_element_type=f32)
            total[part] = grad * factor
        first = 0
        for stream, size in enumerate(sizes):
            count = size // 4
            for m in range(4):
                begin = pl.multiple_of(first + jnp.bitwise_xor(index_ref[0], m) * count, 32)
                outs[4 * stream + m][...] = total[pl.ds(begin, count), :].astype(bf16)
            first += size

    outs = quarters_of(sizes, width, 4)
    return kernel_call(body, outs, (index,), (*features, *through), (pltpu.VMEM((columns, width), f32),), 60)


def sum_and_split(index, pieces):
    width = pieces[0].shape[1]
    sizes = [pieces[0].shape[0], pieces[4].shape[0]]
    count = sum(sizes) // 4

    def body(index_ref, *refs):
        ins, outs, total = refs[:8], refs[8:12], refs[12]
        first = 0
        for stream, size in enumerate(sizes):
            a, b, c, d = (ins[4 * stream + m][...].astype(f32) for m in range(4))
            total[first : first + size] = (a + b) + (c + d)
            first += size
        for m in range(4):
            begin = pl.multiple_of(jnp.bitwise_xor(index_ref[0], m) * count, 8)
            outs[m][...] = total[pl.ds(begin, count), :].astype(bf16)

    outs = tuple(jax.ShapeDtypeStruct((count, width), bf16) for _ in range(4))
    return kernel_call(body, outs, (index,), pieces, (pltpu.VMEM((sum(sizes), width), f32),))


def join(index, pieces):
    count, width = pieces[0].shape
    sizes = [size // 4 for size, _ in STREAMS]

    def body(index_ref, *refs):
        ins, outs, rows = refs[:4], refs[4:6], refs[6]
        for m in range(4):
            begin = pl.multiple_of(jnp.bitwise_xor(index_ref[0], m) * count, 8)
            rows[pl.ds(begin, count), :] = ins[m][...].astype(f32)
        outs[0][...] = rows[: sizes[0]].astype(bf16)
        outs[1][...] = rows[sizes[0] :].astype(bf16)

    outs = tuple(jax.ShapeDtypeStruct((size, width), bf16) for size in sizes)
    return kernel_call(body, outs, (index,), pieces, (pltpu.VMEM((4 * count, width), f32),))


def exchange(pieces, axis):
    return [pieces[0]] + [swap(pieces[m], axis, m) for m in (1, 2, 3)]


def exchange_streams(pieces):
    got = list(pieces)
    for m in (2, 1, 3):
        for stream, (_, axis) in enumerate(STREAMS):
            got[4 * stream + m] = swap(pieces[4 * stream + m], axis, m)
    return got


def reduce_streams(pieces, beside):
    along_z = lax.axis_index("z").astype(jnp.int32)[None]
    pieces = lax.optimization_barrier(exchange_streams(pieces))
    pieces = exchange(sum_and_split(along_z, pieces), "z")
    total = total_of(pieces[0], pieces[1:])
    away, beside = lax.optimization_barrier((swap(total, ("x", "y"), 1), beside))
    total = (total.astype(f32) + away.astype(f32)).astype(bf16)
    total = (total.astype(f32) + swap(total, ("x", "y"), 3).astype(f32)).astype(bf16)
    kept = join(along_z, exchange([total] * 4, "z"))
    pieces = exchange_streams([kept[0]] * 4 + [kept[1]] * 4)
    out = []
    for stream in range(2):
        joined = jnp.concatenate(pieces[4 * stream : 4 * stream + 4], axis=0)
        out += [joined, swap(joined, "c", 1)]
    return out, beside


def write_half(index_ref, pieces, target, wide, sems):
    copies = []
    first = 0
    for stream in range(2):
        count = pieces[stream].shape[0] // 4
        for m in range(4):
            at = first + m * count
            wide[at : at + count] = pieces[stream][m * count : (m + 1) * count].astype(f32)
            begin = pl.multiple_of(first + jnp.bitwise_xor(index_ref[0], m) * count, 32)
            copy = pltpu.make_async_copy(
                wide.at[pl.ds(at, count)], target.at[pl.ds(begin, count)], sems.at[4 * stream + m]
            )
            copy.start()
            copies.append(copy)
        first += 4 * count
    for copy in copies:
        copy.wait()


def assemble(index, tower, pieces, rows, written=()):
    width = pieces[0].shape[1]
    shape = jax.ShapeDtypeStruct((rows, width), f32)
    hbm = pl.BlockSpec(memory_space=pltpu.HBM)

    def body(index_ref, tower_ref, *refs):
        out_img, out_txt, wide, sems = refs[2 + len(written) :]

        @pl.when(tower_ref[0] == 0)
        def _():
            write_half(index_ref, refs[:2], out_img, wide, sems)

        @pl.when(tower_ref[0] != 0)
        def _():
            write_half(index_ref, refs[:2], out_txt, wide, sems)

    return pl.pallas_call(
        body,
        grid=(1,),
        out_shape=(shape, shape),
        in_specs=[pl.BlockSpec(memory_space=pltpu.SMEM)] * 2
        + [whole(piece.shape) for piece in pieces]
        + [hbm] * len(written),
        out_specs=(hbm, hbm),
        input_output_aliases={4 + k: k for k in range(len(written))},
        scratch_shapes=[pltpu.VMEM((rows, width), f32), pltpu.SemaphoreType.DMA((8,))],
        compiler_params=pltpu.CompilerParams(vmem_limit_bytes=40 * 2**20),
    )(index, tower, *pieces, *written)


def pair_kernel(number_ref, count_ref, own_ref, mates_ref, begin_ref, out_ref):
    scale, shift = number_ref[0], number_ref[1]
    mates = mates_ref[...]
    logits = lax.dot_general(own_ref[...], mates, TRANSPOSED, preferred_element_type=f32)
    logits = scale * logits + shift
    column = lax.broadcasted_iota(jnp.int32, logits.shape, 1) & 15
    row = lax.broadcasted_iota(jnp.int32, logits.shape, 0)
    keep = ((column & 7) + 1 < count_ref[0]) & ((column < 8) == (row < logits.shape[0] // 2))
    coef = jnp.where(keep, scale / (1.0 + jnp.exp(-logits)), 0.0).astype(bf16)
    part = jnp.dot(coef, mates, preferred_element_type=f32)

    @pl.when(pl.program_id(0) == 0)
    def _():
        out_ref[...] = begin_ref[...] + part

    @pl.when(pl.program_id(0) != 0)
    def _():
        out_ref[...] += part


def pair_stage(numbers, count, own, mates, begin):
    rows, width = own.shape
    per = 512

    return pl.pallas_call(
        pair_kernel,
        grid=(mates.shape[0] // per,),
        out_shape=jax.ShapeDtypeStruct((rows, width), f32),
        in_specs=[
            pl.BlockSpec(memory_space=pltpu.SMEM),
            pl.BlockSpec(memory_space=pltpu.SMEM),
            whole((rows, width)),
            pl.BlockSpec((per, width), lambda i: (i, 0)),
            whole((rows, width)),
        ],
        out_specs=whole((rows, width)),
        compiler_params=pltpu.CompilerParams(vmem_limit_bytes=60 * 2**20),
    )(numbers, count, own, mates, begin)


def finish_kernel(
    number_ref, count_ref, own_hbm, last_hbm, begin_hbm, inverse_ref, out_ref, mine_ref, other_ref, own, last, begin, sems
):
    copies = [
        pltpu.make_async_copy(source, target, sems.at[k])
        for k, (source, target) in enumerate(((own_hbm, own), (last_hbm, last), (begin_hbm, begin)))
    ]
    for copy in copies:
        copy.start()
    for copy in copies:
        copy.wait()
    scale, shift = number_ref[0], number_ref[1]
    rows = out_ref.shape[0] // 2
    for tower in range(2):
        part = slice(tower * rows, (tower + 1) * rows)
        mates = last[:, tower, :]
        logits = lax.dot_general(own[part], mates, TRANSPOSED, preferred_element_type=f32)
        logits = scale * logits + shift
        coef = jnp.where(count_ref[0] > 9, scale / (1.0 + jnp.exp(-logits)), 0.0).astype(bf16)
        upstream = begin[part] + jnp.dot(coef, mates, preferred_element_type=f32)
        unit = own[part].astype(f32)
        radial = jnp.sum(unit * upstream, axis=-1, keepdims=True)
        through = (inverse_ref[part] * (upstream - unit * radial)).astype(bf16)
        out_ref[part] = through

        @pl.when(count_ref[1] == tower)
        def _():
            mine_ref[...] = through

        @pl.when(count_ref[1] != tower)
        def _():
            other_ref[...] = through


def finish_stage(numbers, count, own, last, begin, inverse):
    smem = pl.BlockSpec(memory_space=pltpu.SMEM)
    hbm = pl.BlockSpec(memory_space=pltpu.HBM)
    return pl.pallas_call(
        finish_kernel,
        grid=(1,),
        out_shape=(
            jax.ShapeDtypeStruct(own.shape, bf16),
            jax.ShapeDtypeStruct((own.shape[0] // 2, own.shape[1]), bf16),
            jax.ShapeDtypeStruct((own.shape[0] // 2, own.shape[1]), bf16),
        ),
        in_specs=[smem, smem, hbm, hbm, hbm, whole(inverse.shape)],
        out_specs=(whole(own.shape),) + (whole((own.shape[0] // 2, own.shape[1])),) * 2,
        scratch_shapes=[pltpu.VMEM(a.shape, a.dtype) for a in (own, last, begin)] + [pltpu.SemaphoreType.DMA((3,))],
        compiler_params=pltpu.CompilerParams(vmem_limit_bytes=60 * 2**20),
    )(numbers, count, own, last, begin, inverse)


def stack_kernel(text_ref, image_ref, out_ref):
    out_ref[:, 0, :] = text_ref[...]
    out_ref[:, 1, :] = image_ref[...]


def stack_rows(text, image):
    rows, width = text.shape
    return pl.pallas_call(
        stack_kernel,
        grid=(1,),
        out_shape=jax.ShapeDtypeStruct((rows, 2, width), bf16),
        in_specs=[whole(text.shape)] * 2,
        out_specs=whole((rows, 2, width)),
        compiler_params=pltpu.CompilerParams(vmem_limit_bytes=60 * 2**20),
    )(text, image)


def select_kernel(
    pick_hbm, spread_hbm, text_hbm, image_hbm, send_hbm, unit_ref, pick, spread, text_weight, image_weight, send, sems
):
    rows = spread.shape[0]
    pairs = ((spread_hbm, spread), (text_hbm, text_weight), (image_hbm, image_weight), (pick_hbm, pick))
    loads = [pltpu.make_async_copy(source, target, sems.at[k]) for k, (source, target) in enumerate(pairs)]
    for load in loads:
        load.start()
    loads[0].wait()
    for tower, weight in ((0, text_weight), (1, image_weight)):
        loads[1 + tower].wait()
        product = jnp.dot(spread[:, tower, :], weight[...], preferred_element_type=f32)
        inverse = lax.rsqrt(jnp.sum(product * product, axis=-1, keepdims=True) + eps_norm)
        unit_ref[tower * rows : (tower + 1) * rows] = (product * inverse).astype(bf16)
    loads[3].wait()
    copies = []
    per = send.shape[0] // 4
    for k in range(4):
        part = pl.ds(k * per, per)
        send[part] = jnp.dot(pick[part], unit_ref[...], preferred_element_type=f32).astype(bf16)
        copy = pltpu.make_async_copy(send.at[part], send_hbm.at[part], sems.at[4 + k])
        copy.start()
        copies.append(copy)
    for copy in copies:
        copy.wait()


def select_stage(pick, spread, text_weight, image_weight):
    rows, _, width = spread.shape
    hbm = pl.BlockSpec(memory_space=pltpu.HBM)
    return pl.pallas_call(
        select_kernel,
        grid=(1,),
        out_shape=(
            jax.ShapeDtypeStruct((pick.shape[0], width), bf16),
            jax.ShapeDtypeStruct((2 * rows, width), bf16),
        ),
        in_specs=[hbm] * 4,
        out_specs=(hbm, whole((2 * rows, width))),
        scratch_shapes=[
            *(pltpu.VMEM(array.shape, bf16) for array in (pick, spread, text_weight, image_weight)),
            pltpu.VMEM((pick.shape[0], width), bf16),
            pltpu.SemaphoreType.DMA((8,)),
        ],
        compiler_params=pltpu.CompilerParams(vmem_limit_bytes=50 * 2**20),
    )(pick, spread, text_weight, image_weight)


def local(x_img, x_txt, w_img, w_txt, sharpness, offset, lists, counts, holder):
    devices = lax.axis_size(ALL)
    me = lax.axis_index(ALL)
    core = lax.axis_index("c")
    rows, width = x_img.shape
    slots = lists.shape[1]
    scale = sharpness[0]
    shift = offset[0]
    spread = lax.all_to_all(stack_rows(x_txt, x_img), ALL, 0, 0, tiled=True)
    z_txt, r_txt = project(x_txt, w_txt)
    z_img, r_img = project(x_img, w_img)

    numbers = jnp.arange(devices, dtype=jnp.int32)
    hot = holder[None, :] == numbers[:, None]
    source = jnp.sum(jnp.where(lists[:, :, None] == numbers, holder, 0), axis=2)
    table = jnp.dot(hot.astype(bf16), source.astype(bf16), preferred_element_type=f32).astype(jnp.int32)
    count = jnp.sum(jnp.where(hot[me], counts, 0))

    columns = jnp.arange(2 * devices, dtype=jnp.int32)
    near = jnp.concatenate([table[:, 1:9], table[:, 1:9] + devices], axis=1)
    last = jnp.concatenate([table[:, 9:], table[:, 9:] + devices], axis=1)
    pick = (near[:, :, None] == columns).astype(bf16).reshape(16 * devices, 2 * devices)
    pick_last = (last[:, :, None] == columns).astype(bf16).reshape(2 * devices, 2 * devices)
    send, units = select_stage(pick, spread, w_txt, w_img)
    send = send.reshape(devices, 16, width)
    send_last = jnp.dot(pick_last, units, preferred_element_type=f32).astype(bf16).reshape(devices, 2, width)
    mates = lax.all_to_all(send, ALL, 0, 0, tiled=True).reshape(16 * devices, width)
    mates, send_last = lax.optimization_barrier((mates, send_last))
    last = lax.all_to_all(send_last, ALL, 0, 0, tiled=True)

    x_mine = jnp.where(core == 0, x_img, x_txt)
    x_other = swap(jnp.where(core == 0, x_txt, x_img), "c", 1)

    own = jnp.concatenate([z_img, z_txt], axis=0)
    logits = scale * lax.dot_general(z_img, z_txt, TRANSPOSED, preferred_element_type=f32) + shift
    sign = jnp.where(jnp.eye(rows, dtype=bool), 1.0, -1.0)
    coef = (-scale * sign * jax.nn.sigmoid(-sign * logits)).astype(bf16)
    dz = jnp.concatenate(
        [
            jnp.dot(coef, z_txt, preferred_element_type=f32),
            lax.dot_general(coef, z_img, ROWS_FIRST, preferred_element_type=f32),
        ],
        axis=0,
    )
    inverse = jnp.concatenate([r_img, r_txt], axis=0)
    scalars = jnp.stack([scale, shift])
    dz = pair_stage(scalars, count[None], own, mates, dz)
    number = core[None].astype(jnp.int32)
    du, du_mine, du_away = finish_stage(
        scalars, jnp.concatenate([count[None], number]), own, last, dz, inverse
    )
    du_img = du[:rows]
    du_txt = du[rows:]
    du_other = swap(du_away, "c", 1)
    g_img = lax.dot_general(du_img, w_img, TRANSPOSED, preferred_element_type=f32).astype(bf16)
    g_txt = lax.dot_general(du_txt, w_txt, TRANSPOSED, preferred_element_type=f32).astype(bf16)

    factor = (64.0 / (devices * rows)) ** 0.5
    quarter = jnp.bitwise_xor(lax.axis_index("x"), lax.axis_index("y")).astype(jnp.int32)[None]
    pieces = head_gradient(factor, quarter, (x_mine, x_other), (du_mine, du_other))
    pieces, (g_img, g_txt) = reduce_streams(pieces, (g_img, g_txt))
    written = assemble(quarter, number, pieces[::2], width)
    head_img, head_txt = assemble(quarter, 1 - number, pieces[1::2], width, written)
    return (g_img, g_txt, head_img, head_txt)


def solution(mesh):
    grid = Mesh(mesh.devices.reshape(4, 4, 4, 2), ALL)
    placed = (P(ALL, None), P(ALL, None), P(), P(), P(), P(), P(), P(), P())
    return jax.shard_map(
        local,
        mesh=grid,
        in_specs=placed,
        out_specs=(P(ALL, None), P(ALL, None), P(), P()),
        check_vma=False,
    )
```

```python
import jax
import jax.numpy as jnp
from jax import lax
from jax.experimental import pallas as pl
from jax.experimental.pallas import tpu as pltpu
from jax.sharding import Mesh, PartitionSpec as P

eps_norm = 1e-06
ALL = ("x", "z", "y", "c")
TRANSPOSED = (((1,), (1,)), ((), ()))
ROWS_FIRST = (((0,), (0,)), ((), ()))
STREAMS = ((512, "y"), (640, "x"))
bf16 = jnp.bfloat16
f32 = jnp.float32


def project(features, weight):
    product = jnp.dot(features, weight, preferred_element_type=f32)
    inverse = lax.rsqrt(jnp.sum(product * product, axis=-1, keepdims=True) + eps_norm)
    return ((product * inverse).astype(bf16), inverse)


def swap(array, axis, mask):
    if isinstance(axis, str):
        return lax.ppermute(array, axis, [(i, i ^ mask) for i in range(lax.axis_size(axis))])
    size = lax.axis_size(axis[1])
    pairs = [(i * size + j, (i ^ mask) * size + (j ^ mask)) for i in range(size) for j in range(size)]
    return lax.ppermute(array, axis, pairs)


def shift(array, axis, step):
    size = lax.axis_size(axis)
    return lax.ppermute(array, axis, [(i, (i + step) % size) for i in range(size)])


def total_of(own, got):
    total = (own.astype(f32) + got[0].astype(f32)) + (got[1].astype(f32) + got[2].astype(f32))
    return total.astype(bf16)


def whole(shape):
    return pl.BlockSpec(shape, lambda i: (0,) * len(shape))


def kernel_call(body, outs, scalars, arrays, scratch=()):
    return pl.pallas_call(
        body,
        grid=(1,),
        out_shape=outs,
        in_specs=[pl.BlockSpec(memory_space=pltpu.SMEM)] * len(scalars) + [whole(a.shape) for a in arrays],
        out_specs=tuple(whole(o.shape) for o in outs),
        scratch_shapes=scratch,
        compiler_params=pltpu.CompilerParams(vmem_limit_bytes=40 * 2**20),
    )(*scalars, *arrays)


def head_gradient(factor, places, features, through):
    rows, columns = features[0].shape
    width = through[0].shape[1]
    per = columns // 3
    direct = STREAMS[0][0]
    quarter, half = direct // 4, STREAMS[1][0] // 8

    def body(place_ref, xa, xb, da, db, *rest):
        outs, (forth, back, upper, lower, kept), total = rest[:4], rest[4:9], rest[9]
        for k in range(3):
            part = slice(k * per, (k + 1) * per)
            grad = lax.dot_general(xa[:, part], da[...], ROWS_FIRST, preferred_element_type=f32)
            grad += lax.dot_general(xb[:, part], db[...], ROWS_FIRST, preferred_element_type=f32)
            total[part] = grad * factor
        for m in range(4):
            begin = pl.multiple_of(jnp.bitwise_xor(place_ref[0], m) * quarter, 32)
            outs[m][...] = total[pl.ds(begin, quarter), :].astype(bf16)

        def rows_of(place, which):
            begin = direct + (2 * place_ref[place] + which) * half
            return total[pl.ds(pl.multiple_of(begin, 16), half), :].astype(bf16)

        forth[:half] = rows_of(3, 0)
        forth[half:] = rows_of(2, 1)
        back[:half] = rows_of(1, 0)
        back[half:] = rows_of(3, 1)
        upper[...] = rows_of(2, 0)
        lower[...] = rows_of(1, 1)
        kept[:half] = rows_of(0, 0)
        kept[half:] = rows_of(0, 1)

    sizes = (quarter,) * 4 + (2 * half, 2 * half, half, half, 2 * half)
    outs = tuple(jax.ShapeDtypeStruct((size, width), bf16) for size in sizes)
    return kernel_call(body, outs, (places,), (*features, *through), (pltpu.VMEM((columns, width), f32),))


def pass_on(before, after, upper, lower):
    half, width = upper.shape

    def body(before_ref, after_ref, upper_ref, lower_ref, forth, back):
        forth[...] = (upper_ref[...].astype(f32) + before_ref[:half].astype(f32)).astype(bf16)
        back[...] = (lower_ref[...].astype(f32) + after_ref[half:].astype(f32)).astype(bf16)

    return kernel_call(body, (jax.ShapeDtypeStruct((half, width), bf16),) * 2, (), (before, after, upper, lower))


def sum_and_split(index, direct, ring):
    quarter, width = direct[0].shape
    half = ring[0].shape[0] // 2
    count = (quarter + 2 * half) // 4

    def body(index_ref, *refs):
        (own, before, after, upper, lower), outs, total = refs[4:9], refs[9:13], refs[13]
        a, b, c, d = (ref[...].astype(f32) for ref in refs[:4])
        total[:quarter] = (a + b) + (c + d)
        middle = quarter + half
        total[quarter:middle] = own[:half].astype(f32) + after[:half].astype(f32) + upper[...].astype(f32)
        total[middle:] = own[half:].astype(f32) + before[half:].astype(f32) + lower[...].astype(f32)
        for m in range(4):
            begin = pl.multiple_of(jnp.bitwise_xor(index_ref[0], m) * count, 8)
            outs[m][...] = total[pl.ds(begin, count), :].astype(bf16)

    outs = tuple(jax.ShapeDtypeStruct((count, width), bf16) for _ in range(4))
    return kernel_call(body, outs, (index,), (*direct, *ring), (pltpu.VMEM((quarter + 2 * half, width), f32),))


def join(index, pieces):
    count, width = pieces[0].shape
    sizes = [size // 4 for size, _ in STREAMS]

    def body(index_ref, *refs):
        ins, outs, rows = refs[:4], refs[4:6], refs[6]
        for m in range(4):
            begin = pl.multiple_of(jnp.bitwise_xor(index_ref[0], m) * count, 8)
            rows[pl.ds(begin, count), :] = ins[m][...].astype(f32)
        outs[0][...] = rows[: sizes[0]].astype(bf16)
        outs[1][...] = rows[sizes[0] :].astype(bf16)

    outs = tuple(jax.ShapeDtypeStruct((size, width), bf16) for size in sizes)
    return kernel_call(body, outs, (index,), pieces, (pltpu.VMEM((4 * count, width), f32),))


def exchange(pieces, axis):
    return [pieces[0]] + [swap(pieces[m], axis, m) for m in (1, 2, 3)]


def exchange_streams(pieces):
    got = list(pieces)
    for m in (2, 1, 3):
        for stream, (_, axis) in enumerate(STREAMS):
            got[4 * stream + m] = swap(pieces[4 * stream + m], axis, m)
    return got


def reduce_streams(pieces, beside):
    along_z = lax.axis_index("z").astype(jnp.int32)[None]
    forth, back, upper, lower, own = pieces[4:]
    axis = STREAMS[1][1]
    before, after = shift(forth, axis, 1), shift(back, axis, -1)
    direct = exchange(pieces[:4], STREAMS[0][1])
    forth, back = pass_on(before, after, upper, lower)
    ring = [own, before, after, shift(forth, axis, 1), shift(back, axis, -1)]
    pieces = exchange(sum_and_split(along_z, direct, ring), "z")
    total = total_of(pieces[0], pieces[1:])
    away, beside = lax.optimization_barrier((swap(total, ("x", "y"), 1), beside))
    total = (total.astype(f32) + away.astype(f32)).astype(bf16)
    total = (total.astype(f32) + swap(total, ("x", "y"), 3).astype(f32)).astype(bf16)
    kept = join(along_z, exchange([total] * 4, "z"))
    pieces = lax.optimization_barrier(exchange_streams([kept[0]] * 4 + [kept[1]] * 4))
    out = []
    for stream in range(2):
        joined = jnp.concatenate(pieces[4 * stream : 4 * stream + 4], axis=0)
        out += [joined, swap(joined, "c", 1)]
    return out, beside


def write_half(index_ref, pieces, target, wide, sems):
    copies = []
    first = 0
    for stream in range(2):
        count = pieces[stream].shape[0] // 4
        for m in range(4):
            at = first + m * count
            wide[at : at + count] = pieces[stream][m * count : (m + 1) * count].astype(f32)
            begin = pl.multiple_of(first + jnp.bitwise_xor(index_ref[0], m) * count, 32)
            copy = pltpu.make_async_copy(
                wide.at[pl.ds(at, count)], target.at[pl.ds(begin, count)], sems.at[4 * stream + m]
            )
            copy.start()
            copies.append(copy)
        first += 4 * count
    for copy in copies:
        copy.wait()


def assemble(index, tower, pieces, rows, written=()):
    width = pieces[0].shape[1]
    shape = jax.ShapeDtypeStruct((rows, width), f32)
    hbm = pl.BlockSpec(memory_space=pltpu.HBM)

    def body(index_ref, tower_ref, *refs):
        out_img, out_txt, wide, sems = refs[2 + len(written) :]

        @pl.when(tower_ref[0] == 0)
        def _():
            write_half(index_ref, refs[:2], out_img, wide, sems)

        @pl.when(tower_ref[0] != 0)
        def _():
            write_half(index_ref, refs[:2], out_txt, wide, sems)

    return pl.pallas_call(
        body,
        grid=(1,),
        out_shape=(shape, shape),
        in_specs=[pl.BlockSpec(memory_space=pltpu.SMEM)] * 2
        + [whole(piece.shape) for piece in pieces]
        + [hbm] * len(written),
        out_specs=(hbm, hbm),
        input_output_aliases={4 + k: k for k in range(len(written))},
        scratch_shapes=[pltpu.VMEM((rows, width), f32), pltpu.SemaphoreType.DMA((8,))],
        compiler_params=pltpu.CompilerParams(vmem_limit_bytes=40 * 2**20),
    )(index, tower, *pieces, *written)


def pair_kernel(number_ref, count_ref, own_ref, mates_ref, begin_ref, out_ref):
    scale, shift = number_ref[0], number_ref[1]
    mates = mates_ref[...]
    logits = lax.dot_general(own_ref[...], mates, TRANSPOSED, preferred_element_type=f32)
    logits = scale * logits + shift
    column = lax.broadcasted_iota(jnp.int32, logits.shape, 1) & 15
    row = lax.broadcasted_iota(jnp.int32, logits.shape, 0)
    keep = ((column & 7) + 1 < count_ref[0]) & ((column < 8) == (row < logits.shape[0] // 2))
    coef = jnp.where(keep, scale / (1.0 + jnp.exp(-logits)), 0.0).astype(bf16)
    part = jnp.dot(coef, mates, preferred_element_type=f32)

    @pl.when(pl.program_id(0) == 0)
    def _():
        out_ref[...] = begin_ref[...] + part

    @pl.when(pl.program_id(0) != 0)
    def _():
        out_ref[...] += part


def pair_stage(numbers, count, own, mates, begin):
    rows, width = own.shape
    per = 512

    return pl.pallas_call(
        pair_kernel,
        grid=(mates.shape[0] // per,),
        out_shape=jax.ShapeDtypeStruct((rows, width), f32),
        in_specs=[
            pl.BlockSpec(memory_space=pltpu.SMEM),
            pl.BlockSpec(memory_space=pltpu.SMEM),
            whole((rows, width)),
            pl.BlockSpec((per, width), lambda i: (i, 0)),
            whole((rows, width)),
        ],
        out_specs=whole((rows, width)),
        compiler_params=pltpu.CompilerParams(vmem_limit_bytes=60 * 2**20),
    )(numbers, count, own, mates, begin)


def finish_kernel(
    number_ref, count_ref, own_hbm, last_hbm, begin_hbm, inverse_ref, out_ref, mine_ref, other_ref, own, last, begin, sems
):
    copies = [
        pltpu.make_async_copy(source, target, sems.at[k])
        for k, (source, target) in enumerate(((own_hbm, own), (last_hbm, last), (begin_hbm, begin)))
    ]
    for copy in copies:
        copy.start()
    for copy in copies:
        copy.wait()
    scale, shift = number_ref[0], number_ref[1]
    rows = out_ref.shape[0] // 2
    for tower in range(2):
        part = slice(tower * rows, (tower + 1) * rows)
        mates = last[:, tower, :]
        logits = lax.dot_general(own[part], mates, TRANSPOSED, preferred_element_type=f32)
        logits = scale * logits + shift
        coef = jnp.where(count_ref[0] > 9, scale / (1.0 + jnp.exp(-logits)), 0.0).astype(bf16)
        upstream = begin[part] + jnp.dot(coef, mates, preferred_element_type=f32)
        unit = own[part].astype(f32)
        radial = jnp.sum(unit * upstream, axis=-1, keepdims=True)
        through = (inverse_ref[part] * (upstream - unit * radial)).astype(bf16)
        out_ref[part] = through

        @pl.when(count_ref[1] == tower)
        def _():
            mine_ref[...] = through

        @pl.when(count_ref[1] != tower)
        def _():
            other_ref[...] = through


def finish_stage(numbers, count, own, last, begin, inverse):
    smem = pl.BlockSpec(memory_space=pltpu.SMEM)
    hbm = pl.BlockSpec(memory_space=pltpu.HBM)
    return pl.pallas_call(
        finish_kernel,
        grid=(1,),
        out_shape=(
            jax.ShapeDtypeStruct(own.shape, bf16),
            jax.ShapeDtypeStruct((own.shape[0] // 2, own.shape[1]), bf16),
            jax.ShapeDtypeStruct((own.shape[0] // 2, own.shape[1]), bf16),
        ),
        in_specs=[smem, smem, hbm, hbm, hbm, whole(inverse.shape)],
        out_specs=(whole(own.shape),) + (whole((own.shape[0] // 2, own.shape[1])),) * 2,
        scratch_shapes=[pltpu.VMEM(a.shape, a.dtype) for a in (own, last, begin)] + [pltpu.SemaphoreType.DMA((3,))],
        compiler_params=pltpu.CompilerParams(vmem_limit_bytes=60 * 2**20),
    )(numbers, count, own, last, begin, inverse)


def stack_kernel(text_ref, image_ref, out_ref):
    out_ref[:, 0, :] = text_ref[...]
    out_ref[:, 1, :] = image_ref[...]


def stack_rows(text, image):
    rows, width = text.shape
    return pl.pallas_call(
        stack_kernel,
        grid=(1,),
        out_shape=jax.ShapeDtypeStruct((rows, 2, width), bf16),
        in_specs=[whole(text.shape)] * 2,
        out_specs=whole((rows, 2, width)),
        compiler_params=pltpu.CompilerParams(vmem_limit_bytes=60 * 2**20),
    )(text, image)


def select_kernel(
    pick_hbm, spread_hbm, text_hbm, image_hbm, send_hbm, unit_ref, pick, spread, text_weight, image_weight, send, sems
):
    rows = spread.shape[0]
    pairs = ((spread_hbm, spread), (text_hbm, text_weight), (image_hbm, image_weight), (pick_hbm, pick))
    loads = [pltpu.make_async_copy(source, target, sems.at[k]) for k, (source, target) in enumerate(pairs)]
    for load in loads:
        load.start()
    loads[0].wait()
    for tower, weight in ((0, text_weight), (1, image_weight)):
        loads[1 + tower].wait()
        product = jnp.dot(spread[:, tower, :], weight[...], preferred_element_type=f32)
        inverse = lax.rsqrt(jnp.sum(product * product, axis=-1, keepdims=True) + eps_norm)
        unit_ref[tower * rows : (tower + 1) * rows] = (product * inverse).astype(bf16)
    loads[3].wait()
    copies = []
    per = send.shape[0] // 4
    for k in range(4):
        part = pl.ds(k * per, per)
        send[part] = jnp.dot(pick[part], unit_ref[...], preferred_element_type=f32).astype(bf16)
        copy = pltpu.make_async_copy(send.at[part], send_hbm.at[part], sems.at[4 + k])
        copy.start()
        copies.append(copy)
    for copy in copies:
        copy.wait()


def select_stage(pick, spread, text_weight, image_weight):
    rows, _, width = spread.shape
    hbm = pl.BlockSpec(memory_space=pltpu.HBM)
    return pl.pallas_call(
        select_kernel,
        grid=(1,),
        out_shape=(
            jax.ShapeDtypeStruct((pick.shape[0], width), bf16),
            jax.ShapeDtypeStruct((2 * rows, width), bf16),
        ),
        in_specs=[hbm] * 4,
        out_specs=(hbm, whole((2 * rows, width))),
        scratch_shapes=[
            *(pltpu.VMEM(array.shape, bf16) for array in (pick, spread, text_weight, image_weight)),
            pltpu.VMEM((pick.shape[0], width), bf16),
            pltpu.SemaphoreType.DMA((8,)),
        ],
        compiler_params=pltpu.CompilerParams(vmem_limit_bytes=50 * 2**20),
    )(pick, spread, text_weight, image_weight)


def local(x_img, x_txt, w_img, w_txt, sharpness, offset, lists, counts, holder):
    devices = lax.axis_size(ALL)
    me = lax.axis_index(ALL)
    core = lax.axis_index("c")
    rows, width = x_img.shape
    slots = lists.shape[1]
    scale = sharpness[0]
    shift = offset[0]
    spread = lax.all_to_all(stack_rows(x_txt, x_img), ALL, 0, 0, tiled=True)
    z_txt, r_txt = project(x_txt, w_txt)
    z_img, r_img = project(x_img, w_img)

    numbers = jnp.arange(devices, dtype=jnp.int32)
    hot = holder[None, :] == numbers[:, None]
    source = jnp.sum(jnp.where(lists[:, :, None] == numbers, holder, 0), axis=2)
    table = jnp.dot(hot.astype(bf16), source.astype(bf16), preferred_element_type=f32).astype(jnp.int32)
    count = jnp.sum(jnp.where(hot[me], counts, 0))

    columns = jnp.arange(2 * devices, dtype=jnp.int32)
    near = jnp.concatenate([table[:, 1:9], table[:, 1:9] + devices], axis=1)
    last = jnp.concatenate([table[:, 9:], table[:, 9:] + devices], axis=1)
    pick = (near[:, :, None] == columns).astype(bf16).reshape(16 * devices, 2 * devices)
    pick_last = (last[:, :, None] == columns).astype(bf16).reshape(2 * devices, 2 * devices)
    send, units = select_stage(pick, spread, w_txt, w_img)
    send = send.reshape(devices, 16, width)
    send_last = jnp.dot(pick_last, units, preferred_element_type=f32).astype(bf16).reshape(devices, 2, width)
    mates = lax.all_to_all(send, ALL, 0, 0, tiled=True).reshape(16 * devices, width)
    mates, send_last = lax.optimization_barrier((mates, send_last))
    last = lax.all_to_all(send_last, ALL, 0, 0, tiled=True)

    x_mine = jnp.where(core == 0, x_img, x_txt)
    x_other = swap(jnp.where(core == 0, x_txt, x_img), "c", 1)

    own = jnp.concatenate([z_img, z_txt], axis=0)
    logits = scale * lax.dot_general(z_img, z_txt, TRANSPOSED, preferred_element_type=f32) + shift
    sign = jnp.where(jnp.eye(rows, dtype=bool), 1.0, -1.0)
    coef = (-scale * sign * jax.nn.sigmoid(-sign * logits)).astype(bf16)
    dz = jnp.concatenate(
        [
            jnp.dot(coef, z_txt, preferred_element_type=f32),
            lax.dot_general(coef, z_img, ROWS_FIRST, preferred_element_type=f32),
        ],
        axis=0,
    )
    inverse = jnp.concatenate([r_img, r_txt], axis=0)
    scalars = jnp.stack([scale, shift])
    dz = pair_stage(scalars, count[None], own, mates, dz)
    number = core[None].astype(jnp.int32)
    du, du_mine, du_away = finish_stage(
        scalars, jnp.concatenate([count[None], number]), own, last, dz, inverse
    )
    du_img = du[:rows]
    du_txt = du[rows:]
    du_other = swap(du_away, "c", 1)
    g_img = lax.dot_general(du_img, w_img, TRANSPOSED, preferred_element_type=f32).astype(bf16)
    g_txt = lax.dot_general(du_txt, w_txt, TRANSPOSED, preferred_element_type=f32).astype(bf16)

    factor = (64.0 / (devices * rows)) ** 0.5
    quarter = jnp.bitwise_xor(lax.axis_index("x"), lax.axis_index("y"))
    index = lax.axis_index(STREAMS[1][1])
    places = [jnp.bitwise_xor(jnp.bitwise_xor((index + step) & 3, index), quarter) for step in (0, 3, 1, 2)]
    places = jnp.stack(places).astype(jnp.int32)
    pieces = head_gradient(factor, places, (x_mine, x_other), (du_mine, du_other))
    pieces, (g_img, g_txt) = reduce_streams(pieces, (g_img, g_txt))
    written = assemble(places, number, pieces[::2], width)
    head_img, head_txt = assemble(places, 1 - number, pieces[1::2], width, written)
    return (g_img, g_txt, head_img, head_txt)


def solution(mesh):
    grid = Mesh(mesh.devices.reshape(4, 4, 4, 2), ALL)
    placed = (P(ALL, None), P(ALL, None), P(), P(), P(), P(), P(), P(), P())
    return jax.shard_map(
        local,
        mesh=grid,
        in_specs=placed,
        out_specs=(P(ALL, None), P(ALL, None), P(), P()),
        check_vma=False,
    )
```

```python
import jax
import jax.numpy as jnp
from jax import lax
from jax.experimental import pallas as pl
from jax.experimental.pallas import tpu as pltpu
from jax.sharding import Mesh, PartitionSpec as P

eps_norm = 1e-06
ALL = ("x", "z", "y", "c")
TRANSPOSED = (((1,), (1,)), ((), ()))
ROWS_FIRST = (((0,), (0,)), ((), ()))
STREAMS = ((512, "y"), (640, "x"))
bf16 = jnp.bfloat16
f32 = jnp.float32


def project(features, weight):
    product = jnp.dot(features, weight, preferred_element_type=f32)
    inverse = lax.rsqrt(jnp.sum(product * product, axis=-1, keepdims=True) + eps_norm)
    return ((product * inverse).astype(bf16), inverse)


def swap(array, axis, mask):
    if isinstance(axis, str):
        return lax.ppermute(array, axis, [(i, i ^ mask) for i in range(lax.axis_size(axis))])
    size = lax.axis_size(axis[1])
    pairs = [(i * size + j, (i ^ mask) * size + (j ^ mask)) for i in range(size) for j in range(size)]
    return lax.ppermute(array, axis, pairs)


def shift(array, axis, step):
    size = lax.axis_size(axis)
    return lax.ppermute(array, axis, [(i, (i + step) % size) for i in range(size)])


def total_of(own, got):
    total = (own.astype(f32) + got[0].astype(f32)) + (got[1].astype(f32) + got[2].astype(f32))
    return total.astype(bf16)


def whole(shape):
    return pl.BlockSpec(shape, lambda i: (0,) * len(shape))


def kernel_call(body, outs, scalars, arrays, scratch=()):
    return pl.pallas_call(
        body,
        grid=(1,),
        out_shape=outs,
        in_specs=[pl.BlockSpec(memory_space=pltpu.SMEM)] * len(scalars) + [whole(a.shape) for a in arrays],
        out_specs=tuple(whole(o.shape) for o in outs),
        scratch_shapes=scratch,
        compiler_params=pltpu.CompilerParams(vmem_limit_bytes=40 * 2**20),
    )(*scalars, *arrays)


def head_gradient(factor, places, features, through):
    rows, columns = features[0].shape
    width = through[0].shape[1]
    per = columns // 3
    direct = STREAMS[0][0]
    quarter, half = direct // 4, STREAMS[1][0] // 8

    def body(place_ref, xa, xb, da, db, *rest):
        outs, (forth, back, upper, lower, kept), total = rest[:4], rest[4:9], rest[9]
        for k in range(3):
            part = slice(k * per, (k + 1) * per)
            grad = lax.dot_general(xa[:, part], da[...], ROWS_FIRST, preferred_element_type=f32)
            grad += lax.dot_general(xb[:, part], db[...], ROWS_FIRST, preferred_element_type=f32)
            total[part] = grad * factor
        for m in range(4):
            begin = pl.multiple_of(jnp.bitwise_xor(place_ref[0], m) * quarter, 32)
            outs[m][...] = total[pl.ds(begin, quarter), :].astype(bf16)

        def rows_of(place, which):
            begin = direct + (2 * place_ref[place] + which) * half
            return total[pl.ds(pl.multiple_of(begin, 16), half), :].astype(bf16)

        forth[:half] = rows_of(3, 0)
        forth[half:] = rows_of(2, 1)
        back[:half] = rows_of(1, 0)
        back[half:] = rows_of(3, 1)
        upper[...] = rows_of(2, 0)
        lower[...] = rows_of(1, 1)
        kept[:half] = rows_of(0, 0)
        kept[half:] = rows_of(0, 1)

    sizes = (quarter,) * 4 + (2 * half, 2 * half, half, half, 2 * half)
    outs = tuple(jax.ShapeDtypeStruct((size, width), bf16) for size in sizes)
    return kernel_call(body, outs, (places,), (*features, *through), (pltpu.VMEM((columns, width), f32),))


def pass_on(before, after, upper, lower):
    half, width = upper.shape

    def body(before_ref, after_ref, upper_ref, lower_ref, forth, back):
        forth[...] = (upper_ref[...].astype(f32) + before_ref[:half].astype(f32)).astype(bf16)
        back[...] = (lower_ref[...].astype(f32) + after_ref[half:].astype(f32)).astype(bf16)

    return kernel_call(body, (jax.ShapeDtypeStruct((half, width), bf16),) * 2, (), (before, after, upper, lower))


def sum_and_split(index, direct, ring):
    quarter, width = direct[0].shape
    half = ring[0].shape[0] // 2
    count = (quarter + 2 * half) // 4

    def body(index_ref, *refs):
        (own, before, after, upper, lower), outs, total = refs[4:9], refs[9:13], refs[13]
        a, b, c, d = (ref[...].astype(f32) for ref in refs[:4])
        total[:quarter] = (a + b) + (c + d)
        middle = quarter + half
        total[quarter:middle] = own[:half].astype(f32) + after[:half].astype(f32) + upper[...].astype(f32)
        total[middle:] = own[half:].astype(f32) + before[half:].astype(f32) + lower[...].astype(f32)
        for m in range(4):
            begin = pl.multiple_of(jnp.bitwise_xor(index_ref[0], m) * count, 8)
            outs[m][...] = total[pl.ds(begin, count), :].astype(bf16)

    outs = tuple(jax.ShapeDtypeStruct((count, width), bf16) for _ in range(4))
    return kernel_call(body, outs, (index,), (*direct, *ring), (pltpu.VMEM((quarter + 2 * half, width), f32),))


def join(index, pieces):
    count, width = pieces[0].shape
    sizes = [size // 4 for size, _ in STREAMS]

    def body(index_ref, *refs):
        ins, outs, rows = refs[:4], refs[4:6], refs[6]
        for m in range(4):
            begin = pl.multiple_of(jnp.bitwise_xor(index_ref[0], m) * count, 8)
            rows[pl.ds(begin, count), :] = ins[m][...].astype(f32)
        outs[0][...] = rows[: sizes[0]].astype(bf16)
        outs[1][...] = rows[sizes[0] :].astype(bf16)

    outs = tuple(jax.ShapeDtypeStruct((size, width), bf16) for size in sizes)
    return kernel_call(body, outs, (index,), pieces, (pltpu.VMEM((4 * count, width), f32),))


def exchange(pieces, axis):
    return [pieces[0]] + [swap(pieces[m], axis, m) for m in (1, 2, 3)]


def reduce_streams(pieces, beside):
    along_z = lax.axis_index("z").astype(jnp.int32)[None]
    forth, back, upper, lower, own = pieces[4:]
    axis = STREAMS[1][1]
    before, after = shift(forth, axis, 1), shift(back, axis, -1)
    direct = exchange(pieces[:4], STREAMS[0][1])
    forth, back = pass_on(before, after, upper, lower)
    ring = [own, before, after, shift(forth, axis, 1), shift(back, axis, -1)]
    pieces = exchange(sum_and_split(along_z, direct, ring), "z")
    total = total_of(pieces[0], pieces[1:])
    away, beside = lax.optimization_barrier((swap(total, ("x", "y"), 1), beside))
    total = (total.astype(f32) + away.astype(f32)).astype(bf16)
    total = (total.astype(f32) + swap(total, ("x", "y"), 3).astype(f32)).astype(bf16)
    kept = join(along_z, exchange([total] * 4, "z"))
    before, after = shift(kept[1], axis, 1), shift(kept[1], axis, -1)
    direct = exchange([kept[0]] * 4, STREAMS[0][1])
    half = before.shape[0] // 2
    ring = [kept[1], before, after, shift(before[:half], axis, 1), shift(after[half:], axis, -1)]
    direct, ring = lax.optimization_barrier((direct, ring))
    return [jnp.concatenate(direct, axis=0), jnp.concatenate(ring, axis=0)], beside


def write_rows(index_ref, streams, pieces, target, wide, sems):
    copies = []
    for stream, piece in zip(streams, pieces):
        first = stream * STREAMS[0][0]
        count = piece.shape[0] // 4
        for m in range(4):
            at = first + m * count
            wide[at : at + count] = piece[m * count : (m + 1) * count].astype(f32)
            place = index_ref[m] if stream else jnp.bitwise_xor(index_ref[0], m)
            begin = pl.multiple_of(first + place * count, 32)
            copy = pltpu.make_async_copy(
                wide.at[pl.ds(at, count)], target.at[pl.ds(begin, count)], sems.at[4 * stream + m]
            )
            copy.start()
            copies.append(copy)
    for copy in copies:
        copy.wait()


def assemble(index, tower, streams, pieces, rows, written=()):
    width = pieces[0].shape[1]
    shape = jax.ShapeDtypeStruct((rows, width), f32)
    hbm = pl.BlockSpec(memory_space=pltpu.HBM)
    number = len(pieces)

    def body(index_ref, tower_ref, *refs):
        out_img, out_txt, wide, sems = refs[number + len(written) :]

        @pl.when(tower_ref[0] == 0)
        def _():
            write_rows(index_ref, streams, refs[:number], out_img, wide, sems)

        @pl.when(tower_ref[0] != 0)
        def _():
            write_rows(index_ref, streams, refs[:number], out_txt, wide, sems)

    return pl.pallas_call(
        body,
        grid=(1,),
        out_shape=(shape, shape),
        in_specs=[pl.BlockSpec(memory_space=pltpu.SMEM)] * 2
        + [whole(piece.shape) for piece in pieces]
        + [hbm] * len(written),
        out_specs=(hbm, hbm),
        input_output_aliases={2 + number + k: k for k in range(len(written))},
        scratch_shapes=[pltpu.VMEM((rows, width), f32), pltpu.SemaphoreType.DMA((8,))],
        compiler_params=pltpu.CompilerParams(vmem_limit_bytes=40 * 2**20),
    )(index, tower, *pieces, *written)


def pair_kernel(number_ref, count_ref, own_ref, mates_ref, begin_ref, out_ref):
    scale, shift = number_ref[0], number_ref[1]
    mates = mates_ref[...]
    logits = lax.dot_general(own_ref[...], mates, TRANSPOSED, preferred_element_type=f32)
    logits = scale * logits + shift
    column = lax.broadcasted_iota(jnp.int32, logits.shape, 1) & 15
    row = lax.broadcasted_iota(jnp.int32, logits.shape, 0)
    keep = ((column & 7) + 1 < count_ref[0]) & ((column < 8) == (row < logits.shape[0] // 2))
    coef = jnp.where(keep, scale / (1.0 + jnp.exp(-logits)), 0.0).astype(bf16)
    part = jnp.dot(coef, mates, preferred_element_type=f32)

    @pl.when(pl.program_id(0) == 0)
    def _():
        out_ref[...] = begin_ref[...] + part

    @pl.when(pl.program_id(0) != 0)
    def _():
        out_ref[...] += part


def pair_stage(numbers, count, own, mates, begin):
    rows, width = own.shape
    per = 512

    return pl.pallas_call(
        pair_kernel,
        grid=(mates.shape[0] // per,),
        out_shape=jax.ShapeDtypeStruct((rows, width), f32),
        in_specs=[
            pl.BlockSpec(memory_space=pltpu.SMEM),
            pl.BlockSpec(memory_space=pltpu.SMEM),
            whole((rows, width)),
            pl.BlockSpec((per, width), lambda i: (i, 0)),
            whole((rows, width)),
        ],
        out_specs=whole((rows, width)),
        compiler_params=pltpu.CompilerParams(vmem_limit_bytes=60 * 2**20),
    )(numbers, count, own, mates, begin)


def finish_kernel(
    number_ref, count_ref, own_hbm, last_hbm, begin_hbm, inverse_ref, out_ref, mine_ref, other_ref, own, last, begin, sems
):
    copies = [
        pltpu.make_async_copy(source, target, sems.at[k])
        for k, (source, target) in enumerate(((own_hbm, own), (last_hbm, last), (begin_hbm, begin)))
    ]
    for copy in copies:
        copy.start()
    for copy in copies:
        copy.wait()
    scale, shift = number_ref[0], number_ref[1]
    rows = out_ref.shape[0] // 2
    for tower in range(2):
        part = slice(tower * rows, (tower + 1) * rows)
        mates = last[:, tower, :]
        logits = lax.dot_general(own[part], mates, TRANSPOSED, preferred_element_type=f32)
        logits = scale * logits + shift
        coef = jnp.where(count_ref[0] > 9, scale / (1.0 + jnp.exp(-logits)), 0.0).astype(bf16)
        upstream = begin[part] + jnp.dot(coef, mates, preferred_element_type=f32)
        unit = own[part].astype(f32)
        radial = jnp.sum(unit * upstream, axis=-1, keepdims=True)
        through = (inverse_ref[part] * (upstream - unit * radial)).astype(bf16)
        out_ref[part] = through

        @pl.when(count_ref[1] == tower)
        def _():
            mine_ref[...] = through

        @pl.when(count_ref[1] != tower)
        def _():
            other_ref[...] = through


def finish_stage(numbers, count, own, last, begin, inverse):
    smem = pl.BlockSpec(memory_space=pltpu.SMEM)
    hbm = pl.BlockSpec(memory_space=pltpu.HBM)
    return pl.pallas_call(
        finish_kernel,
        grid=(1,),
        out_shape=(
            jax.ShapeDtypeStruct(own.shape, bf16),
            jax.ShapeDtypeStruct((own.shape[0] // 2, own.shape[1]), bf16),
            jax.ShapeDtypeStruct((own.shape[0] // 2, own.shape[1]), bf16),
        ),
        in_specs=[smem, smem, hbm, hbm, hbm, whole(inverse.shape)],
        out_specs=(whole(own.shape),) + (whole((own.shape[0] // 2, own.shape[1])),) * 2,
        scratch_shapes=[pltpu.VMEM(a.shape, a.dtype) for a in (own, last, begin)] + [pltpu.SemaphoreType.DMA((3,))],
        compiler_params=pltpu.CompilerParams(vmem_limit_bytes=60 * 2**20),
    )(numbers, count, own, last, begin, inverse)


def stack_kernel(text_ref, image_ref, out_ref):
    out_ref[:, 0, :] = text_ref[...]
    out_ref[:, 1, :] = image_ref[...]


def stack_rows(text, image):
    rows, width = text.shape
    return pl.pallas_call(
        stack_kernel,
        grid=(1,),
        out_shape=jax.ShapeDtypeStruct((rows, 2, width), bf16),
        in_specs=[whole(text.shape)] * 2,
        out_specs=whole((rows, 2, width)),
        compiler_params=pltpu.CompilerParams(vmem_limit_bytes=60 * 2**20),
    )(text, image)


def select_kernel(
    pick_hbm, spread_hbm, text_hbm, image_hbm, send_hbm, unit_ref, pick, spread, text_weight, image_weight, send, sems
):
    rows = spread.shape[0]
    pairs = ((spread_hbm, spread), (text_hbm, text_weight), (image_hbm, image_weight), (pick_hbm, pick))
    loads = [pltpu.make_async_copy(source, target, sems.at[k]) for k, (source, target) in enumerate(pairs)]
    for load in loads:
        load.start()
    loads[0].wait()
    for tower, weight in ((0, text_weight), (1, image_weight)):
        loads[1 + tower].wait()
        product = jnp.dot(spread[:, tower, :], weight[...], preferred_element_type=f32)
        inverse = lax.rsqrt(jnp.sum(product * product, axis=-1, keepdims=True) + eps_norm)
        unit_ref[tower * rows : (tower + 1) * rows] = (product * inverse).astype(bf16)
    loads[3].wait()
    copies = []
    per = send.shape[0] // 4
    for k in range(4):
        part = pl.ds(k * per, per)
        send[part] = jnp.dot(pick[part], unit_ref[...], preferred_element_type=f32).astype(bf16)
        copy = pltpu.make_async_copy(send.at[part], send_hbm.at[part], sems.at[4 + k])
        copy.start()
        copies.append(copy)
    for copy in copies:
        copy.wait()


def select_stage(pick, spread, text_weight, image_weight):
    rows, _, width = spread.shape
    hbm = pl.BlockSpec(memory_space=pltpu.HBM)
    return pl.pallas_call(
        select_kernel,
        grid=(1,),
        out_shape=(
            jax.ShapeDtypeStruct((pick.shape[0], width), bf16),
            jax.ShapeDtypeStruct((2 * rows, width), bf16),
        ),
        in_specs=[hbm] * 4,
        out_specs=(hbm, whole((2 * rows, width))),
        scratch_shapes=[
            *(pltpu.VMEM(array.shape, bf16) for array in (pick, spread, text_weight, image_weight)),
            pltpu.VMEM((pick.shape[0], width), bf16),
            pltpu.SemaphoreType.DMA((8,)),
        ],
        compiler_params=pltpu.CompilerParams(vmem_limit_bytes=50 * 2**20),
    )(pick, spread, text_weight, image_weight)


def local(x_img, x_txt, w_img, w_txt, sharpness, offset, lists, counts, holder):
    devices = lax.axis_size(ALL)
    me = lax.axis_index(ALL)
    core = lax.axis_index("c")
    rows, width = x_img.shape
    slots = lists.shape[1]
    scale = sharpness[0]
    shift = offset[0]
    spread = lax.all_to_all(stack_rows(x_txt, x_img), ALL, 0, 0, tiled=True)
    z_txt, r_txt = project(x_txt, w_txt)
    z_img, r_img = project(x_img, w_img)

    numbers = jnp.arange(devices, dtype=jnp.int32)
    hot = holder[None, :] == numbers[:, None]
    source = jnp.sum(jnp.where(lists[:, :, None] == numbers, holder, 0), axis=2)
    table = jnp.dot(hot.astype(bf16), source.astype(bf16), preferred_element_type=f32).astype(jnp.int32)
    count = jnp.sum(jnp.where(hot[me], counts, 0))

    columns = jnp.arange(2 * devices, dtype=jnp.int32)
    near = jnp.concatenate([table[:, 1:9], table[:, 1:9] + devices], axis=1)
    last = jnp.concatenate([table[:, 9:], table[:, 9:] + devices], axis=1)
    pick = (near[:, :, None] == columns).astype(bf16).reshape(16 * devices, 2 * devices)
    pick_last = (last[:, :, None] == columns).astype(bf16).reshape(2 * devices, 2 * devices)
    send, units = select_stage(pick, spread, w_txt, w_img)
    send = send.reshape(devices, 16, width)
    send_last = jnp.dot(pick_last, units, preferred_element_type=f32).astype(bf16).reshape(devices, 2, width)
    mates = lax.all_to_all(send, ALL, 0, 0, tiled=True).reshape(16 * devices, width)
    mates, send_last = lax.optimization_barrier((mates, send_last))
    last = lax.all_to_all(send_last, ALL, 0, 0, tiled=True)

    x_mine = jnp.where(core == 0, x_img, x_txt)
    x_other = swap(jnp.where(core == 0, x_txt, x_img), "c", 1)

    own = jnp.concatenate([z_img, z_txt], axis=0)
    logits = scale * lax.dot_general(z_img, z_txt, TRANSPOSED, preferred_element_type=f32) + shift
    sign = jnp.where(jnp.eye(rows, dtype=bool), 1.0, -1.0)
    coef = (-scale * sign * jax.nn.sigmoid(-sign * logits)).astype(bf16)
    dz = jnp.concatenate(
        [
            jnp.dot(coef, z_txt, preferred_element_type=f32),
            lax.dot_general(coef, z_img, ROWS_FIRST, preferred_element_type=f32),
        ],
        axis=0,
    )
    inverse = jnp.concatenate([r_img, r_txt], axis=0)
    scalars = jnp.stack([scale, shift])
    dz = pair_stage(scalars, count[None], own, mates, dz)
    number = core[None].astype(jnp.int32)
    du, du_mine, du_away = finish_stage(
        scalars, jnp.concatenate([count[None], number]), own, last, dz, inverse
    )
    du_img = du[:rows]
    du_txt = du[rows:]
    du_other = swap(du_away, "c", 1)
    g_img = lax.dot_general(du_img, w_img, TRANSPOSED, preferred_element_type=f32).astype(bf16)
    g_txt = lax.dot_general(du_txt, w_txt, TRANSPOSED, preferred_element_type=f32).astype(bf16)

    factor = (64.0 / (devices * rows)) ** 0.5
    quarter = jnp.bitwise_xor(lax.axis_index("x"), lax.axis_index("y"))
    index = lax.axis_index(STREAMS[1][1])
    places = [jnp.bitwise_xor(jnp.bitwise_xor((index + step) & 3, index), quarter) for step in (0, 3, 1, 2)]
    places = jnp.stack(places).astype(jnp.int32)
    pieces = head_gradient(factor, places, (x_mine, x_other), (du_mine, du_other))
    pieces, (g_img, g_txt) = reduce_streams(pieces, (g_img, g_txt))
    written = assemble(places, number, (0, 1), pieces, width)
    away = [swap(piece, "c", 1) for piece in pieces]
    written = assemble(places, 1 - number, (1,), away[1:], width, written)
    head_img, head_txt = assemble(places, 1 - number, (0,), away[:1], width, written)
    return (g_img, g_txt, head_img, head_txt)


def solution(mesh):
    grid = Mesh(mesh.devices.reshape(4, 4, 4, 2), ALL)
    placed = (P(ALL, None), P(ALL, None), P(), P(), P(), P(), P(), P(), P())
    return jax.shard_map(
        local,
        mesh=grid,
        in_specs=placed,
        out_specs=(P(ALL, None), P(ALL, None), P(), P()),
        check_vma=False,
    )
```

```python
import jax
import jax.numpy as jnp
from jax import lax
from jax.experimental import pallas as pl
from jax.experimental.pallas import tpu as pltpu
from jax.sharding import Mesh, PartitionSpec as P

eps_norm = 1e-06
ALL = ("x", "z", "y", "c")
TRANSPOSED = (((1,), (1,)), ((), ()))
ROWS_FIRST = (((0,), (0,)), ((), ()))
SIDE = 4
STREAMS = (512, 640)
bf16 = jnp.bfloat16
f32 = jnp.float32


def project(features, weight):
    product = jnp.dot(features, weight, preferred_element_type=f32)
    inverse = lax.rsqrt(jnp.sum(product * product, axis=-1, keepdims=True) + eps_norm)
    return ((product * inverse).astype(bf16), inverse)


def permute(array, move):
    pairs = []
    for device in range(2 * SIDE**3):
        x, z, y, c = move(device // (2 * SIDE**2), device // (2 * SIDE) % SIDE, device // 2 % SIDE, device % 2)
        pairs.append((device, ((x * SIDE + z) * SIDE + y) * 2 + c))
    return lax.ppermute(array, ALL, pairs)


def swap_cores(array):
    return permute(array, lambda x, z, y, c: (x, z, y, 1 - c))


def send_large(array, stream, change):
    return permute(array, lambda x, z, y, c: (x, z, change(y), c) if c == stream else (change(x), z, y, c))


def send_small(array, core, mask):
    return permute(array, lambda x, z, y, c: (x, z ^ mask, y, c) if c == core else (x ^ mask, z, y ^ mask, c))


def shift(array, stream, step):
    return send_large(array, stream, lambda i: (i + step) % SIDE)


def total_of(own, got):
    total = (own.astype(f32) + got[0].astype(f32)) + (got[1].astype(f32) + got[2].astype(f32))
    return total.astype(bf16)


def whole(shape):
    return pl.BlockSpec(shape, lambda i: (0,) * len(shape))


def kernel_call(body, outs, scalars, arrays, scratch=()):
    return pl.pallas_call(
        body,
        grid=(1,),
        out_shape=outs,
        in_specs=[pl.BlockSpec(memory_space=pltpu.SMEM)] * len(scalars) + [whole(a.shape) for a in arrays],
        out_specs=tuple(whole(o.shape) for o in outs),
        scratch_shapes=scratch,
        compiler_params=pltpu.CompilerParams(vmem_limit_bytes=40 * 2**20),
    )(*scalars, *arrays)


def head_gradient(factor, places, features, through):
    rows, columns = features[0].shape
    width = through[0].shape[1]
    per = columns // 3
    direct = STREAMS[0]
    quarter, half = direct // 4, STREAMS[1] // 8

    def body(place_ref, xa, xb, da, db, *rest):
        outs, (forth, back, upper, lower, kept), total = rest[:4], rest[4:9], rest[9]
        for k in range(3):
            part = slice(k * per, (k + 1) * per)
            grad = lax.dot_general(xa[:, part], da[...], ROWS_FIRST, preferred_element_type=f32)
            grad += lax.dot_general(xb[:, part], db[...], ROWS_FIRST, preferred_element_type=f32)
            total[part] = grad * factor
        for m in range(4):
            begin = pl.multiple_of(jnp.bitwise_xor(place_ref[0], m) * quarter, 32)
            outs[m][...] = total[pl.ds(begin, quarter), :].astype(bf16)

        def rows_of(place, which):
            begin = direct + (2 * place_ref[place] + which) * half
            return total[pl.ds(pl.multiple_of(begin, 16), half), :].astype(bf16)

        forth[:half] = rows_of(3, 0)
        forth[half:] = rows_of(2, 1)
        back[:half] = rows_of(1, 0)
        back[half:] = rows_of(3, 1)
        upper[...] = rows_of(2, 0)
        lower[...] = rows_of(1, 1)
        kept[:half] = rows_of(0, 0)
        kept[half:] = rows_of(0, 1)

    sizes = (quarter,) * 4 + (2 * half, 2 * half, half, half, 2 * half)
    outs = tuple(jax.ShapeDtypeStruct((size, width), bf16) for size in sizes)
    return kernel_call(body, outs, (places,), (*features, *through), (pltpu.VMEM((columns, width), f32),))


def pass_on(before, after, upper, lower):
    half, width = upper.shape

    def body(before_ref, after_ref, upper_ref, lower_ref, forth, back):
        forth[...] = (upper_ref[...].astype(f32) + before_ref[:half].astype(f32)).astype(bf16)
        back[...] = (lower_ref[...].astype(f32) + after_ref[half:].astype(f32)).astype(bf16)

    return kernel_call(body, (jax.ShapeDtypeStruct((half, width), bf16),) * 2, (), (before, after, upper, lower))


def sum_and_split(index, direct, ring):
    quarter, width = direct[0].shape
    half = ring[0].shape[0] // 2
    count = (quarter + 2 * half) // 4

    def body(index_ref, *refs):
        (own, before, after, upper, lower), outs, total = refs[4:9], refs[9:13], refs[13]
        a, b, c, d = (ref[...].astype(f32) for ref in refs[:4])
        total[:quarter] = (a + b) + (c + d)
        middle = quarter + half
        total[quarter:middle] = own[:half].astype(f32) + after[:half].astype(f32) + upper[...].astype(f32)
        total[middle:] = own[half:].astype(f32) + before[half:].astype(f32) + lower[...].astype(f32)
        for m in range(4):
            begin = pl.multiple_of(jnp.bitwise_xor(index_ref[0], m) * count, 8)
            outs[m][...] = total[pl.ds(begin, count), :].astype(bf16)

    outs = tuple(jax.ShapeDtypeStruct((count, width), bf16) for _ in range(4))
    return kernel_call(body, outs, (index,), (*direct, *ring), (pltpu.VMEM((quarter + 2 * half, width), f32),))


def join(index, pieces):
    count, width = pieces[0].shape
    sizes = [size // 4 for size in STREAMS]

    def body(index_ref, *refs):
        ins, outs, rows = refs[:4], refs[4:6], refs[6]
        for m in range(4):
            begin = pl.multiple_of(jnp.bitwise_xor(index_ref[0], m) * count, 8)
            rows[pl.ds(begin, count), :] = ins[m][...].astype(f32)
        outs[0][...] = rows[: sizes[0]].astype(bf16)
        outs[1][...] = rows[sizes[0] :].astype(bf16)

    outs = tuple(jax.ShapeDtypeStruct((size, width), bf16) for size in sizes)
    return kernel_call(body, outs, (index,), pieces, (pltpu.VMEM((4 * count, width), f32),))


def exchange(pieces, core):
    return [pieces[0]] + [send_small(pieces[m], core, m) for m in (1, 2, 3)]


def exchange_stream(pieces, stream):
    return [pieces[0]] + [send_large(pieces[m], stream, lambda i, m=m: i ^ m) for m in (1, 2, 3)]


def reduce_streams(pieces, beside):
    index = jnp.where(lax.axis_index("c") == 0, lax.axis_index("z"), lax.axis_index("x")).astype(jnp.int32)[None]
    forth, back, upper, lower, own = pieces[4:]
    before, after = shift(forth, 1, 1), shift(back, 1, -1)
    direct = exchange_stream(pieces[:4], 0)
    forth, back = pass_on(before, after, upper, lower)
    ring = [own, before, after, shift(forth, 1, 1), shift(back, 1, -1)]
    pieces = exchange(sum_and_split(index, direct, ring), 0)
    total = total_of(pieces[0], pieces[1:])
    pieces, beside = lax.optimization_barrier((exchange([total] * 4, 1), beside))
    total = total_of(pieces[0], pieces[1:])
    kept = join(index, exchange([total] * 4, 0))
    pieces = lax.optimization_barrier([exchange_stream([quarter] * 4, k) for k, quarter in enumerate(kept)])
    out = []
    for four in pieces:
        joined = jnp.concatenate(four, axis=0)
        out += [joined, swap_cores(joined)]
    return out, beside


def write_half(index_ref, pieces, target, wide, sems):
    copies = []
    first = 0
    for stream in range(2):
        count = pieces[stream].shape[0] // 4
        for m in range(4):
            at = first + m * count
            wide[at : at + count] = pieces[stream][m * count : (m + 1) * count].astype(f32)
            begin = pl.multiple_of(first + jnp.bitwise_xor(index_ref[0], m) * count, 32)
            copy = pltpu.make_async_copy(
                wide.at[pl.ds(at, count)], target.at[pl.ds(begin, count)], sems.at[4 * stream + m]
            )
            copy.start()
            copies.append(copy)
        first += 4 * count
    for copy in copies:
        copy.wait()


def assemble(index, tower, pieces, rows, written=()):
    width = pieces[0].shape[1]
    shape = jax.ShapeDtypeStruct((rows, width), f32)
    hbm = pl.BlockSpec(memory_space=pltpu.HBM)

    def body(index_ref, tower_ref, *refs):
        out_img, out_txt, wide, sems = refs[2 + len(written) :]

        @pl.when(tower_ref[0] == 0)
        def _():
            write_half(index_ref, refs[:2], out_img, wide, sems)

        @pl.when(tower_ref[0] != 0)
        def _():
            write_half(index_ref, refs[:2], out_txt, wide, sems)

    return pl.pallas_call(
        body,
        grid=(1,),
        out_shape=(shape, shape),
        in_specs=[pl.BlockSpec(memory_space=pltpu.SMEM)] * 2
        + [whole(piece.shape) for piece in pieces]
        + [hbm] * len(written),
        out_specs=(hbm, hbm),
        input_output_aliases={4 + k: k for k in range(len(written))},
        scratch_shapes=[pltpu.VMEM((rows, width), f32), pltpu.SemaphoreType.DMA((8,))],
        compiler_params=pltpu.CompilerParams(vmem_limit_bytes=40 * 2**20),
    )(index, tower, *pieces, *written)


def pair_kernel(number_ref, count_ref, own_ref, mates_ref, begin_ref, out_ref):
    scale, shift = number_ref[0], number_ref[1]
    mates = mates_ref[...]
    logits = lax.dot_general(own_ref[...], mates, TRANSPOSED, preferred_element_type=f32)
    logits = scale * logits + shift
    column = lax.broadcasted_iota(jnp.int32, logits.shape, 1) & 15
    row = lax.broadcasted_iota(jnp.int32, logits.shape, 0)
    keep = ((column & 7) + 1 < count_ref[0]) & ((column < 8) == (row < logits.shape[0] // 2))
    coef = jnp.where(keep, scale / (1.0 + jnp.exp(-logits)), 0.0).astype(bf16)
    part = jnp.dot(coef, mates, preferred_element_type=f32)

    @pl.when(pl.program_id(0) == 0)
    def _():
        out_ref[...] = begin_ref[...] + part

    @pl.when(pl.program_id(0) != 0)
    def _():
        out_ref[...] += part


def pair_stage(numbers, count, own, mates, begin):
    rows, width = own.shape
    per = 512

    return pl.pallas_call(
        pair_kernel,
        grid=(mates.shape[0] // per,),
        out_shape=jax.ShapeDtypeStruct((rows, width), f32),
        in_specs=[
            pl.BlockSpec(memory_space=pltpu.SMEM),
            pl.BlockSpec(memory_space=pltpu.SMEM),
            whole((rows, width)),
            pl.BlockSpec((per, width), lambda i: (i, 0)),
            whole((rows, width)),
        ],
        out_specs=whole((rows, width)),
        compiler_params=pltpu.CompilerParams(vmem_limit_bytes=60 * 2**20),
    )(numbers, count, own, mates, begin)


def finish_kernel(
    number_ref, count_ref, own_hbm, last_hbm, begin_hbm, inverse_ref, out_ref, mine_ref, other_ref, own, last, begin, sems
):
    copies = [
        pltpu.make_async_copy(source, target, sems.at[k])
        for k, (source, target) in enumerate(((own_hbm, own), (last_hbm, last), (begin_hbm, begin)))
    ]
    for copy in copies:
        copy.start()
    for copy in copies:
        copy.wait()
    scale, shift = number_ref[0], number_ref[1]
    rows = out_ref.shape[0] // 2
    for tower in range(2):
        part = slice(tower * rows, (tower + 1) * rows)
        mates = last[:, tower, :]
        logits = lax.dot_general(own[part], mates, TRANSPOSED, preferred_element_type=f32)
        logits = scale * logits + shift
        coef = jnp.where(count_ref[0] > 9, scale / (1.0 + jnp.exp(-logits)), 0.0).astype(bf16)
        upstream = begin[part] + jnp.dot(coef, mates, preferred_element_type=f32)
        unit = own[part].astype(f32)
        radial = jnp.sum(unit * upstream, axis=-1, keepdims=True)
        through = (inverse_ref[part] * (upstream - unit * radial)).astype(bf16)
        out_ref[part] = through

        @pl.when(count_ref[1] == tower)
        def _():
            mine_ref[...] = through

        @pl.when(count_ref[1] != tower)
        def _():
            other_ref[...] = through


def finish_stage(numbers, count, own, last, begin, inverse):
    smem = pl.BlockSpec(memory_space=pltpu.SMEM)
    hbm = pl.BlockSpec(memory_space=pltpu.HBM)
    return pl.pallas_call(
        finish_kernel,
        grid=(1,),
        out_shape=(
            jax.ShapeDtypeStruct(own.shape, bf16),
            jax.ShapeDtypeStruct((own.shape[0] // 2, own.shape[1]), bf16),
            jax.ShapeDtypeStruct((own.shape[0] // 2, own.shape[1]), bf16),
        ),
        in_specs=[smem, smem, hbm, hbm, hbm, whole(inverse.shape)],
        out_specs=(whole(own.shape),) + (whole((own.shape[0] // 2, own.shape[1])),) * 2,
        scratch_shapes=[pltpu.VMEM(a.shape, a.dtype) for a in (own, last, begin)] + [pltpu.SemaphoreType.DMA((3,))],
        compiler_params=pltpu.CompilerParams(vmem_limit_bytes=60 * 2**20),
    )(numbers, count, own, last, begin, inverse)


def stack_kernel(text_ref, image_ref, out_ref):
    out_ref[:, 0, :] = text_ref[...]
    out_ref[:, 1, :] = image_ref[...]


def stack_rows(text, image):
    rows, width = text.shape
    return pl.pallas_call(
        stack_kernel,
        grid=(1,),
        out_shape=jax.ShapeDtypeStruct((rows, 2, width), bf16),
        in_specs=[whole(text.shape)] * 2,
        out_specs=whole((rows, 2, width)),
        compiler_params=pltpu.CompilerParams(vmem_limit_bytes=60 * 2**20),
    )(text, image)


def select_kernel(
    pick_hbm, spread_hbm, text_hbm, image_hbm, send_hbm, unit_ref, pick, spread, text_weight, image_weight, send, sems
):
    rows = spread.shape[0]
    pairs = ((spread_hbm, spread), (text_hbm, text_weight), (image_hbm, image_weight), (pick_hbm, pick))
    loads = [pltpu.make_async_copy(source, target, sems.at[k]) for k, (source, target) in enumerate(pairs)]
    for load in loads:
        load.start()
    loads[0].wait()
    for tower, weight in ((0, text_weight), (1, image_weight)):
        loads[1 + tower].wait()
        product = jnp.dot(spread[:, tower, :], weight[...], preferred_element_type=f32)
        inverse = lax.rsqrt(jnp.sum(product * product, axis=-1, keepdims=True) + eps_norm)
        unit_ref[tower * rows : (tower + 1) * rows] = (product * inverse).astype(bf16)
    loads[3].wait()
    copies = []
    per = send.shape[0] // 4
    for k in range(4):
        part = pl.ds(k * per, per)
        send[part] = jnp.dot(pick[part], unit_ref[...], preferred_element_type=f32).astype(bf16)
        copy = pltpu.make_async_copy(send.at[part], send_hbm.at[part], sems.at[4 + k])
        copy.start()
        copies.append(copy)
    for copy in copies:
        copy.wait()


def select_stage(pick, spread, text_weight, image_weight):
    rows, _, width = spread.shape
    hbm = pl.BlockSpec(memory_space=pltpu.HBM)
    return pl.pallas_call(
        select_kernel,
        grid=(1,),
        out_shape=(
            jax.ShapeDtypeStruct((pick.shape[0], width), bf16),
            jax.ShapeDtypeStruct((2 * rows, width), bf16),
        ),
        in_specs=[hbm] * 4,
        out_specs=(hbm, whole((2 * rows, width))),
        scratch_shapes=[
            *(pltpu.VMEM(array.shape, bf16) for array in (pick, spread, text_weight, image_weight)),
            pltpu.VMEM((pick.shape[0], width), bf16),
            pltpu.SemaphoreType.DMA((8,)),
        ],
        compiler_params=pltpu.CompilerParams(vmem_limit_bytes=50 * 2**20),
    )(pick, spread, text_weight, image_weight)


def local(x_img, x_txt, w_img, w_txt, sharpness, offset, lists, counts, holder):
    devices = lax.axis_size(ALL)
    me = lax.axis_index(ALL)
    core = lax.axis_index("c")
    rows, width = x_img.shape
    slots = lists.shape[1]
    scale = sharpness[0]
    shift = offset[0]
    spread = lax.all_to_all(stack_rows(x_txt, x_img), ALL, 0, 0, tiled=True)
    z_txt, r_txt = project(x_txt, w_txt)
    z_img, r_img = project(x_img, w_img)

    numbers = jnp.arange(devices, dtype=jnp.int32)
    hot = holder[None, :] == numbers[:, None]
    source = jnp.sum(jnp.where(lists[:, :, None] == numbers, holder, 0), axis=2)
    table = jnp.dot(hot.astype(bf16), source.astype(bf16), preferred_element_type=f32).astype(jnp.int32)
    count = jnp.sum(jnp.where(hot[me], counts, 0))

    columns = jnp.arange(2 * devices, dtype=jnp.int32)
    near = jnp.concatenate([table[:, 1:9], table[:, 1:9] + devices], axis=1)
    last = jnp.concatenate([table[:, 9:], table[:, 9:] + devices], axis=1)
    pick = (near[:, :, None] == columns).astype(bf16).reshape(16 * devices, 2 * devices)
    pick_last = (last[:, :, None] == columns).astype(bf16).reshape(2 * devices, 2 * devices)
    send, units = select_stage(pick, spread, w_txt, w_img)
    send = send.reshape(devices, 16, width)
    send_last = jnp.dot(pick_last, units, preferred_element_type=f32).astype(bf16).reshape(devices, 2, width)
    mates = lax.all_to_all(send, ALL, 0, 0, tiled=True).reshape(16 * devices, width)
    mates, send_last = lax.optimization_barrier((mates, send_last))
    last = lax.all_to_all(send_last, ALL, 0, 0, tiled=True)

    x_mine = jnp.where(core == 0, x_img, x_txt)
    x_other = swap_cores(jnp.where(core == 0, x_txt, x_img))

    own = jnp.concatenate([z_img, z_txt], axis=0)
    logits = scale * lax.dot_general(z_img, z_txt, TRANSPOSED, preferred_element_type=f32) + shift
    sign = jnp.where(jnp.eye(rows, dtype=bool), 1.0, -1.0)
    coef = (-scale * sign * jax.nn.sigmoid(-sign * logits)).astype(bf16)
    dz = jnp.concatenate(
        [
            jnp.dot(coef, z_txt, preferred_element_type=f32),
            lax.dot_general(coef, z_img, ROWS_FIRST, preferred_element_type=f32),
        ],
        axis=0,
    )
    inverse = jnp.concatenate([r_img, r_txt], axis=0)
    scalars = jnp.stack([scale, shift])
    dz = pair_stage(scalars, count[None], own, mates, dz)
    number = core[None].astype(jnp.int32)
    du, du_mine, du_away = finish_stage(
        scalars, jnp.concatenate([count[None], number]), own, last, dz, inverse
    )
    du_img = du[:rows]
    du_txt = du[rows:]
    du_other = swap_cores(du_away)
    g_img = lax.dot_general(du_img, w_img, TRANSPOSED, preferred_element_type=f32).astype(bf16)
    g_txt = lax.dot_general(du_txt, w_txt, TRANSPOSED, preferred_element_type=f32).astype(bf16)

    factor = (64.0 / (devices * rows)) ** 0.5
    quarter = jnp.bitwise_xor(lax.axis_index("x"), lax.axis_index("y"))
    index = jnp.where(core == 0, lax.axis_index("x"), lax.axis_index("y"))
    places = [jnp.bitwise_xor(jnp.bitwise_xor((index + step) & 3, index), quarter) for step in (0, 3, 1, 2)]
    places = jnp.stack(places).astype(jnp.int32)
    pieces = head_gradient(factor, places, (x_mine, x_other), (du_mine, du_other))
    pieces, (g_img, g_txt) = reduce_streams(pieces, (g_img, g_txt))
    written = assemble(places, number, pieces[::2], width)
    head_img, head_txt = assemble(places, 1 - number, pieces[1::2], width, written)
    return (g_img, g_txt, head_img, head_txt)


def solution(mesh):
    grid = Mesh(mesh.devices.reshape(4, 4, 4, 2), ALL)
    placed = (P(ALL, None), P(ALL, None), P(), P(), P(), P(), P(), P(), P())
    return jax.shard_map(
        local,
        mesh=grid,
        in_specs=placed,
        out_specs=(P(ALL, None), P(ALL, None), P(), P()),
        check_vma=False,
    )
```

```python
import jax
import jax.numpy as jnp
from jax import lax
from jax.experimental import pallas as pl
from jax.experimental.pallas import tpu as pltpu
from jax.sharding import Mesh, PartitionSpec as P

eps_norm = 1e-06
ALL = ("x", "z", "y", "c")
TRANSPOSED = (((1,), (1,)), ((), ()))
ROWS_FIRST = (((0,), (0,)), ((), ()))
STREAMS = ((512, "y"), (640, "x"))
bf16 = jnp.bfloat16
f32 = jnp.float32


def project(features, weight):
    product = jnp.dot(features, weight, preferred_element_type=f32)
    inverse = lax.rsqrt(jnp.sum(product * product, axis=-1, keepdims=True) + eps_norm)
    return ((product * inverse).astype(bf16), inverse)


def swap(array, axis, mask):
    if isinstance(axis, str):
        return lax.ppermute(array, axis, [(i, i ^ mask) for i in range(lax.axis_size(axis))])
    size = lax.axis_size(axis[1])
    pairs = [(i * size + j, (i ^ mask) * size + (j ^ mask)) for i in range(size) for j in range(size)]
    return lax.ppermute(array, axis, pairs)


def shift(array, axis, step):
    size = lax.axis_size(axis)
    return lax.ppermute(array, axis, [(i, (i + step) % size) for i in range(size)])


def total_of(own, got):
    total = (own.astype(f32) + got[0].astype(f32)) + (got[1].astype(f32) + got[2].astype(f32))
    return total.astype(bf16)


def whole(shape):
    return pl.BlockSpec(shape, lambda i: (0,) * len(shape))


def kernel_call(body, outs, scalars, arrays, scratch=()):
    return pl.pallas_call(
        body,
        grid=(1,),
        out_shape=outs,
        in_specs=[pl.BlockSpec(memory_space=pltpu.SMEM)] * len(scalars) + [whole(a.shape) for a in arrays],
        out_specs=tuple(whole(o.shape) for o in outs),
        scratch_shapes=scratch,
        compiler_params=pltpu.CompilerParams(vmem_limit_bytes=40 * 2**20),
    )(*scalars, *arrays)


def head_gradient(factor, places, features, through):
    rows, columns = features[0].shape
    width = through[0].shape[1]
    per = columns // 3
    direct = STREAMS[0][0]
    quarter, half = direct // 4, STREAMS[1][0] // 8

    def body(place_ref, xa, xb, da, db, *rest):
        outs, (forth, back, upper, lower, kept), total = rest[:4], rest[4:9], rest[9]
        for k in range(3):
            part = slice(k * per, (k + 1) * per)
            grad = lax.dot_general(xa[:, part], da[...], ROWS_FIRST, preferred_element_type=f32)
            grad += lax.dot_general(xb[:, part], db[...], ROWS_FIRST, preferred_element_type=f32)
            total[part] = grad * factor
        for m in range(4):
            begin = pl.multiple_of(jnp.bitwise_xor(place_ref[0], m) * quarter, 32)
            outs[m][...] = total[pl.ds(begin, quarter), :].astype(bf16)

        def rows_of(place, which):
            begin = direct + (2 * place_ref[place] + which) * half
            return total[pl.ds(pl.multiple_of(begin, 16), half), :].astype(bf16)

        forth[:half] = rows_of(3, 0)
        forth[half:] = rows_of(2, 1)
        back[:half] = rows_of(1, 0)
        back[half:] = rows_of(3, 1)
        upper[...] = rows_of(2, 0)
        lower[...] = rows_of(1, 1)
        kept[:half] = rows_of(0, 0)
        kept[half:] = rows_of(0, 1)

    sizes = (quarter,) * 4 + (2 * half, 2 * half, half, half, 2 * half)
    outs = tuple(jax.ShapeDtypeStruct((size, width), bf16) for size in sizes)
    return kernel_call(body, outs, (places,), (*features, *through), (pltpu.VMEM((columns, width), f32),))


def pass_on(before, after, upper, lower):
    half, width = upper.shape

    def body(before_ref, after_ref, upper_ref, lower_ref, forth, back):
        forth[...] = (upper_ref[...].astype(f32) + before_ref[:half].astype(f32)).astype(bf16)
        back[...] = (lower_ref[...].astype(f32) + after_ref[half:].astype(f32)).astype(bf16)

    return kernel_call(body, (jax.ShapeDtypeStruct((half, width), bf16),) * 2, (), (before, after, upper, lower))


def sum_and_split(index, direct, ring):
    quarter, width = direct[0].shape
    half = ring[0].shape[0] // 2
    count = (quarter + 2 * half) // 4

    def body(index_ref, *refs):
        (own, before, after, upper, lower), outs, total = refs[4:9], refs[9:13], refs[13]
        a, b, c, d = (ref[...].astype(f32) for ref in refs[:4])
        total[:quarter] = (a + b) + (c + d)
        middle = quarter + half
        total[quarter:middle] = own[:half].astype(f32) + after[:half].astype(f32) + upper[...].astype(f32)
        total[middle:] = own[half:].astype(f32) + before[half:].astype(f32) + lower[...].astype(f32)
        for m in range(4):
            begin = pl.multiple_of(jnp.bitwise_xor(index_ref[0], m) * count, 8)
            outs[m][...] = total[pl.ds(begin, count), :].astype(bf16)

    outs = tuple(jax.ShapeDtypeStruct((count, width), bf16) for _ in range(4))
    return kernel_call(body, outs, (index,), (*direct, *ring), (pltpu.VMEM((quarter + 2 * half, width), f32),))


def join(index, pieces):
    count, width = pieces[0].shape
    sizes = [size // 4 for size, _ in STREAMS]

    def body(index_ref, *refs):
        ins, outs, rows = refs[:4], refs[4:6], refs[6]
        for m in range(4):
            begin = pl.multiple_of(jnp.bitwise_xor(index_ref[0], m) * count, 8)
            rows[pl.ds(begin, count), :] = ins[m][...].astype(f32)
        outs[0][...] = rows[: sizes[0]].astype(bf16)
        outs[1][...] = rows[sizes[0] :].astype(bf16)

    outs = tuple(jax.ShapeDtypeStruct((size, width), bf16) for size in sizes)
    return kernel_call(body, outs, (index,), pieces, (pltpu.VMEM((4 * count, width), f32),))


def exchange(pieces, axis):
    return [pieces[0]] + [swap(pieces[m], axis, m) for m in (1, 2, 3)]


def exchange_streams(pieces):
    got = list(pieces)
    for m in (2, 1, 3):
        for stream, (_, axis) in enumerate(STREAMS):
            got[4 * stream + m] = swap(pieces[4 * stream + m], axis, m)
    return got


def reduce_streams(pieces, beside):
    along_z = lax.axis_index("z").astype(jnp.int32)[None]
    forth, back, upper, lower, own = pieces[4:]
    axis = STREAMS[1][1]
    before, after = shift(forth, axis, 1), shift(back, axis, -1)
    direct = exchange(pieces[:4], STREAMS[0][1])
    forth, back = pass_on(before, after, upper, lower)
    ring = [own, before, after, shift(forth, axis, 1), shift(back, axis, -1)]
    pieces = exchange(sum_and_split(along_z, direct, ring), "z")
    total = total_of(pieces[0], pieces[1:])
    pieces, beside = lax.optimization_barrier((exchange([total] * 4, ("x", "y")), beside))
    total = total_of(pieces[0], pieces[1:])
    kept = join(along_z, exchange([total] * 4, "z"))
    pieces = lax.optimization_barrier(exchange_streams([kept[0]] * 4 + [kept[1]] * 4))
    out = []
    for stream in range(2):
        joined = jnp.concatenate(pieces[4 * stream : 4 * stream + 4], axis=0)
        out += [joined, swap(joined, "c", 1)]
    return out, beside


def write_half(index_ref, pieces, target, wide, sems):
    copies = []
    first = 0
    for stream in range(2):
        count = pieces[stream].shape[0] // 4
        for m in range(4):
            at = first + m * count
            wide[at : at + count] = pieces[stream][m * count : (m + 1) * count].astype(f32)
            begin = pl.multiple_of(first + jnp.bitwise_xor(index_ref[0], m) * count, 32)
            copy = pltpu.make_async_copy(
                wide.at[pl.ds(at, count)], target.at[pl.ds(begin, count)], sems.at[4 * stream + m]
            )
            copy.start()
            copies.append(copy)
        first += 4 * count
    for copy in copies:
        copy.wait()


def assemble(index, tower, pieces, rows, written=()):
    width = pieces[0].shape[1]
    shape = jax.ShapeDtypeStruct((rows, width), f32)
    hbm = pl.BlockSpec(memory_space=pltpu.HBM)

    def body(index_ref, tower_ref, *refs):
        out_img, out_txt, wide, sems = refs[2 + len(written) :]

        @pl.when(tower_ref[0] == 0)
        def _():
            write_half(index_ref, refs[:2], out_img, wide, sems)

        @pl.when(tower_ref[0] != 0)
        def _():
            write_half(index_ref, refs[:2], out_txt, wide, sems)

    return pl.pallas_call(
        body,
        grid=(1,),
        out_shape=(shape, shape),
        in_specs=[pl.BlockSpec(memory_space=pltpu.SMEM)] * 2
        + [whole(piece.shape) for piece in pieces]
        + [hbm] * len(written),
        out_specs=(hbm, hbm),
        input_output_aliases={4 + k: k for k in range(len(written))},
        scratch_shapes=[pltpu.VMEM((rows, width), f32), pltpu.SemaphoreType.DMA((8,))],
        compiler_params=pltpu.CompilerParams(vmem_limit_bytes=40 * 2**20),
    )(index, tower, *pieces, *written)


def pair_kernel(number_ref, count_ref, own_ref, mates_ref, begin_ref, out_ref):
    scale, shift = number_ref[0], number_ref[1]
    mates = mates_ref[...]
    logits = lax.dot_general(own_ref[...], mates, TRANSPOSED, preferred_element_type=f32)
    logits = scale * logits + shift
    column = lax.broadcasted_iota(jnp.int32, logits.shape, 1) & 15
    row = lax.broadcasted_iota(jnp.int32, logits.shape, 0)
    keep = ((column & 7) + 1 < count_ref[0]) & ((column < 8) == (row < logits.shape[0] // 2))
    coef = jnp.where(keep, scale / (1.0 + jnp.exp(-logits)), 0.0).astype(bf16)
    part = jnp.dot(coef, mates, preferred_element_type=f32)

    @pl.when(pl.program_id(0) == 0)
    def _():
        out_ref[...] = begin_ref[...] + part

    @pl.when(pl.program_id(0) != 0)
    def _():
        out_ref[...] += part


def pair_stage(numbers, count, own, mates, begin):
    rows, width = own.shape
    per = 512

    return pl.pallas_call(
        pair_kernel,
        grid=(mates.shape[0] // per,),
        out_shape=jax.ShapeDtypeStruct((rows, width), f32),
        in_specs=[
            pl.BlockSpec(memory_space=pltpu.SMEM),
            pl.BlockSpec(memory_space=pltpu.SMEM),
            whole((rows, width)),
            pl.BlockSpec((per, width), lambda i: (i, 0)),
            whole((rows, width)),
        ],
        out_specs=whole((rows, width)),
        compiler_params=pltpu.CompilerParams(vmem_limit_bytes=63 * 2**20),
    )(numbers, count, own, mates, begin)


def finish_kernel(
    number_ref, count_ref, own_hbm, last_hbm, begin_hbm, inverse_ref, out_ref, mine_ref, other_ref, own, last, begin, sems
):
    copies = [
        pltpu.make_async_copy(source, target, sems.at[k])
        for k, (source, target) in enumerate(((own_hbm, own), (last_hbm, last), (begin_hbm, begin)))
    ]
    for copy in copies:
        copy.start()
    for copy in copies:
        copy.wait()
    scale, shift = number_ref[0], number_ref[1]
    rows = out_ref.shape[0] // 2
    for tower in range(2):
        part = slice(tower * rows, (tower + 1) * rows)
        mates = last[:, tower, :]
        logits = lax.dot_general(own[part], mates, TRANSPOSED, preferred_element_type=f32)
        logits = scale * logits + shift
        coef = jnp.where(count_ref[0] > 9, scale / (1.0 + jnp.exp(-logits)), 0.0).astype(bf16)
        upstream = begin[part] + jnp.dot(coef, mates, preferred_element_type=f32)
        unit = own[part].astype(f32)
        radial = jnp.sum(unit * upstream, axis=-1, keepdims=True)
        through = (inverse_ref[part] * (upstream - unit * radial)).astype(bf16)
        out_ref[part] = through

        @pl.when(count_ref[1] == tower)
        def _():
            mine_ref[...] = through

        @pl.when(count_ref[1] != tower)
        def _():
            other_ref[...] = through


def finish_stage(numbers, count, own, last, begin, inverse):
    smem = pl.BlockSpec(memory_space=pltpu.SMEM)
    hbm = pl.BlockSpec(memory_space=pltpu.HBM)
    return pl.pallas_call(
        finish_kernel,
        grid=(1,),
        out_shape=(
            jax.ShapeDtypeStruct(own.shape, bf16),
            jax.ShapeDtypeStruct((own.shape[0] // 2, own.shape[1]), bf16),
            jax.ShapeDtypeStruct((own.shape[0] // 2, own.shape[1]), bf16),
        ),
        in_specs=[smem, smem, hbm, hbm, hbm, whole(inverse.shape)],
        out_specs=(whole(own.shape),) + (whole((own.shape[0] // 2, own.shape[1])),) * 2,
        scratch_shapes=[pltpu.VMEM(a.shape, a.dtype) for a in (own, last, begin)] + [pltpu.SemaphoreType.DMA((3,))],
        compiler_params=pltpu.CompilerParams(vmem_limit_bytes=60 * 2**20),
    )(numbers, count, own, last, begin, inverse)


def stack_kernel(text_ref, image_ref, out_ref):
    out_ref[:, 0, :] = text_ref[...]
    out_ref[:, 1, :] = image_ref[...]


def stack_rows(text, image):
    rows, width = text.shape
    return pl.pallas_call(
        stack_kernel,
        grid=(1,),
        out_shape=jax.ShapeDtypeStruct((rows, 2, width), bf16),
        in_specs=[whole(text.shape)] * 2,
        out_specs=whole((rows, 2, width)),
        compiler_params=pltpu.CompilerParams(vmem_limit_bytes=60 * 2**20),
    )(text, image)


def select_kernel(
    pick_hbm, spread_hbm, text_hbm, image_hbm, send_hbm, unit_ref, pick, spread, text_weight, image_weight, send, sems
):
    rows = spread.shape[0]
    pairs = ((spread_hbm, spread), (text_hbm, text_weight), (image_hbm, image_weight), (pick_hbm, pick))
    loads = [pltpu.make_async_copy(source, target, sems.at[k]) for k, (source, target) in enumerate(pairs)]
    for load in loads:
        load.start()
    loads[0].wait()
    for tower, weight in ((0, text_weight), (1, image_weight)):
        loads[1 + tower].wait()
        product = jnp.dot(spread[:, tower, :], weight[...], preferred_element_type=f32)
        inverse = lax.rsqrt(jnp.sum(product * product, axis=-1, keepdims=True) + eps_norm)
        unit_ref[tower * rows : (tower + 1) * rows] = (product * inverse).astype(bf16)
    loads[3].wait()
    copies = []
    per = send.shape[0] // 4
    for k in range(4):
        part = pl.ds(k * per, per)
        send[part] = jnp.dot(pick[part], unit_ref[...], preferred_element_type=f32).astype(bf16)
        copy = pltpu.make_async_copy(send.at[part], send_hbm.at[part], sems.at[4 + k])
        copy.start()
        copies.append(copy)
    for copy in copies:
        copy.wait()


def select_stage(pick, spread, text_weight, image_weight):
    rows, _, width = spread.shape
    hbm = pl.BlockSpec(memory_space=pltpu.HBM)
    return pl.pallas_call(
        select_kernel,
        grid=(1,),
        out_shape=(
            jax.ShapeDtypeStruct((pick.shape[0], width), bf16),
            jax.ShapeDtypeStruct((2 * rows, width), bf16),
        ),
        in_specs=[hbm] * 4,
        out_specs=(hbm, whole((2 * rows, width))),
        scratch_shapes=[
            *(pltpu.VMEM(array.shape, bf16) for array in (pick, spread, text_weight, image_weight)),
            pltpu.VMEM((pick.shape[0], width), bf16),
            pltpu.SemaphoreType.DMA((8,)),
        ],
        compiler_params=pltpu.CompilerParams(vmem_limit_bytes=50 * 2**20),
    )(pick, spread, text_weight, image_weight)


def local(x_img, x_txt, w_img, w_txt, sharpness, offset, lists, counts, holder):
    devices = lax.axis_size(ALL)
    me = lax.axis_index(ALL)
    core = lax.axis_index("c")
    rows, width = x_img.shape
    slots = lists.shape[1]
    scale = sharpness[0]
    shift = offset[0]
    spread = lax.all_to_all(stack_rows(x_txt, x_img), ALL, 0, 0, tiled=True)
    z_txt, r_txt = project(x_txt, w_txt)
    z_img, r_img = project(x_img, w_img)

    numbers = jnp.arange(devices, dtype=jnp.int32)
    hot = holder[None, :] == numbers[:, None]
    source = jnp.sum(jnp.where(lists[:, :, None] == numbers, holder, 0), axis=2)
    table = jnp.dot(hot.astype(bf16), source.astype(bf16), preferred_element_type=f32).astype(jnp.int32)
    count = jnp.sum(jnp.where(hot[me], counts, 0))

    columns = jnp.arange(2 * devices, dtype=jnp.int32)
    near = jnp.concatenate([table[:, 1:9], table[:, 1:9] + devices], axis=1)
    last = jnp.concatenate([table[:, 9:], table[:, 9:] + devices], axis=1)
    pick = (near[:, :, None] == columns).astype(bf16).reshape(16 * devices, 2 * devices)
    pick_last = (last[:, :, None] == columns).astype(bf16).reshape(2 * devices, 2 * devices)
    send, units = select_stage(pick, spread, w_txt, w_img)
    send = send.reshape(devices, 16, width)
    send_last = jnp.dot(pick_last, units, preferred_element_type=f32).astype(bf16).reshape(devices, 2, width)
    mates = lax.all_to_all(send, ALL, 0, 0, tiled=True).reshape(16 * devices, width)
    mates, send_last = lax.optimization_barrier((mates, send_last))
    last = lax.all_to_all(send_last, ALL, 0, 0, tiled=True)

    x_mine = jnp.where(core == 0, x_img, x_txt)
    x_other = swap(jnp.where(core == 0, x_txt, x_img), "c", 1)

    own = jnp.concatenate([z_img, z_txt], axis=0)
    logits = scale * lax.dot_general(z_img, z_txt, TRANSPOSED, preferred_element_type=f32) + shift
    sign = jnp.where(jnp.eye(rows, dtype=bool), 1.0, -1.0)
    coef = (-scale * sign * jax.nn.sigmoid(-sign * logits)).astype(bf16)
    dz = jnp.concatenate(
        [
            jnp.dot(coef, z_txt, preferred_element_type=f32),
            lax.dot_general(coef, z_img, ROWS_FIRST, preferred_element_type=f32),
        ],
        axis=0,
    )
    inverse = jnp.concatenate([r_img, r_txt], axis=0)
    scalars = jnp.stack([scale, shift])
    dz = pair_stage(scalars, count[None], own, mates, dz)
    number = core[None].astype(jnp.int32)
    du, du_mine, du_away = finish_stage(
        scalars, jnp.concatenate([count[None], number]), own, last, dz, inverse
    )
    du_img = du[:rows]
    du_txt = du[rows:]
    du_other = swap(du_away, "c", 1)
    g_img = lax.dot_general(du_img, w_img, TRANSPOSED, preferred_element_type=f32).astype(bf16)
    g_txt = lax.dot_general(du_txt, w_txt, TRANSPOSED, preferred_element_type=f32).astype(bf16)

    factor = (64.0 / (devices * rows)) ** 0.5
    quarter = jnp.bitwise_xor(lax.axis_index("x"), lax.axis_index("y"))
    index = lax.axis_index(STREAMS[1][1])
    places = [jnp.bitwise_xor(jnp.bitwise_xor((index + step) & 3, index), quarter) for step in (0, 3, 1, 2)]
    places = jnp.stack(places).astype(jnp.int32)
    pieces = head_gradient(factor, places, (x_mine, x_other), (du_mine, du_other))
    pieces, (g_img, g_txt) = reduce_streams(pieces, (g_img, g_txt))
    written = assemble(places, number, pieces[::2], width)
    head_img, head_txt = assemble(places, 1 - number, pieces[1::2], width, written)
    return (g_img, g_txt, head_img, head_txt)


def solution(mesh):
    grid = Mesh(mesh.devices.reshape(4, 4, 4, 2), ALL)
    placed = (P(ALL, None), P(ALL, None), P(), P(), P(), P(), P(), P(), P())
    return jax.shard_map(
        local,
        mesh=grid,
        in_specs=placed,
        out_specs=(P(ALL, None), P(ALL, None), P(), P()),
        check_vma=False,
    )
```

```python
import jax
import jax.numpy as jnp
from jax import lax
from jax.experimental import pallas as pl
from jax.experimental.pallas import tpu as pltpu
from jax.sharding import Mesh, PartitionSpec as P

eps_norm = 1e-06
ALL = ("x", "z", "y", "c")
TRANSPOSED = (((1,), (1,)), ((), ()))
ROWS_FIRST = (((0,), (0,)), ((), ()))
STREAMS = ((512, "y"), (640, "x"))
bf16 = jnp.bfloat16
f32 = jnp.float32


def project(features, weight):
    product = jnp.dot(features, weight, preferred_element_type=f32)
    inverse = lax.rsqrt(jnp.sum(product * product, axis=-1, keepdims=True) + eps_norm)
    return ((product * inverse).astype(bf16), inverse)


def swap(array, axis, mask):
    if isinstance(axis, str):
        return lax.ppermute(array, axis, [(i, i ^ mask) for i in range(lax.axis_size(axis))])
    size = lax.axis_size(axis[1])
    pairs = [(i * size + j, (i ^ mask) * size + (j ^ mask)) for i in range(size) for j in range(size)]
    return lax.ppermute(array, axis, pairs)


def shift(array, axis, step):
    size = lax.axis_size(axis)
    return lax.ppermute(array, axis, [(i, (i + step) % size) for i in range(size)])


def total_of(own, got):
    total = (own.astype(f32) + got[0].astype(f32)) + (got[1].astype(f32) + got[2].astype(f32))
    return total.astype(bf16)


def whole(shape):
    return pl.BlockSpec(shape, lambda i: (0,) * len(shape))


def kernel_call(body, outs, scalars, arrays, scratch=()):
    return pl.pallas_call(
        body,
        grid=(1,),
        out_shape=outs,
        in_specs=[pl.BlockSpec(memory_space=pltpu.SMEM)] * len(scalars) + [whole(a.shape) for a in arrays],
        out_specs=tuple(whole(o.shape) for o in outs),
        scratch_shapes=scratch,
        compiler_params=pltpu.CompilerParams(vmem_limit_bytes=40 * 2**20),
    )(*scalars, *arrays)


def head_gradient(factor, places, features, through):
    rows, columns = features[0].shape
    width = through[0].shape[1]
    per = columns // 3
    direct = STREAMS[0][0]
    quarter, half = direct // 4, STREAMS[1][0] // 8

    def body(place_ref, xa, xb, da, db, *rest):
        outs, (forth, back, upper, lower, kept), total = rest[:4], rest[4:9], rest[9]
        for k in range(3):
            part = slice(k * per, (k + 1) * per)
            grad = lax.dot_general(xa[:, part], da[...], ROWS_FIRST, preferred_element_type=f32)
            grad += lax.dot_general(xb[:, part], db[...], ROWS_FIRST, preferred_element_type=f32)
            total[part] = grad * factor
        for m in range(4):
            begin = pl.multiple_of(jnp.bitwise_xor(place_ref[0], m) * quarter, 32)
            outs[m][...] = total[pl.ds(begin, quarter), :].astype(bf16)

        def rows_of(place, which):
            begin = direct + (2 * place_ref[place] + which) * half
            return total[pl.ds(pl.multiple_of(begin, 16), half), :].astype(bf16)

        forth[:half] = rows_of(3, 0)
        forth[half:] = rows_of(2, 1)
        back[:half] = rows_of(1, 0)
        back[half:] = rows_of(3, 1)
        upper[...] = rows_of(2, 0)
        lower[...] = rows_of(1, 1)
        kept[:half] = rows_of(0, 0)
        kept[half:] = rows_of(0, 1)

    sizes = (quarter,) * 4 + (2 * half, 2 * half, half, half, 2 * half)
    outs = tuple(jax.ShapeDtypeStruct((size, width), bf16) for size in sizes)
    return kernel_call(body, outs, (places,), (*features, *through), (pltpu.VMEM((columns, width), f32),))


def pass_on(before, after, upper, lower):
    half, width = upper.shape

    def body(before_ref, after_ref, upper_ref, lower_ref, forth, back):
        forth[...] = (upper_ref[...].astype(f32) + before_ref[:half].astype(f32)).astype(bf16)
        back[...] = (lower_ref[...].astype(f32) + after_ref[half:].astype(f32)).astype(bf16)

    return kernel_call(body, (jax.ShapeDtypeStruct((half, width), bf16),) * 2, (), (before, after, upper, lower))


def sum_and_split(index, direct, ring):
    quarter, width = direct[0].shape
    half = ring[0].shape[0] // 2
    count = (quarter + 2 * half) // 4

    def body(index_ref, *refs):
        (own, before, after, upper, lower), outs, total = refs[4:9], refs[9:13], refs[13]
        a, b, c, d = (ref[...].astype(f32) for ref in refs[:4])
        total[:quarter] = (a + b) + (c + d)
        middle = quarter + half
        total[quarter:middle] = own[:half].astype(f32) + after[:half].astype(f32) + upper[...].astype(f32)
        total[middle:] = own[half:].astype(f32) + before[half:].astype(f32) + lower[...].astype(f32)
        for m in range(4):
            begin = pl.multiple_of(jnp.bitwise_xor(index_ref[0], m) * count, 8)
            outs[m][...] = total[pl.ds(begin, count), :].astype(bf16)

    outs = tuple(jax.ShapeDtypeStruct((count, width), bf16) for _ in range(4))
    return kernel_call(body, outs, (index,), (*direct, *ring), (pltpu.VMEM((quarter + 2 * half, width), f32),))


def join(index, pieces):
    count, width = pieces[0].shape
    sizes = [2 * count, 2 * count]

    def body(index_ref, *refs):
        ins, outs, rows = refs[:4], refs[4:6], refs[6]
        for m in range(4):
            begin = pl.multiple_of(jnp.bitwise_xor(index_ref[0], m) * count, 8)
            rows[pl.ds(begin, count), :] = ins[m][...].astype(f32)
        outs[0][...] = rows[: sizes[0]].astype(bf16)
        outs[1][...] = rows[sizes[0] :].astype(bf16)

    outs = tuple(jax.ShapeDtypeStruct((size, width), bf16) for size in sizes)
    return kernel_call(body, outs, (index,), pieces, (pltpu.VMEM((4 * count, width), f32),))


def exchange(pieces, axis):
    return [pieces[0]] + [swap(pieces[m], axis, m) for m in (1, 2, 3)]


def exchange_streams(pieces):
    got = list(pieces)
    for m in (2, 1, 3):
        for stream, (_, axis) in enumerate(STREAMS):
            got[4 * stream + m] = swap(pieces[4 * stream + m], axis, m)
    return got


def reduce_streams(pieces, beside):
    along_z = lax.axis_index("z").astype(jnp.int32)[None]
    forth, back, upper, lower, own = pieces[4:]
    axis = STREAMS[1][1]
    before, after = shift(forth, axis, 1), shift(back, axis, -1)
    direct = exchange(pieces[:4], STREAMS[0][1])
    forth, back = pass_on(before, after, upper, lower)
    ring = [own, before, after, shift(forth, axis, 1), shift(back, axis, -1)]
    pieces = exchange(sum_and_split(along_z, direct, ring), "z")
    total = total_of(pieces[0], pieces[1:])
    pieces, beside = lax.optimization_barrier((exchange([total] * 4, ("x", "y")), beside))
    total = total_of(pieces[0], pieces[1:])
    kept = join(along_z, exchange([total] * 4, "z"))
    pieces = lax.optimization_barrier(exchange_streams([kept[0]] * 4 + [kept[1]] * 4))
    out = []
    for stream in range(2):
        joined = jnp.concatenate(pieces[4 * stream : 4 * stream + 4], axis=0)
        out += [joined, swap(joined, "c", 1)]
    return out, beside


def write_half(index_ref, pieces, target, wide, sems):
    direct, ring = STREAMS[0][0] // 4, STREAMS[1][0] // 4
    count = pieces[0].shape[0] // 4
    more = count - direct
    copies = []
    for m in range(4):
        place = jnp.bitwise_xor(index_ref[0], m)
        begin = 4 * direct + place * ring
        for half, skip, size, to in ((0, 0, direct, place * direct), (0, direct, more, begin), (1, 0, count, begin + more)):
            if skip == 0:
                wide[half, m] = pieces[half][m * count : (m + 1) * count].astype(f32)
            copy = pltpu.make_async_copy(
                wide.at[half, m, pl.ds(skip, size)],
                target.at[pl.ds(pl.multiple_of(to, 16), size)],
                sems.at[len(copies)],
            )
            copy.start()
            copies.append(copy)
    for copy in copies:
        copy.wait()


def assemble(index, tower, pieces, rows, written=()):
    width = pieces[0].shape[1]
    shape = jax.ShapeDtypeStruct((rows, width), f32)
    hbm = pl.BlockSpec(memory_space=pltpu.HBM)

    def body(index_ref, tower_ref, *refs):
        out_img, out_txt, wide, sems = refs[2 + len(written) :]

        @pl.when(tower_ref[0] == 0)
        def _():
            write_half(index_ref, refs[:2], out_img, wide, sems)

        @pl.when(tower_ref[0] != 0)
        def _():
            write_half(index_ref, refs[:2], out_txt, wide, sems)

    return pl.pallas_call(
        body,
        grid=(1,),
        out_shape=(shape, shape),
        in_specs=[pl.BlockSpec(memory_space=pltpu.SMEM)] * 2
        + [whole(piece.shape) for piece in pieces]
        + [hbm] * len(written),
        out_specs=(hbm, hbm),
        input_output_aliases={4 + k: k for k in range(len(written))},
        scratch_shapes=[pltpu.VMEM((2, 4, rows // 8, width), f32), pltpu.SemaphoreType.DMA((12,))],
        compiler_params=pltpu.CompilerParams(vmem_limit_bytes=40 * 2**20),
    )(index, tower, *pieces, *written)


def pair_kernel(number_ref, count_ref, own_ref, mates_ref, begin_ref, out_ref):
    scale, shift = number_ref[0], number_ref[1]
    mates = mates_ref[...]
    logits = lax.dot_general(own_ref[...], mates, TRANSPOSED, preferred_element_type=f32)
    logits = scale * logits + shift
    column = lax.broadcasted_iota(jnp.int32, logits.shape, 1) & 15
    row = lax.broadcasted_iota(jnp.int32, logits.shape, 0)
    keep = ((column & 7) + 1 < count_ref[0]) & ((column < 8) == (row < logits.shape[0] // 2))
    coef = jnp.where(keep, scale / (1.0 + jnp.exp(-logits)), 0.0).astype(bf16)
    part = jnp.dot(coef, mates, preferred_element_type=f32)

    @pl.when(pl.program_id(0) == 0)
    def _():
        out_ref[...] = begin_ref[...] + part

    @pl.when(pl.program_id(0) != 0)
    def _():
        out_ref[...] += part


def pair_stage(numbers, count, own, mates, begin):
    rows, width = own.shape
    per = 512

    return pl.pallas_call(
        pair_kernel,
        grid=(mates.shape[0] // per,),
        out_shape=jax.ShapeDtypeStruct((rows, width), f32),
        in_specs=[
            pl.BlockSpec(memory_space=pltpu.SMEM),
            pl.BlockSpec(memory_space=pltpu.SMEM),
            whole((rows, width)),
            pl.BlockSpec((per, width), lambda i: (i, 0)),
            whole((rows, width)),
        ],
        out_specs=whole((rows, width)),
        compiler_params=pltpu.CompilerParams(vmem_limit_bytes=63 * 2**20),
    )(numbers, count, own, mates, begin)


def finish_kernel(
    number_ref, count_ref, own_hbm, last_hbm, begin_hbm, inverse_ref, out_ref, mine_ref, other_ref, own, last, begin, sems
):
    copies = [
        pltpu.make_async_copy(source, target, sems.at[k])
        for k, (source, target) in enumerate(((own_hbm, own), (last_hbm, last), (begin_hbm, begin)))
    ]
    for copy in copies:
        copy.start()
    for copy in copies:
        copy.wait()
    scale, shift = number_ref[0], number_ref[1]
    rows = out_ref.shape[0] // 2
    for tower in range(2):
        part = slice(tower * rows, (tower + 1) * rows)
        mates = last[:, tower, :]
        logits = lax.dot_general(own[part], mates, TRANSPOSED, preferred_element_type=f32)
        logits = scale * logits + shift
        coef = jnp.where(count_ref[0] > 9, scale / (1.0 + jnp.exp(-logits)), 0.0).astype(bf16)
        upstream = begin[part] + jnp.dot(coef, mates, preferred_element_type=f32)
        unit = own[part].astype(f32)
        radial = jnp.sum(unit * upstream, axis=-1, keepdims=True)
        through = (inverse_ref[part] * (upstream - unit * radial)).astype(bf16)
        out_ref[part] = through

        @pl.when(count_ref[1] == tower)
        def _():
            mine_ref[...] = through

        @pl.when(count_ref[1] != tower)
        def _():
            other_ref[...] = through


def finish_stage(numbers, count, own, last, begin, inverse):
    smem = pl.BlockSpec(memory_space=pltpu.SMEM)
    hbm = pl.BlockSpec(memory_space=pltpu.HBM)
    return pl.pallas_call(
        finish_kernel,
        grid=(1,),
        out_shape=(
            jax.ShapeDtypeStruct(own.shape, bf16),
            jax.ShapeDtypeStruct((own.shape[0] // 2, own.shape[1]), bf16),
            jax.ShapeDtypeStruct((own.shape[0] // 2, own.shape[1]), bf16),
        ),
        in_specs=[smem, smem, hbm, hbm, hbm, whole(inverse.shape)],
        out_specs=(whole(own.shape),) + (whole((own.shape[0] // 2, own.shape[1])),) * 2,
        scratch_shapes=[pltpu.VMEM(a.shape, a.dtype) for a in (own, last, begin)] + [pltpu.SemaphoreType.DMA((3,))],
        compiler_params=pltpu.CompilerParams(vmem_limit_bytes=60 * 2**20),
    )(numbers, count, own, last, begin, inverse)


def stack_kernel(text_ref, image_ref, out_ref):
    out_ref[:, 0, :] = text_ref[...]
    out_ref[:, 1, :] = image_ref[...]


def stack_rows(text, image):
    rows, width = text.shape
    return pl.pallas_call(
        stack_kernel,
        grid=(1,),
        out_shape=jax.ShapeDtypeStruct((rows, 2, width), bf16),
        in_specs=[whole(text.shape)] * 2,
        out_specs=whole((rows, 2, width)),
        compiler_params=pltpu.CompilerParams(vmem_limit_bytes=60 * 2**20),
    )(text, image)


def select_kernel(
    pick_hbm, spread_hbm, text_hbm, image_hbm, send_hbm, unit_ref, pick, spread, text_weight, image_weight, send, sems
):
    rows = spread.shape[0]
    pairs = ((spread_hbm, spread), (text_hbm, text_weight), (image_hbm, image_weight), (pick_hbm, pick))
    loads = [pltpu.make_async_copy(source, target, sems.at[k]) for k, (source, target) in enumerate(pairs)]
    for load in loads:
        load.start()
    loads[0].wait()
    for tower, weight in ((0, text_weight), (1, image_weight)):
        loads[1 + tower].wait()
        product = jnp.dot(spread[:, tower, :], weight[...], preferred_element_type=f32)
        inverse = lax.rsqrt(jnp.sum(product * product, axis=-1, keepdims=True) + eps_norm)
        unit_ref[tower * rows : (tower + 1) * rows] = (product * inverse).astype(bf16)
    loads[3].wait()
    copies = []
    per = send.shape[0] // 4
    for k in range(4):
        part = pl.ds(k * per, per)
        send[part] = jnp.dot(pick[part], unit_ref[...], preferred_element_type=f32).astype(bf16)
        copy = pltpu.make_async_copy(send.at[part], send_hbm.at[part], sems.at[4 + k])
        copy.start()
        copies.append(copy)
    for copy in copies:
        copy.wait()


def select_stage(pick, spread, text_weight, image_weight):
    rows, _, width = spread.shape
    hbm = pl.BlockSpec(memory_space=pltpu.HBM)
    return pl.pallas_call(
        select_kernel,
        grid=(1,),
        out_shape=(
            jax.ShapeDtypeStruct((pick.shape[0], width), bf16),
            jax.ShapeDtypeStruct((2 * rows, width), bf16),
        ),
        in_specs=[hbm] * 4,
        out_specs=(hbm, whole((2 * rows, width))),
        scratch_shapes=[
            *(pltpu.VMEM(array.shape, bf16) for array in (pick, spread, text_weight, image_weight)),
            pltpu.VMEM((pick.shape[0], width), bf16),
            pltpu.SemaphoreType.DMA((8,)),
        ],
        compiler_params=pltpu.CompilerParams(vmem_limit_bytes=50 * 2**20),
    )(pick, spread, text_weight, image_weight)


def local(x_img, x_txt, w_img, w_txt, sharpness, offset, lists, counts, holder):
    devices = lax.axis_size(ALL)
    me = lax.axis_index(ALL)
    core = lax.axis_index("c")
    rows, width = x_img.shape
    slots = lists.shape[1]
    scale = sharpness[0]
    shift = offset[0]
    spread = lax.all_to_all(stack_rows(x_txt, x_img), ALL, 0, 0, tiled=True)
    z_txt, r_txt = project(x_txt, w_txt)
    z_img, r_img = project(x_img, w_img)

    numbers = jnp.arange(devices, dtype=jnp.int32)
    hot = holder[None, :] == numbers[:, None]
    source = jnp.sum(jnp.where(lists[:, :, None] == numbers, holder, 0), axis=2)
    table = jnp.dot(hot.astype(bf16), source.astype(bf16), preferred_element_type=f32).astype(jnp.int32)
    count = jnp.sum(jnp.where(hot[me], counts, 0))

    columns = jnp.arange(2 * devices, dtype=jnp.int32)
    near = jnp.concatenate([table[:, 1:9], table[:, 1:9] + devices], axis=1)
    last = jnp.concatenate([table[:, 9:], table[:, 9:] + devices], axis=1)
    pick = (near[:, :, None] == columns).astype(bf16).reshape(16 * devices, 2 * devices)
    pick_last = (last[:, :, None] == columns).astype(bf16).reshape(2 * devices, 2 * devices)
    send, units = select_stage(pick, spread, w_txt, w_img)
    send = send.reshape(devices, 16, width)
    send_last = jnp.dot(pick_last, units, preferred_element_type=f32).astype(bf16).reshape(devices, 2, width)
    mates = lax.all_to_all(send, ALL, 0, 0, tiled=True).reshape(16 * devices, width)
    mates, send_last = lax.optimization_barrier((mates, send_last))
    last = lax.all_to_all(send_last, ALL, 0, 0, tiled=True)

    x_mine = jnp.where(core == 0, x_img, x_txt)
    x_other = swap(jnp.where(core == 0, x_txt, x_img), "c", 1)

    own = jnp.concatenate([z_img, z_txt], axis=0)
    logits = scale * lax.dot_general(z_img, z_txt, TRANSPOSED, preferred_element_type=f32) + shift
    sign = jnp.where(jnp.eye(rows, dtype=bool), 1.0, -1.0)
    coef = (-scale * sign * jax.nn.sigmoid(-sign * logits)).astype(bf16)
    dz = jnp.concatenate(
        [
            jnp.dot(coef, z_txt, preferred_element_type=f32),
            lax.dot_general(coef, z_img, ROWS_FIRST, preferred_element_type=f32),
        ],
        axis=0,
    )
    inverse = jnp.concatenate([r_img, r_txt], axis=0)
    scalars = jnp.stack([scale, shift])
    dz = pair_stage(scalars, count[None], own, mates, dz)
    number = core[None].astype(jnp.int32)
    du, du_mine, du_away = finish_stage(
        scalars, jnp.concatenate([count[None], number]), own, last, dz, inverse
    )
    du_img = du[:rows]
    du_txt = du[rows:]
    du_other = swap(du_away, "c", 1)
    g_img = lax.dot_general(du_img, w_img, TRANSPOSED, preferred_element_type=f32).astype(bf16)
    g_txt = lax.dot_general(du_txt, w_txt, TRANSPOSED, preferred_element_type=f32).astype(bf16)

    factor = (64.0 / (devices * rows)) ** 0.5
    quarter = jnp.bitwise_xor(lax.axis_index("x"), lax.axis_index("y"))
    index = lax.axis_index(STREAMS[1][1])
    places = [jnp.bitwise_xor(jnp.bitwise_xor((index + step) & 3, index), quarter) for step in (0, 3, 1, 2)]
    places = jnp.stack(places).astype(jnp.int32)
    pieces = head_gradient(factor, places, (x_mine, x_other), (du_mine, du_other))
    pieces, (g_img, g_txt) = reduce_streams(pieces, (g_img, g_txt))
    written = assemble(places, number, pieces[::2], width)
    head_img, head_txt = assemble(places, 1 - number, pieces[1::2], width, written)
    return (g_img, g_txt, head_img, head_txt)


def solution(mesh):
    grid = Mesh(mesh.devices.reshape(4, 4, 4, 2), ALL)
    placed = (P(ALL, None), P(ALL, None), P(), P(), P(), P(), P(), P(), P())
    return jax.shard_map(
        local,
        mesh=grid,
        in_specs=placed,
        out_specs=(P(ALL, None), P(ALL, None), P(), P()),
        check_vma=False,
    )
```

```python
import jax
import jax.numpy as jnp
from jax import lax
from jax.experimental import pallas as pl
from jax.experimental.pallas import tpu as pltpu
from jax.sharding import Mesh, PartitionSpec as P

eps_norm = 1e-06
ALL = ("x", "z", "y", "c")
TRANSPOSED = (((1,), (1,)), ((), ()))
ROWS_FIRST = (((0,), (0,)), ((), ()))
STREAMS = ((640, "y"), (512, "x"))
bf16 = jnp.bfloat16
f32 = jnp.float32


def project(features, weight):
    product = jnp.dot(features, weight, preferred_element_type=f32)
    inverse = lax.rsqrt(jnp.sum(product * product, axis=-1, keepdims=True) + eps_norm)
    return ((product * inverse).astype(bf16), inverse)


def swap(array, axis, mask):
    if isinstance(axis, str):
        return lax.ppermute(array, axis, [(i, i ^ mask) for i in range(lax.axis_size(axis))])
    size = lax.axis_size(axis[1])
    pairs = [(i * size + j, (i ^ mask) * size + (j ^ mask)) for i in range(size) for j in range(size)]
    return lax.ppermute(array, axis, pairs)


def shift(array, axis, step):
    size = lax.axis_size(axis)
    return lax.ppermute(array, axis, [(i, (i + step) % size) for i in range(size)])


def total_of(own, got):
    total = (own.astype(f32) + got[0].astype(f32)) + (got[1].astype(f32) + got[2].astype(f32))
    return total.astype(bf16)


def whole(shape):
    return pl.BlockSpec(shape, lambda i: (0,) * len(shape))


def kernel_call(body, outs, scalars, arrays, scratch=()):
    return pl.pallas_call(
        body,
        grid=(1,),
        out_shape=outs,
        in_specs=[pl.BlockSpec(memory_space=pltpu.SMEM)] * len(scalars) + [whole(a.shape) for a in arrays],
        out_specs=tuple(whole(o.shape) for o in outs),
        scratch_shapes=scratch,
        compiler_params=pltpu.CompilerParams(vmem_limit_bytes=40 * 2**20),
    )(*scalars, *arrays)


def head_gradient(factor, places, features, through):
    rows, columns = features[0].shape
    width = through[0].shape[1]
    per = columns // 3
    direct = STREAMS[0][0]
    quarter, half = direct // 4, STREAMS[1][0] // 8

    def body(place_ref, xa, xb, da, db, *rest):
        outs, (forth, back, upper, lower, kept), total = rest[:4], rest[4:9], rest[9]
        for k in range(3):
            part = slice(k * per, (k + 1) * per)
            grad = lax.dot_general(xa[:, part], da[...], ROWS_FIRST, preferred_element_type=f32)
            grad += lax.dot_general(xb[:, part], db[...], ROWS_FIRST, preferred_element_type=f32)
            total[part] = grad * factor
        for m in range(4):
            begin = pl.multiple_of(jnp.bitwise_xor(place_ref[0], m) * quarter, 32)
            outs[m][...] = total[pl.ds(begin, quarter), :].astype(bf16)

        def rows_of(place, which):
            begin = direct + (2 * place_ref[place] + which) * half
            return total[pl.ds(pl.multiple_of(begin, 16), half), :].astype(bf16)

        forth[:half] = rows_of(3, 0)
        forth[half:] = rows_of(2, 1)
        back[:half] = rows_of(1, 0)
        back[half:] = rows_of(3, 1)
        upper[...] = rows_of(2, 0)
        lower[...] = rows_of(1, 1)
        kept[:half] = rows_of(0, 0)
        kept[half:] = rows_of(0, 1)

    sizes = (quarter,) * 4 + (2 * half, 2 * half, half, half, 2 * half)
    outs = tuple(jax.ShapeDtypeStruct((size, width), bf16) for size in sizes)
    return kernel_call(body, outs, (places,), (*features, *through), (pltpu.VMEM((columns, width), f32),))


def pass_on(before, after, upper, lower):
    half, width = upper.shape

    def body(before_ref, after_ref, upper_ref, lower_ref, forth, back):
        forth[...] = (upper_ref[...].astype(f32) + before_ref[:half].astype(f32)).astype(bf16)
        back[...] = (lower_ref[...].astype(f32) + after_ref[half:].astype(f32)).astype(bf16)

    return kernel_call(body, (jax.ShapeDtypeStruct((half, width), bf16),) * 2, (), (before, after, upper, lower))


def sum_and_split(index, direct, ring):
    quarter, width = direct[0].shape
    half = ring[0].shape[0] // 2
    count = (quarter + 2 * half) // 4

    def body(index_ref, *refs):
        (own, before, after, upper, lower), outs, total = refs[4:9], refs[9:13], refs[13]
        a, b, c, d = (ref[...].astype(f32) for ref in refs[:4])
        total[:quarter] = (a + b) + (c + d)
        middle = quarter + half
        total[quarter:middle] = own[:half].astype(f32) + after[:half].astype(f32) + upper[...].astype(f32)
        total[middle:] = own[half:].astype(f32) + before[half:].astype(f32) + lower[...].astype(f32)
        for m in range(4):
            begin = pl.multiple_of(jnp.bitwise_xor(index_ref[0], m) * count, 8)
            outs[m][...] = total[pl.ds(begin, count), :].astype(bf16)

    outs = tuple(jax.ShapeDtypeStruct((count, width), bf16) for _ in range(4))
    return kernel_call(body, outs, (index,), (*direct, *ring), (pltpu.VMEM((quarter + 2 * half, width), f32),))


def join(index, pieces):
    count, width = pieces[0].shape
    sizes = [size // 4 for size, _ in STREAMS]

    def body(index_ref, *refs):
        ins, outs, rows = refs[:4], refs[4:6], refs[6]
        for m in range(4):
            begin = pl.multiple_of(jnp.bitwise_xor(index_ref[0], m) * count, 8)
            rows[pl.ds(begin, count), :] = ins[m][...].astype(f32)
        outs[0][...] = rows[: sizes[0]].astype(bf16)
        outs[1][...] = rows[sizes[0] :].astype(bf16)

    outs = tuple(jax.ShapeDtypeStruct((size, width), bf16) for size in sizes)
    return kernel_call(body, outs, (index,), pieces, (pltpu.VMEM((4 * count, width), f32),))


def exchange(pieces, axis):
    return [pieces[0]] + [swap(pieces[m], axis, m) for m in (1, 2, 3)]


def exchange_streams(pieces):
    got = list(pieces)
    for m in (2, 1, 3):
        for stream, (_, axis) in enumerate(STREAMS):
            got[4 * stream + m] = swap(pieces[4 * stream + m], axis, m)
    return got


def reduce_streams(pieces, beside):
    along_z = lax.axis_index("z").astype(jnp.int32)[None]
    forth, back, upper, lower, own = pieces[4:]
    axis = STREAMS[1][1]
    before, after = shift(forth, axis, 1), shift(back, axis, -1)
    direct = exchange(pieces[:4], STREAMS[0][1])
    forth, back = pass_on(before, after, upper, lower)
    ring = [own, before, after, shift(forth, axis, 1), shift(back, axis, -1)]
    pieces = exchange(sum_and_split(along_z, direct, ring), "z")
    total = total_of(pieces[0], pieces[1:])
    pieces, beside = lax.optimization_barrier((exchange([total] * 4, ("x", "y")), beside))
    total = total_of(pieces[0], pieces[1:])
    kept = join(along_z, exchange([total] * 4, "z"))
    pieces = lax.optimization_barrier(exchange_streams([kept[0]] * 4 + [kept[1]] * 4))
    out = []
    for stream in range(2):
        joined = jnp.concatenate(pieces[4 * stream : 4 * stream + 4], axis=0)
        out += [joined, swap(joined, "c", 1)]
    return out, beside


def write_half(index_ref, pieces, target, wide, sems):
    copies = []
    first = 0
    for stream in range(2):
        count = pieces[stream].shape[0] // 4
        for m in range(4):
            at = first + m * count
            wide[at : at + count] = pieces[stream][m * count : (m + 1) * count].astype(f32)
            begin = pl.multiple_of(first + jnp.bitwise_xor(index_ref[0], m) * count, 32)
            copy = pltpu.make_async_copy(
                wide.at[pl.ds(at, count)], target.at[pl.ds(begin, count)], sems.at[4 * stream + m]
            )
            copy.start()
            copies.append(copy)
        first += 4 * count
    for copy in copies:
        copy.wait()


def assemble(index, tower, pieces, rows, written=()):
    width = pieces[0].shape[1]
    shape = jax.ShapeDtypeStruct((rows, width), f32)
    hbm = pl.BlockSpec(memory_space=pltpu.HBM)

    def body(index_ref, tower_ref, *refs):
        out_img, out_txt, wide, sems = refs[2 + len(written) :]

        @pl.when(tower_ref[0] == 0)
        def _():
            write_half(index_ref, refs[:2], out_img, wide, sems)

        @pl.when(tower_ref[0] != 0)
        def _():
            write_half(index_ref, refs[:2], out_txt, wide, sems)

    return pl.pallas_call(
        body,
        grid=(1,),
        out_shape=(shape, shape),
        in_specs=[pl.BlockSpec(memory_space=pltpu.SMEM)] * 2
        + [whole(piece.shape) for piece in pieces]
        + [hbm] * len(written),
        out_specs=(hbm, hbm),
        input_output_aliases={4 + k: k for k in range(len(written))},
        scratch_shapes=[pltpu.VMEM((rows, width), f32), pltpu.SemaphoreType.DMA((8,))],
        compiler_params=pltpu.CompilerParams(vmem_limit_bytes=40 * 2**20),
    )(index, tower, *pieces, *written)


def pair_kernel(number_ref, count_ref, own_ref, mates_ref, begin_ref, out_ref):
    scale, shift = number_ref[0], number_ref[1]
    mates = mates_ref[...]
    logits = lax.dot_general(own_ref[...], mates, TRANSPOSED, preferred_element_type=f32)
    logits = scale * logits + shift
    column = lax.broadcasted_iota(jnp.int32, logits.shape, 1) & 15
    row = lax.broadcasted_iota(jnp.int32, logits.shape, 0)
    keep = ((column & 7) + 1 < count_ref[0]) & ((column < 8) == (row < logits.shape[0] // 2))
    coef = jnp.where(keep, scale / (1.0 + jnp.exp(-logits)), 0.0).astype(bf16)
    part = jnp.dot(coef, mates, preferred_element_type=f32)

    @pl.when(pl.program_id(0) == 0)
    def _():
        out_ref[...] = begin_ref[...] + part

    @pl.when(pl.program_id(0) != 0)
    def _():
        out_ref[...] += part


def pair_stage(numbers, count, own, mates, begin):
    rows, width = own.shape
    per = 512

    return pl.pallas_call(
        pair_kernel,
        grid=(mates.shape[0] // per,),
        out_shape=jax.ShapeDtypeStruct((rows, width), f32),
        in_specs=[
            pl.BlockSpec(memory_space=pltpu.SMEM),
            pl.BlockSpec(memory_space=pltpu.SMEM),
            whole((rows, width)),
            pl.BlockSpec((per, width), lambda i: (i, 0)),
            whole((rows, width)),
        ],
        out_specs=whole((rows, width)),
        compiler_params=pltpu.CompilerParams(vmem_limit_bytes=63 * 2**20),
    )(numbers, count, own, mates, begin)


def finish_kernel(
    number_ref, count_ref, own_hbm, last_hbm, begin_hbm, inverse_ref, out_ref, mine_ref, other_ref, own, last, begin, sems
):
    copies = [
        pltpu.make_async_copy(source, target, sems.at[k])
        for k, (source, target) in enumerate(((own_hbm, own), (last_hbm, last), (begin_hbm, begin)))
    ]
    for copy in copies:
        copy.start()
    for copy in copies:
        copy.wait()
    scale, shift = number_ref[0], number_ref[1]
    rows = out_ref.shape[0] // 2
    for tower in range(2):
        part = slice(tower * rows, (tower + 1) * rows)
        mates = last[:, tower, :]
        logits = lax.dot_general(own[part], mates, TRANSPOSED, preferred_element_type=f32)
        logits = scale * logits + shift
        coef = jnp.where(count_ref[0] > 9, scale / (1.0 + jnp.exp(-logits)), 0.0).astype(bf16)
        upstream = begin[part] + jnp.dot(coef, mates, preferred_element_type=f32)
        unit = own[part].astype(f32)
        radial = jnp.sum(unit * upstream, axis=-1, keepdims=True)
        through = (inverse_ref[part] * (upstream - unit * radial)).astype(bf16)
        out_ref[part] = through

        @pl.when(count_ref[1] == tower)
        def _():
            mine_ref[...] = through

        @pl.when(count_ref[1] != tower)
        def _():
            other_ref[...] = through


def finish_stage(numbers, count, own, last, begin, inverse):
    smem = pl.BlockSpec(memory_space=pltpu.SMEM)
    hbm = pl.BlockSpec(memory_space=pltpu.HBM)
    return pl.pallas_call(
        finish_kernel,
        grid=(1,),
        out_shape=(
            jax.ShapeDtypeStruct(own.shape, bf16),
            jax.ShapeDtypeStruct((own.shape[0] // 2, own.shape[1]), bf16),
            jax.ShapeDtypeStruct((own.shape[0] // 2, own.shape[1]), bf16),
        ),
        in_specs=[smem, smem, hbm, hbm, hbm, whole(inverse.shape)],
        out_specs=(whole(own.shape),) + (whole((own.shape[0] // 2, own.shape[1])),) * 2,
        scratch_shapes=[pltpu.VMEM(a.shape, a.dtype) for a in (own, last, begin)] + [pltpu.SemaphoreType.DMA((3,))],
        compiler_params=pltpu.CompilerParams(vmem_limit_bytes=60 * 2**20),
    )(numbers, count, own, last, begin, inverse)


def stack_kernel(text_ref, image_ref, out_ref):
    out_ref[:, 0, :] = text_ref[...]
    out_ref[:, 1, :] = image_ref[...]


def stack_rows(text, image):
    rows, width = text.shape
    return pl.pallas_call(
        stack_kernel,
        grid=(1,),
        out_shape=jax.ShapeDtypeStruct((rows, 2, width), bf16),
        in_specs=[whole(text.shape)] * 2,
        out_specs=whole((rows, 2, width)),
        compiler_params=pltpu.CompilerParams(vmem_limit_bytes=60 * 2**20),
    )(text, image)


def select_kernel(
    pick_hbm, spread_hbm, text_hbm, image_hbm, send_hbm, unit_ref, pick, spread, text_weight, image_weight, send, sems
):
    rows = spread.shape[0]
    pairs = ((spread_hbm, spread), (text_hbm, text_weight), (image_hbm, image_weight), (pick_hbm, pick))
    loads = [pltpu.make_async_copy(source, target, sems.at[k]) for k, (source, target) in enumerate(pairs)]
    for load in loads:
        load.start()
    loads[0].wait()
    for tower, weight in ((0, text_weight), (1, image_weight)):
        loads[1 + tower].wait()
        product = jnp.dot(spread[:, tower, :], weight[...], preferred_element_type=f32)
        inverse = lax.rsqrt(jnp.sum(product * product, axis=-1, keepdims=True) + eps_norm)
        unit_ref[tower * rows : (tower + 1) * rows] = (product * inverse).astype(bf16)
    loads[3].wait()
    copies = []
    per = send.shape[0] // 4
    for k in range(4):
        part = pl.ds(k * per, per)
        send[part] = jnp.dot(pick[part], unit_ref[...], preferred_element_type=f32).astype(bf16)
        copy = pltpu.make_async_copy(send.at[part], send_hbm.at[part], sems.at[4 + k])
        copy.start()
        copies.append(copy)
    for copy in copies:
        copy.wait()


def select_stage(pick, spread, text_weight, image_weight):
    rows, _, width = spread.shape
    hbm = pl.BlockSpec(memory_space=pltpu.HBM)
    return pl.pallas_call(
        select_kernel,
        grid=(1,),
        out_shape=(
            jax.ShapeDtypeStruct((pick.shape[0], width), bf16),
            jax.ShapeDtypeStruct((2 * rows, width), bf16),
        ),
        in_specs=[hbm] * 4,
        out_specs=(hbm, whole((2 * rows, width))),
        scratch_shapes=[
            *(pltpu.VMEM(array.shape, bf16) for array in (pick, spread, text_weight, image_weight)),
            pltpu.VMEM((pick.shape[0], width), bf16),
            pltpu.SemaphoreType.DMA((8,)),
        ],
        compiler_params=pltpu.CompilerParams(vmem_limit_bytes=50 * 2**20),
    )(pick, spread, text_weight, image_weight)


def local(x_img, x_txt, w_img, w_txt, sharpness, offset, lists, counts, holder):
    devices = lax.axis_size(ALL)
    me = lax.axis_index(ALL)
    core = lax.axis_index("c")
    rows, width = x_img.shape
    slots = lists.shape[1]
    scale = sharpness[0]
    shift = offset[0]
    spread = lax.all_to_all(stack_rows(x_txt, x_img), ALL, 0, 0, tiled=True)
    z_txt, r_txt = project(x_txt, w_txt)
    z_img, r_img = project(x_img, w_img)

    numbers = jnp.arange(devices, dtype=jnp.int32)
    hot = holder[None, :] == numbers[:, None]
    source = jnp.sum(jnp.where(lists[:, :, None] == numbers, holder, 0), axis=2)
    table = jnp.dot(hot.astype(bf16), source.astype(bf16), preferred_element_type=f32).astype(jnp.int32)
    count = jnp.sum(jnp.where(hot[me], counts, 0))

    columns = jnp.arange(2 * devices, dtype=jnp.int32)
    near = jnp.concatenate([table[:, 1:9], table[:, 1:9] + devices], axis=1)
    last = jnp.concatenate([table[:, 9:], table[:, 9:] + devices], axis=1)
    pick = (near[:, :, None] == columns).astype(bf16).reshape(16 * devices, 2 * devices)
    pick_last = (last[:, :, None] == columns).astype(bf16).reshape(2 * devices, 2 * devices)
    send, units = select_stage(pick, spread, w_txt, w_img)
    send = send.reshape(devices, 16, width)
    send_last = jnp.dot(pick_last, units, preferred_element_type=f32).astype(bf16).reshape(devices, 2, width)
    mates = lax.all_to_all(send, ALL, 0, 0, tiled=True).reshape(16 * devices, width)
    mates, send_last = lax.optimization_barrier((mates, send_last))
    last = lax.all_to_all(send_last, ALL, 0, 0, tiled=True)

    x_mine = jnp.where(core == 0, x_img, x_txt)
    x_other = swap(jnp.where(core == 0, x_txt, x_img), "c", 1)

    own = jnp.concatenate([z_img, z_txt], axis=0)
    logits = scale * lax.dot_general(z_img, z_txt, TRANSPOSED, preferred_element_type=f32) + shift
    sign = jnp.where(jnp.eye(rows, dtype=bool), 1.0, -1.0)
    coef = (-scale * sign * jax.nn.sigmoid(-sign * logits)).astype(bf16)
    dz = jnp.concatenate(
        [
            jnp.dot(coef, z_txt, preferred_element_type=f32),
            lax.dot_general(coef, z_img, ROWS_FIRST, preferred_element_type=f32),
        ],
        axis=0,
    )
    inverse = jnp.concatenate([r_img, r_txt], axis=0)
    scalars = jnp.stack([scale, shift])
    dz = pair_stage(scalars, count[None], own, mates, dz)
    number = core[None].astype(jnp.int32)
    du, du_mine, du_away = finish_stage(
        scalars, jnp.concatenate([count[None], number]), own, last, dz, inverse
    )
    du_img = du[:rows]
    du_txt = du[rows:]
    du_other = swap(du_away, "c", 1)
    g_img = lax.dot_general(du_img, w_img, TRANSPOSED, preferred_element_type=f32).astype(bf16)
    g_txt = lax.dot_general(du_txt, w_txt, TRANSPOSED, preferred_element_type=f32).astype(bf16)

    factor = (64.0 / (devices * rows)) ** 0.5
    quarter = jnp.bitwise_xor(lax.axis_index("x"), lax.axis_index("y"))
    index = lax.axis_index(STREAMS[1][1])
    places = [jnp.bitwise_xor(jnp.bitwise_xor((index + step) & 3, index), quarter) for step in (0, 3, 1, 2)]
    places = jnp.stack(places).astype(jnp.int32)
    pieces = head_gradient(factor, places, (x_mine, x_other), (du_mine, du_other))
    pieces, (g_img, g_txt) = reduce_streams(pieces, (g_img, g_txt))
    written = assemble(places, number, pieces[::2], width)
    head_img, head_txt = assemble(places, 1 - number, pieces[1::2], width, written)
    return (g_img, g_txt, head_img, head_txt)


def solution(mesh):
    grid = Mesh(mesh.devices.reshape(4, 4, 4, 2), ALL)
    placed = (P(ALL, None), P(ALL, None), P(), P(), P(), P(), P(), P(), P())
    return jax.shard_map(
        local,
        mesh=grid,
        in_specs=placed,
        out_specs=(P(ALL, None), P(ALL, None), P(), P()),
        check_vma=False,
    )
```
